32 devices in a mesh: dp: 4 (over z), expert: 8 (over y, x, core).
Axes of the slice: x: 2, y: 2, z: 4, core: 2. Of those that a mesh axis runs over, the one named last changes fastest.
Arguments:
- tokens: bfloat16 [32, 1024, 768], P(('dp', 'expert')), may hold values from -6 to 6
- token_ids: int32 [32, 1024], P(('dp', 'expert')), may hold values from 0 to 8191, as said below
- hash_table: int32 [8192], replicated, may hold values from 0 to 7, as said below
- gain_one: float32 [768], replicated, may hold values from 0.5 to 1.5
- w_qkv: bfloat16 [768, 2304], replicated, may hold values from -0.21875 to 0.21875
- w_proj: bfloat16 [768, 768], replicated, may hold values from -0.875 to 0.875
- gain_two: float32 [768], replicated, may hold values from 0.5 to 1.5
- w_in: bfloat16 [8, 768, 3072], P('expert'), may hold values from -0.21875 to 0.21875
- w_out: bfloat16 [8, 768, 3072], P('expert'), may hold values from -0.109375 to 0.109375
- cotangent: bfloat16 [32, 1024, 768], P(('dp', 'expert')), may hold values from -10 to 10
Outputs:
- outputs: bfloat16 [32, 1024, 768], P(('dp', 'expert'))
- grad_tokens: float32 [32, 1024, 768], P(('dp', 'expert'))
- grad_gain_one: float32 [768], replicated
- grad_qkv: float32 [768, 2304], replicated
- grad_proj: float32 [768, 768], replicated
- grad_gain_two: float32 [768], replicated
- grad_w_in: float32 [8, 768, 3072], P('expert', None, 'dp')
- grad_w_out: float32 [8, 768, 3072], P('expert', None, 'dp')
The draws below stay inside these ranges and needn't reach their ends.
Inputs may be any that keep to these rules, and one draw needn't show every extreme that they name: `token_ids`: among the 1024 tokens of one device, at most 256 have an id that hash_table gives to one expert; in every draw, in each dp group, every device has exactly 256 tokens of one common expert. `hash_table`: every expert is given exactly 1024 ids.
All inputs are finite; a program needn't handle non-finite values.
Results may differ from the reference program's by a relative error of at most 0.011.
Values may be sent and summed in bfloat16 or wider, within the bound.
No kernel may reach another device: no remote copies, remote signals or barrier semaphores. Data moves between devices by JAX's collectives and lax.ppermute only.
A program may use at most 256 MiB of HBM per device.

```python
import jax
import jax.numpy as jnp
from jax import lax

D = 768
HEADS = 12
HEAD_DIM = 64
FF = 3072
VOCAB = 8192
LEN = 1024
SEQ_DEV = 1
EXPERTS = 8
SEQS = 32
MOST = 256


def balanced_table(key):
    shuffled = jax.random.permutation(key, VOCAB).astype(jnp.int32)
    return ((shuffled % EXPERTS).astype(jnp.int32), jnp.argsort(shuffled).astype(jnp.int32))


def draw_hash_table(key, part):
    expert_of, _ = balanced_table(key)
    return expert_of


def draw_token_ids(key, part):
    expert_of, inverse = balanced_table(key)
    key = jax.random.fold_in(key, 37)
    key_tier, key_hot, key_slot, key_place, key_pick = jax.random.split(key, 5)
    devices = SEQS // SEQ_DEV
    groups = devices // EXPERTS
    row_count = SEQ_DEV * LEN
    slot_total = EXPERTS * MOST
    slot_index = jnp.arange(slot_total, dtype=jnp.int32)
    slot_owner = slot_index // MOST
    tier_draw = jax.random.randint(key_tier, (groups, EXPERTS), 0, 3)
    hottest = jax.random.randint(key_hot, (groups,), 0, EXPERTS)
    group_of = jnp.arange(devices, dtype=jnp.int32) // EXPERTS
    slot_noise = jax.random.randint(key_slot, (devices, slot_total), 0, 4096)
    slot_level = tier_draw[group_of][:, slot_owner] * 4096 + slot_noise
    slot_score = slot_level * slot_total + slot_index[None, :]
    forced = slot_owner[None, :] == hottest[group_of][:, None]
    slot_score = jnp.where(forced, slot_index[None, :] - slot_total, slot_score)
    chosen = jnp.argsort(slot_score, axis=1)[:, :row_count]
    owners = slot_owner[chosen]
    position_score = jax.random.randint(key_place, (devices, row_count), 0, 4096) * row_count
    position_score = position_score + jnp.arange(row_count, dtype=jnp.int32)[None, :]
    owners = jnp.take_along_axis(owners, jnp.argsort(position_score, axis=1), axis=1)
    within = jax.random.randint(key_pick, (devices, row_count), 0, VOCAB // EXPERTS)
    picked_ids = inverse[owners + EXPERTS * within]
    return picked_ids.reshape(SEQS, LEN).astype(jnp.int32)


def draw_cotangent(key, part):
    key = jax.random.fold_in(key, 21)
    key_values, key_scales = jax.random.split(key, 2)
    scales = jnp.exp(jax.random.uniform(key_scales, (SEQS, 1, 1), jnp.float32, jnp.log(0.4), jnp.log(2.5)))
    values = jnp.clip(jax.random.normal(key_values, (SEQS, LEN, D), jnp.float32), -4.0, 4.0)
    return (values * scales).astype(jnp.bfloat16)


def shard_levels(key, extent, pieces, smallest, high):
    def one(axis_at, blocks):
        steps = jax.random.uniform(jax.random.fold_in(jax.random.fold_in(key, 6), axis_at), (blocks,), jnp.float32, smallest / len(pieces), high / len(pieces))
        return jnp.repeat(jnp.exp(steps), extent[axis_at] // blocks).reshape((-1,) + (1,) * (len(extent) - axis_at - 1))

    loudness = one(*pieces[0])
    for cut in pieces[1:]:
        loudness = loudness * one(*cut)
    return loudness


def normal_values(stream_key, dims, scale, reach, cuts=(), kind=jnp.bfloat16):
    gain = shard_levels(stream_key, dims, cuts, -0.22, 0.18) if cuts else 1.0
    values = jax.random.normal(stream_key, dims, jnp.float32) * scale * gain
    return jnp.minimum(jnp.maximum(values, -reach), reach).astype(kind)


def setup_inputs(seed: int = 0) -> dict:
    splits = jax.random.split(jax.random.key(seed), 11)
    return {
        "tokens": normal_values(splits[0], (SEQS, LEN, D), 1.0, 6.0, ((0, 32),)),
        "token_ids": draw_token_ids(jax.random.fold_in(splits[10], 71), 0),
        "hash_table": draw_hash_table(jax.random.fold_in(splits[10], 71), 0),
        "gain_one": jnp.clip(1.0 + 0.1 * jax.random.normal(splits[3], (D,), jnp.float32), 0.5, 1.5),
        "w_qkv": normal_values(splits[4], (D, 3 * D), D ** -0.5, 0.21875),
        "w_proj": normal_values(splits[5], (D, D), (D // 16) ** -0.5, 0.875),
        "gain_two": jnp.clip(1.0 + 0.1 * jax.random.normal(splits[6], (D,), jnp.float32), 0.5, 1.5),
        "w_in": normal_values(splits[7], (EXPERTS, D, FF), D ** -0.5, 0.21875, ((0, 8),)),
        "w_out": normal_values(splits[8], (EXPERTS, D, FF), FF ** -0.5, 0.109375, ((0, 8),)),
        "cotangent": draw_cotangent(jax.random.fold_in(splits[10], 71), 0),
    }


EPSILON = 1e-05
NEGATIVE = -1e+30
HIGHEST = lax.Precision.HIGHEST

@jax.custom_vjp
def low(v):
    return lax.optimization_barrier(v.astype(jnp.bfloat16)).astype(jnp.float32)

@jax.custom_vjp
def low_back(v):
    return v

def low_keep(v):
    return (low(v), None)

def low_pass(kept, grad):
    return (grad,)

def back_keep(v):
    return (v, None)

def back_low(kept, grad):
    return (low(grad),)
low.defvjp(low_keep, low_pass)
low_back.defvjp(back_keep, back_low)

def layer_norm(values, norm_gain):
    centred = values - lax.optimization_barrier(jnp.mean(values, axis=-1, keepdims=True))
    spread = lax.optimization_barrier(jnp.mean(centred * centred, axis=-1, keepdims=True))
    return centred * lax.rsqrt(spread + EPSILON) * norm_gain

def attend(packed):
    length = packed.shape[0]
    queries = packed[:, :D].reshape(length, HEADS, HEAD_DIM)
    key_rows = packed[:, D:2 * D].reshape(length, HEADS, HEAD_DIM)
    value_rows = packed[:, 2 * D:].reshape(length, HEADS, HEAD_DIM)
    scores = jnp.einsum('qhd,khd->hqk', queries, key_rows, precision=HIGHEST) * HEAD_DIM ** (-0.5)
    scores = low_back(scores)
    positions = jnp.arange(length, dtype=jnp.int32)
    allowed = positions[None, :] <= positions[:, None]
    scores = jnp.where(allowed[None], scores, NEGATIVE)
    highest = lax.optimization_barrier(jnp.max(scores, axis=-1, keepdims=True))
    exponent = jnp.exp(scores - highest)
    probabilities = exponent / lax.optimization_barrier(jnp.sum(exponent, axis=-1, keepdims=True))
    blended = jnp.einsum('hqk,khd->qhd', low(probabilities), value_rows, precision=HIGHEST)
    return blended.reshape(length, HEADS * HEAD_DIM)

def expert_layer(normed, chosen, w_in, w_out, capacity):
    numbers = jnp.arange(EXPERTS, dtype=jnp.int32)

    def one_expert(carried, scanned):
        inner_weight, outer_weight, number = scanned
        member = (chosen == number).astype(jnp.int32)
        ordering = jnp.argsort(1 - member)[:capacity].astype(jnp.int32)
        present = member[ordering].astype(jnp.float32)[:, None]
        hidden = low_back(jnp.dot(normed[ordering], inner_weight, precision=HIGHEST))
        active = low(jax.nn.gelu(hidden, approximate=True))
        result = jnp.dot(active, outer_weight.T, precision=HIGHEST) * present
        return (carried.at[ordering].add(result), None)
    combined, _ = lax.scan(jax.checkpoint(one_expert), jnp.zeros(normed.shape, normed.dtype), (w_in, w_out, numbers))
    return combined

def forward(inputs, chosen, gain_one, w_qkv, w_proj, gain_two, w_in, w_out, capacity):
    flat_rows = inputs.reshape(-1, D)
    normed_one = low(layer_norm(flat_rows, gain_one))
    packed = low(low_back(jnp.dot(normed_one, w_qkv, precision=HIGHEST)))
    attended = lax.map(jax.checkpoint(attend), packed.reshape(-1, LEN, 3 * D))
    attended = low(low_back(attended.reshape(-1, D)))
    residual = flat_rows + low_back(jnp.dot(attended, w_proj, precision=HIGHEST))
    normed_two = low(low_back(layer_norm(residual, gain_two)))
    expert_out = low(low_back(expert_layer(normed_two, chosen.reshape(-1), w_in, w_out, capacity)))
    return (residual + expert_out).reshape(inputs.shape)

def reference(tokens, token_ids, hash_table, gain_one, w_qkv, w_proj, gain_two, w_in, w_out, cotangent):
    group_size = 1
    if SEQS % 2 == 0 and 2 * LEN <= 4096:
        group_size = 2
    if SEQS % 4 == 0 and 4 * LEN <= 4096:
        group_size = 4
    capacity = min(group_size * LEN, group_size * MOST)
    rounds_count = SEQS // group_size
    chosen = jnp.take(hash_table, token_ids).astype(jnp.int32)
    params = (gain_one, w_qkv.astype(jnp.float32), w_proj.astype(jnp.float32), gain_two, w_in.astype(jnp.float32), w_out.astype(jnp.float32))

    def one_group(totals, scanned):
        inputs, group_chosen, upstream = scanned

        def local_forward(values, first_gain, packed_weight, proj_weight, second_gain, inner_weight, outer_weight):
            return forward(values, group_chosen, first_gain, packed_weight, proj_weight, second_gain, inner_weight, outer_weight, capacity)
        results, pullback = jax.vjp(local_forward, inputs.astype(jnp.float32), params[0], params[1], params[2], params[3], params[4], params[5])
        grads = pullback(upstream.astype(jnp.float32))
        return (jax.tree.map(jnp.add, totals, tuple(grads[1:])), (results.astype(jnp.bfloat16), grads[0]))
    initial = jax.tree.map(jnp.zeros_like, params)
    totals, (outputs, grad_inputs) = lax.scan(one_group, initial, (tokens.reshape(rounds_count, group_size, LEN, D), chosen.reshape(rounds_count, group_size, LEN), cotangent.reshape(rounds_count, group_size, LEN, D)))
    return (outputs.reshape(SEQS, LEN, D), grad_inputs.reshape(SEQS, LEN, D), totals[0], totals[1], totals[2], totals[3], totals[4], totals[5])
```

```python
import functools
import math

import jax
import jax.numpy as jnp
from jax import lax
from jax.experimental import pallas as pl
from jax.experimental.pallas import tpu as pltpu
from jax.sharding import Mesh, PartitionSpec as P

HEADS = 12
HEAD_DIM = 64
EPSILON = 1e-05
NEGATIVE = -1e30
SCALE = HEAD_DIM ** (-0.5)
BF = jnp.bfloat16
F32 = jnp.float32
PLANE = ("y", "x", "core")


def nn(a, b):
    return lax.dot_general(a, b, (((1,), (0,)), ((), ())), preferred_element_type=F32)


def nt(a, b):
    return lax.dot_general(a, b, (((1,), (1,)), ((), ())), preferred_element_type=F32)


def tn(a, b):
    return lax.dot_general(a, b, (((0,), (0,)), ((), ())), preferred_element_type=F32)


def iota(shape, dim):
    return lax.broadcasted_iota(jnp.int32, shape, dim)


def call(body, flops=0, moved=0, limit=40, **kw):
    return pl.pallas_call(
        body,
        compiler_params=pltpu.CompilerParams(vmem_limit_bytes=limit << 20),
        cost_estimate=pl.CostEstimate(
            flops=int(flops), bytes_accessed=int(moved), transcendentals=0
        ),
        **kw,
    )


def whole(shape):
    return pl.BlockSpec(shape, lambda *i: (0,) * len(shape))


def norm_parts(v):
    centred = v - jnp.mean(v, axis=-1, keepdims=True)
    rate = lax.rsqrt(jnp.mean(centred * centred, axis=-1, keepdims=True) + EPSILON)
    return centred * rate, rate


def norm_grad(x_hat, rate, u):
    return rate * (
        u
        - jnp.mean(u, axis=-1, keepdims=True)
        - x_hat * jnp.mean(u * x_hat, axis=-1, keepdims=True)
    )


def route_body(ids_ref, table_ref, cot_ref, row_ref, col_ref, send_ref, *, experts, capacity):
    step = pl.program_id(0)
    count = ids_ref.shape[1]
    block = send_ref.shape[0]

    @pl.when(step == 0)
    def _():
        ids = ids_ref[...]
        table = table_ref[...].astype(BF)
        high = (iota((table.shape[0], count), 0) == (ids >> 7)).astype(BF)
        picked = tn(table, high)
        low = iota((128, count), 0) == (ids & 127)
        chosen = jnp.sum(jnp.where(low, picked, 0.0), axis=0, keepdims=True)
        slots = max(16, experts)
        member = iota((slots, count), 0).astype(F32) == chosen
        before = (iota((count, count), 0) < iota((count, count), 1)).astype(BF)
        earlier = nn(member.astype(BF), before)
        rank = jnp.sum(jnp.where(member, earlier, 0.0), axis=0, keepdims=True)
        target = chosen * capacity + rank
        row_ref[...] = target.astype(jnp.int32)
        turned = jnp.transpose(jnp.broadcast_to(target, (8, count)))
        col_ref[...] = turned[:, :1].astype(jnp.int32)

    placer = (iota((block, count), 0) + step * block == row_ref[...]).astype(BF)
    send_ref[...] = nn(placer, cot_ref[...]).astype(BF)


def route(ids, table, cot, experts, capacity):
    count, width = cot.shape
    slots = experts * capacity
    block = min(512, slots)
    return call(
        functools.partial(route_body, experts=experts, capacity=capacity),
        flops=2 * slots * count * width,
        moved=2 * (count + slots) * width,
        grid=(slots // block,),
        in_specs=[whole(ids.shape), whole(table.shape), whole(cot.shape)],
        out_specs=[
            whole((1, count)),
            whole((count, 1)),
            pl.BlockSpec((block, width), lambda i: (i, 0)),
        ],
        out_shape=[
            jax.ShapeDtypeStruct((1, count), jnp.int32),
            jax.ShapeDtypeStruct((count, 1), jnp.int32),
            jax.ShapeDtypeStruct((slots, width), BF),
        ],
    )(ids, table, cot)


def packed_body(x_ref, gain_ref, w_ref, packed_ref, turned_ref):
    x_hat, _ = norm_parts(x_ref[...].astype(F32))
    normed = (x_hat * gain_ref[...]).astype(BF)
    packed_ref[...] = nn(normed, w_ref[...]).astype(BF)
    turned_ref[...] = jnp.transpose(normed)


def make_packed(x, gain, w):
    count, width = x.shape
    wide = w.shape[1]
    block = 256
    return call(
        packed_body,
        flops=2 * count * width * wide,
        moved=2 * (count * (2 * width + wide) + width * wide),
        grid=(count // block,),
        in_specs=[
            pl.BlockSpec((block, width), lambda i: (i, 0)),
            whole(gain.shape),
            whole(w.shape),
        ],
        out_specs=[
            pl.BlockSpec((block, wide), lambda i: (i, 0)),
            pl.BlockSpec((width, block), lambda i: (0, i)),
        ],
        out_shape=[
            jax.ShapeDtypeStruct((count, wide), BF),
            jax.ShapeDtypeStruct((width, count), BF),
        ],
    )(x, gain, w)


def attend_body(q_ref, k_ref, v_ref, o_ref, total_ref, *, block):
    length = q_ref.shape[0]
    lane = iota((1, 128), 1)
    v_turned = jnp.transpose(v_ref[...])
    allowed = iota((block, block), 0) <= iota((block, block), 1)
    for row in range(length // block):
        end = (row + 1) * block
        outs = []
        for head in range(2):
            q = jnp.where(lane // 64 == head, q_ref[row * block : end, :] * BF(SCALE), BF(0))
            s = nt(k_ref[:end, :], q)
            last = jnp.where(allowed, s[end - block :], NEGATIVE)
            s = jnp.concatenate([s[: end - block], last], 0) if row else last
            highest = jnp.max(s, 0, keepdims=True)
            p = jnp.exp(s - highest)
            summed = jnp.sum(p, 0, keepdims=True)
            out = nn(v_turned[head * 64 : (head + 1) * 64, :end], p.astype(BF))
            outs.append(out * (1.0 / summed))
            total_ref[0, head : head + 1, row * block : end] = highest + jnp.log(summed)
        o_ref[row * block : end, :] = jnp.transpose(jnp.concatenate(outs, 0)).astype(BF)


def attend(packed):
    length = packed.shape[0]
    pairs = packed.shape[1] // 384
    part = lambda o: pl.BlockSpec((length, 128), lambda i: (0, o * pairs + i))
    return call(
        functools.partial(attend_body, block=min(512, length)),
        flops=1.2e10,
        moved=2 * length * pairs * 512,
        grid=(pairs,),
        in_specs=[part(0), part(1), part(2)],
        out_specs=[part(0), pl.BlockSpec((1, 2, length), lambda i: (i, 0, 0))],
        out_shape=[
            jax.ShapeDtypeStruct((length, pairs * 128), BF),
            jax.ShapeDtypeStruct((pairs, 2, length), F32),
        ],
    )(packed, packed, packed)


def attend_back_body(
    q_ref, k_ref, v_ref, o_ref, up_ref, total_ref, dq_ref, dk_ref, dv_ref, acc_ref, *, block
):
    length = q_ref.shape[0]
    count = length // block
    lane = iota((1, 128), 1)
    inner = jnp.transpose(o_ref[...].astype(F32) * up_ref[...].astype(F32))
    inner = [jnp.sum(inner[:64], 0, keepdims=True), jnp.sum(inner[64:], 0, keepdims=True)]
    allowed = iota((block, block), 0) <= iota((block, block), 1)
    for part in range(count):
        begin, end = part * block, (part + 1) * block
        k = k_ref[begin:end, :]
        v = v_ref[begin:end, :]
        dk, dv = [], []
        for head in range(2):
            mine = lane // 64 == head
            q = jnp.where(mine, q_ref[begin:, :] * BF(SCALE), BF(0))
            up = jnp.where(mine, up_ref[begin:, :], BF(0))
            s = nt(k, q) - total_ref[0, head : head + 1, begin:]
            first = jnp.where(allowed, s[:, :block], NEGATIVE)
            s = jnp.concatenate([first, s[:, block:]], 1) if part < count - 1 else first
            p = jnp.exp(s)
            ds = (p * (nt(v, up) - inner[head][:, begin:])).astype(BF)
            dv.append(nn(p.astype(BF), up))
            dk.append(nn(ds, q))
            dq = tn(ds, jnp.where(mine, k * BF(SCALE), BF(0)))
            if part == 0 and head == 0:
                acc_ref[...] = dq
            else:
                acc_ref[begin:, :] += dq
        dk_ref[begin:end, :] = (dk[0] + dk[1]).astype(BF)
        dv_ref[begin:end, :] = (dv[0] + dv[1]).astype(BF)
    dq_ref[...] = acc_ref[...].astype(BF)


def attend_back(packed, attended, totals, upstream):
    length = packed.shape[0]
    pairs = packed.shape[1] // 384
    part = lambda o: pl.BlockSpec((length, 128), lambda i: (0, o * pairs + i))
    return call(
        functools.partial(attend_back_body, block=min(256, length)),
        flops=3e10,
        moved=2 * length * pairs * 1024,
        grid=(pairs,),
        in_specs=[
            part(0), part(1), part(2), part(0), part(0),
            pl.BlockSpec((1, 2, length), lambda i: (i, 0, 0)),
        ],
        out_specs=[part(0)] * 3,
        out_shape=[jax.ShapeDtypeStruct((length, pairs * 128), BF)] * 3,
        scratch_shapes=[pltpu.VMEM((length, 128), F32)],
    )(packed, packed, packed, attended, upstream, totals)


def dispatch_body(att_ref, w_ref, x_ref, gain_ref, row_ref, res_ref, send_ref, normed_ref):
    step = pl.program_id(0)
    count = att_ref.shape[0]
    block = send_ref.shape[0]

    @pl.when(step == 0)
    def _():
        for begin in range(0, count, 256):
            rows = slice(begin, begin + 256)
            residual = x_ref[rows, :].astype(F32) + nn(att_ref[rows, :], w_ref[...])
            res_ref[rows, :] = residual
            x_hat, _ = norm_parts(residual)
            normed_ref[rows, :] = (x_hat * gain_ref[...]).astype(BF)

    placer = (iota((block, count), 0) + step * block == row_ref[...]).astype(BF)
    send_ref[...] = nn(placer, normed_ref[...]).astype(BF)


def dispatch(attended, w, x, gain, row, slots):
    count, width = x.shape
    block = min(512, slots)
    return call(
        dispatch_body,
        flops=2 * count * width * (slots + width),
        moved=2 * width * (5 * count + slots),
        grid=(slots // block,),
        in_specs=[whole(a.shape) for a in (attended, w, x, gain, row)],
        out_specs=[
            whole((count, width)),
            pl.BlockSpec((block, width), lambda i: (i, 0)),
        ],
        out_shape=[
            jax.ShapeDtypeStruct((count, width), F32),
            jax.ShapeDtypeStruct((slots, width), BF),
        ],
        scratch_shapes=[pltpu.VMEM((count, width), BF)],
    )(attended, w, x, gain, row)


def expert_body(x_ref, g_ref, w_ref, ga_ref, act_ref, gh_ref, dw_ref, turned_ref):
    @pl.when(pl.program_id(0) == 0)
    def _():
        turned_ref[...] = jnp.transpose(g_ref[...])

    c1 = 2.0 * math.sqrt(2.0 / math.pi)
    c2 = c1 * 0.044715
    for begin in range(0, x_ref.shape[0], 512):
        rows = slice(begin, begin + 512)
        h = nn(x_ref[rows, :], w_ref[...])
        square = h * h
        half = jnp.tanh(h * (0.5 * c1 + (0.5 * c2) * square)) * 0.5 + 0.5
        act = h * half
        slope = half + (act * (1.0 - half)) * (c1 + (3.0 * c2) * square)
        act_ref[rows, :] = act.astype(BF)
        gh_ref[rows, :] = (ga_ref[rows, :].astype(F32) * slope).astype(BF)
    dw_ref[...] = nn(turned_ref[...], act_ref[...]).astype(BF)


def expert(x, g, w, ga):
    rows, width = x.shape
    units = w.shape[1]
    block = min(512, units)
    column = pl.BlockSpec((rows, block), lambda i: (0, i))
    weight = pl.BlockSpec((width, block), lambda i: (0, i))
    return call(
        expert_body,
        flops=4 * rows * width * units,
        moved=2 * (2 * rows * width + 2 * width * units + 3 * rows * units),
        limit=48,
        grid=(units // block,),
        in_specs=[whole(x.shape), whole(g.shape), weight, column],
        out_specs=[column, column, weight],
        out_shape=[
            jax.ShapeDtypeStruct((rows, units), BF),
            jax.ShapeDtypeStruct((rows, units), BF),
            jax.ShapeDtypeStruct((width, units), BF),
        ],
        scratch_shapes=[pltpu.VMEM((width, rows), BF)],
    )(x, g, w, ga)


def collect_back_body(
    back_ref, col_ref, res_ref, cot_ref, gain_ref, w_ref, att_ref,
    gres_ref, gatt_ref, gproj_ref, ggain_ref, acc_ref,
):
    step = pl.program_id(0)
    block = col_ref.shape[0]
    slots = back_ref.shape[0]
    placer = (iota((block, slots), 1) == col_ref[...]).astype(BF)
    grad = nn(placer, back_ref[...])
    x_hat, rate = norm_parts(res_ref[...])
    gres = cot_ref[...].astype(F32) + norm_grad(x_hat, rate, grad * gain_ref[...])
    gres_ref[...] = gres
    gain_part = jnp.sum(grad * x_hat, axis=0, keepdims=True)
    gattn = gres.astype(BF)
    gatt_ref[...] = nt(gattn, w_ref[...]).astype(BF)
    part = tn(att_ref[...], gattn)

    @pl.when(step == 0)
    def _():
        acc_ref[...] = part
        ggain_ref[...] = gain_part

    @pl.when(step > 0)
    def _():
        acc_ref[...] += part
        ggain_ref[...] += gain_part

    @pl.when(step == pl.num_programs(0) - 1)
    def _():
        gproj_ref[...] = acc_ref[...].astype(BF)


def collect_back(back, col, residual, cot, gain, w, attended):
    count, width = cot.shape
    slots = back.shape[0]
    block = 256
    row = pl.BlockSpec((block, width), lambda i: (i, 0))
    return call(
        collect_back_body,
        flops=2 * count * width * (slots + 2 * width),
        moved=2 * width * (slots + 8 * count),
        grid=(count // block,),
        in_specs=[
            whole(back.shape), pl.BlockSpec((block, 1), lambda i: (i, 0)), row, row,
            whole(gain.shape), whole(w.shape), row,
        ],
        out_specs=[row, row, whole((width, width)), whole((1, width))],
        out_shape=[
            jax.ShapeDtypeStruct((count, width), F32),
            jax.ShapeDtypeStruct((count, width), BF),
            jax.ShapeDtypeStruct((width, width), BF),
            jax.ShapeDtypeStruct((1, width), F32),
        ],
        scratch_shapes=[pltpu.VMEM((width, width), F32)],
    )(back, col, residual, cot, gain, w, attended)


def collect_body(back_ref, col_ref, res_ref, out_ref):
    block, slots = col_ref.shape[0], back_ref.shape[0]
    placer = (iota((block, slots), 1) == col_ref[...]).astype(BF)
    out_ref[...] = (res_ref[...] + nn(placer, back_ref[...])).astype(BF)


def collect(back, col, residual):
    count, width = residual.shape
    block = 256
    row = pl.BlockSpec((block, width), lambda i: (i, 0))
    return call(
        collect_body,
        flops=2 * count * width * back.shape[0],
        moved=2 * width * (back.shape[0] + 3 * count),
        grid=(count // block,),
        in_specs=[whole(back.shape), pl.BlockSpec((block, 1), lambda i: (i, 0)), row],
        out_specs=row,
        out_shape=jax.ShapeDtypeStruct((count, width), BF),
    )(back, col, residual)


def grad_qkv_body(turned_ref, g_ref, out_ref):
    out_ref[...] = nn(turned_ref[...], g_ref[...]).astype(BF)


def weight_grad(turned, g):
    width, count = turned.shape
    wide = g.shape[1]
    block = min(384, wide)
    return call(
        grad_qkv_body,
        flops=2 * width * count * wide,
        moved=2 * (width * count + count * wide + width * wide),
        grid=(wide // block,),
        in_specs=[whole(turned.shape), pl.BlockSpec((count, block), lambda i: (0, i))],
        out_specs=pl.BlockSpec((width, block), lambda i: (0, i)),
        out_shape=jax.ShapeDtypeStruct((width, wide), BF),
    )(turned, g)


def grad_in_body(x_ref, gain_ref, w_ref, dq_ref, dk_ref, dv_ref, gres_ref, out_ref, ggain_ref):
    step = pl.program_id(0)
    width = x_ref.shape[1]
    x_hat, rate = norm_parts(x_ref[...].astype(F32))
    grad = nt(dq_ref[...], w_ref[:, :width])
    grad += nt(dk_ref[...], w_ref[:, width : 2 * width])
    grad += nt(dv_ref[...], w_ref[:, 2 * width :])
    out_ref[...] = gres_ref[...] + norm_grad(x_hat, rate, grad * gain_ref[...])
    part = jnp.sum(grad * x_hat, axis=0, keepdims=True)

    @pl.when(step == 0)
    def _():
        ggain_ref[...] = part

    @pl.when(step > 0)
    def _():
        ggain_ref[...] += part


def grad_in(x, gain, w, dq, dk, dv, gres):
    count, width = x.shape
    block = 256
    row = pl.BlockSpec((block, width), lambda i: (i, 0))
    return call(
        grad_in_body,
        flops=6 * count * width * width,
        moved=2 * width * 9 * count,
        grid=(count // block,),
        in_specs=[row, whole(gain.shape), whole(w.shape), row, row, row, row],
        out_specs=[row, whole((1, width))],
        out_shape=[
            jax.ShapeDtypeStruct((count, width), F32),
            jax.ShapeDtypeStruct((1, width), F32),
        ],
    )(x, gain, w, dq, dk, dv, gres)


def shift(a, axis, k):
    n = lax.axis_size(axis)
    return lax.ppermute(a, axis, [(i, (i + k) % n) for i in range(n)])


def cut(a, index, pieces, dim):
    size = a.shape[dim] // pieces
    return lax.dynamic_slice_in_dim(a, index * size, size, dim)


def scatter_sum(a, axis, dim):
    n = lax.axis_size(axis)
    me = lax.axis_index(axis)
    total = cut(a, me, n, dim).astype(F32)
    for k in range(1, n):
        total += shift(cut(a, lax.rem(me + k, n), n, dim), axis, k).astype(F32)
    return total.astype(a.dtype)


def gather_all(a, axis, dim):
    n = lax.axis_size(axis)
    me = lax.axis_index(axis)
    size = a.shape[dim]
    shape = a.shape[:dim] + (n * size,) + a.shape[dim + 1 :]
    out = lax.dynamic_update_slice_in_dim(jnp.zeros(shape, a.dtype), a, me * size, dim)
    for k in range(1, n):
        got = shift(a, axis, k)
        out = lax.dynamic_update_slice_in_dim(out, got, lax.rem(me - k + n, n) * size, dim)
    return out


def sum_all(a):
    a = scatter_sum(a, "core", 1)
    half = a.shape[0] // 2
    top = scatter_sum(scatter_sum(a[:half], "x", 0), "y", 0)
    low = scatter_sum(scatter_sum(a[half:], "y", 0), "x", 0)
    both = scatter_sum(jnp.stack([top, low]), "dp", 1)
    both = gather_all(both, "dp", 1)
    top = gather_all(gather_all(both[0], "y", 0), "x", 0)
    low = gather_all(gather_all(both[1], "x", 0), "y", 0)
    return gather_all(jnp.concatenate([top, low], 0), "core", 1)


def sum_small(a):
    for axis in ("core", "x", "y", "dp"):
        total = a
        for k in range(1, lax.axis_size(axis)):
            total = total + shift(a, axis, k)
        a = total
    return a


def local(tokens, token_ids, hash_table, gain_one, w_qkv, w_proj, gain_two, w_in, w_out, cotangent):
    width = tokens.shape[-1]
    x = tokens.reshape(-1, width)
    cot = cotangent.reshape(-1, width)
    count = x.shape[0]
    experts = lax.axis_size(PLANE)
    capacity = 2 * count // experts
    slots = experts * capacity
    first_gain = gain_one.reshape(1, width)
    second_gain = gain_two.reshape(1, width)
    inner, outer = w_in[0], w_out[0]

    def exchange(rows):
        moved = lax.all_to_all(
            rows.reshape(experts, capacity, width), PLANE, split_axis=0, concat_axis=0, tiled=True
        )
        return moved.reshape(slots, width)

    row, col, grad_send = route(
        token_ids.reshape(1, count), hash_table.reshape(-1, 128), cot, experts, capacity
    )
    flat_grad = exchange(grad_send)
    packed, turned = make_packed(x, first_gain, w_qkv)
    attended, totals = attend(packed)
    residual, outgoing = dispatch(attended, w_proj, x, second_gain, row, slots)
    flat_in = exchange(outgoing)
    grad_active = nn(flat_grad, outer).astype(BF)
    active, grad_hidden, grad_outer = expert(flat_in, flat_grad, inner, grad_active)
    grad_w_out = lax.psum_scatter(
        grad_outer[None], "dp", scatter_dimension=2, tiled=True
    ).astype(F32)
    grad_flat = nt(grad_hidden, inner).astype(BF)
    grad_back = exchange(grad_flat)
    grad_inner = tn(flat_in, grad_hidden).astype(BF)
    grad_w_in = lax.psum_scatter(
        grad_inner[None], "dp", scatter_dimension=2, tiled=True
    ).astype(F32)
    result = nt(active, outer).astype(BF)
    returned = exchange(result)

    grad_residual, grad_attended, grad_proj, grad_gain_two = collect_back(
        grad_back, col, residual, cot, second_gain, w_proj, attended
    )
    dq, dk, dv = attend_back(packed, attended, totals, grad_attended)
    grad_qkv = jnp.concatenate([weight_grad(turned, g) for g in (dq, dk, dv)], axis=1)
    grad_tokens, grad_gain_one = grad_in(x, first_gain, w_qkv, dq, dk, dv, grad_residual)
    outputs = collect(returned, col, residual)

    grad_proj = sum_all(grad_proj).astype(F32)
    grad_qkv = sum_all(grad_qkv).astype(F32)
    gains = sum_small(jnp.concatenate([grad_gain_one, grad_gain_two], 0))
    return (
        outputs.reshape(tokens.shape),
        grad_tokens.reshape(tokens.shape),
        gains[0],
        grad_qkv,
        grad_proj,
        gains[1],
        grad_w_in,
        grad_w_out,
    )


def solution(mesh):
    dp, experts = mesh.devices.shape
    side = math.isqrt(experts // 2)
    parts = Mesh(mesh.devices.reshape(dp, side, experts // 2 // side, 2), ("dp", "y", "x", "core"))
    rows = ("dp",) + PLANE
    in_specs = (
        P(rows, None, None),
        P(rows, None),
        P(),
        P(),
        P(),
        P(),
        P(),
        P(PLANE, None, None),
        P(PLANE, None, None),
        P(rows, None, None),
    )
    out_specs = (
        P(rows, None, None),
        P(rows, None, None),
        P(),
        P(),
        P(),
        P(),
        P(PLANE, None, "dp"),
        P(PLANE, None, "dp"),
    )
    return jax.shard_map(local, mesh=parts, in_specs=in_specs, out_specs=out_specs, check_vma=False)
```

```python
import functools
import math

import jax
import jax.numpy as jnp
from jax import lax
from jax.experimental import pallas as pl
from jax.experimental.pallas import tpu as pltpu
from jax.sharding import Mesh, PartitionSpec as P

HEADS = 12
HEAD_DIM = 64
EPSILON = 1e-05
NEGATIVE = -1e30
SCALE = HEAD_DIM ** (-0.5)
BF = jnp.bfloat16
F32 = jnp.float32
PLANE = ("y", "x", "core")


def nn(a, b):
    return lax.dot_general(a, b, (((1,), (0,)), ((), ())), preferred_element_type=F32)


def nt(a, b):
    return lax.dot_general(a, b, (((1,), (1,)), ((), ())), preferred_element_type=F32)


def tn(a, b):
    return lax.dot_general(a, b, (((0,), (0,)), ((), ())), preferred_element_type=F32)


def iota(shape, dim):
    return lax.broadcasted_iota(jnp.int32, shape, dim)


def call(body, flops=0, moved=0, limit=60, **kw):
    return pl.pallas_call(
        body,
        compiler_params=pltpu.CompilerParams(vmem_limit_bytes=limit << 20),
        cost_estimate=pl.CostEstimate(
            flops=int(flops), bytes_accessed=int(moved), transcendentals=0
        ),
        **kw,
    )


def whole(shape):
    return pl.BlockSpec(shape, lambda *i: (0,) * len(shape))


def norm_parts(v):
    centred = v - jnp.mean(v, axis=-1, keepdims=True)
    rate = lax.rsqrt(jnp.mean(centred * centred, axis=-1, keepdims=True) + EPSILON)
    return centred * rate, rate


def norm_grad(x_hat, rate, u):
    return rate * (
        u
        - jnp.mean(u, axis=-1, keepdims=True)
        - x_hat * jnp.mean(u * x_hat, axis=-1, keepdims=True)
    )


def route_body(
    ids_ref, table_ref, cot_ref, row_ref, col_ref, first_ref, send_ref, *, sides, capacity
):
    high_side, low_side = sides
    count = ids_ref.shape[1]
    ids = ids_ref[...]
    table = table_ref[...].astype(BF)
    high = (iota((table.shape[0], count), 0) == (ids >> 7)).astype(BF)
    picked = tn(table, high)
    low = iota((128, count), 0) == (ids & 127)
    chosen = jnp.sum(jnp.where(low, picked, 0.0), axis=0, keepdims=True).astype(jnp.int32)
    bits = low_side.bit_length()
    here = [lax.axis_index(axis) for axis in PLANE]
    part_y = ((chosen >> bits) - here[0]) & (high_side - 1)
    part_x = ((chosen >> 1) - here[1]) & (low_side - 1)
    part_core = (chosen - here[2]) & 1
    relative = (part_y * low_side + part_x) * 2 + part_core
    slots = max(16, send_ref.shape[0])
    member = iota((slots, count), 0) == relative
    before = (iota((count, count), 0) < iota((count, count), 1)).astype(BF)
    earlier = nn(member.astype(BF), before)
    rank = jnp.sum(jnp.where(member, earlier, 0.0), axis=0, keepdims=True)
    target = relative.astype(F32) * capacity + rank
    row = target.astype(jnp.int32)
    row_ref[...] = row
    first = chosen.astype(F32) * capacity + rank
    turned = jnp.transpose(jnp.concatenate([target, first] * 4, 0))
    col_ref[...] = turned[:, :1].astype(jnp.int32)
    first_ref[...] = turned[:, 1:2].astype(jnp.int32)
    first = first.astype(jnp.int32)
    place([send_ref.at[part] for part in range(send_ref.shape[0])], first, cot_ref, capacity)


def place(send_refs, row, rows_ref, capacity):
    for part, send_ref in enumerate(send_refs):
        placer = (iota((capacity, row.shape[1]), 0) + part * capacity == row).astype(BF)
        send_ref[...] = nn(placer, rows_ref[...]).astype(BF)


def route(ids, table, cot, sides, capacity):
    count, width = cot.shape
    experts = 2 * sides[0] * sides[1]
    slots = experts * capacity
    return call(
        functools.partial(route_body, sides=sides, capacity=capacity),
        flops=2 * slots * count * width,
        moved=2 * (count + slots) * width,
        out_shape=[
            jax.ShapeDtypeStruct((1, count), jnp.int32),
            jax.ShapeDtypeStruct((count, 1), jnp.int32),
            jax.ShapeDtypeStruct((count, 1), jnp.int32),
            jax.ShapeDtypeStruct((experts, capacity, width), BF),
        ],
    )(ids, table, cot)


def packed_body(x_ref, gain_ref, w_ref, packed_ref, normed_ref):
    x_hat, _ = norm_parts(x_ref[...].astype(F32))
    normed = (x_hat * gain_ref[...]).astype(BF)
    packed_ref[...] = nn(normed, w_ref[...]).astype(BF)
    normed_ref[...] = normed


def make_packed(x, gain, w):
    count, width = x.shape
    wide = w.shape[1]
    block = 256
    return call(
        packed_body,
        flops=2 * count * width * wide,
        moved=2 * (count * (2 * width + wide) + width * wide),
        grid=(count // block,),
        in_specs=[
            pl.BlockSpec((block, width), lambda i: (i, 0)),
            whole(gain.shape),
            whole(w.shape),
        ],
        out_specs=[
            pl.BlockSpec((block, wide), lambda i: (i, 0)),
            pl.BlockSpec((block, width), lambda i: (i, 0)),
        ],
        out_shape=[
            jax.ShapeDtypeStruct((count, wide), BF),
            jax.ShapeDtypeStruct((count, width), BF),
        ],
    )(x, gain, w)


def attend_body(q_ref, k_ref, v_ref, o_ref, total_ref, *, block):
    length = q_ref.shape[0]
    lane = iota((1, 128), 1)
    v_turned = jnp.transpose(v_ref[...])
    allowed = iota((block, block), 0) <= iota((block, block), 1)
    for row in range(length // block):
        end = (row + 1) * block
        outs = []
        for head in range(2):
            q = jnp.where(lane // 64 == head, q_ref[row * block : end, :] * BF(SCALE), BF(0))
            s = nt(k_ref[:end, :], q)
            last = jnp.where(allowed, s[end - block :], NEGATIVE)
            s = jnp.concatenate([s[: end - block], last], 0) if row else last
            highest = jnp.max(s, 0, keepdims=True)
            p = jnp.exp(s - highest)
            summed = jnp.sum(p, 0, keepdims=True)
            out = nn(v_turned[head * 64 : (head + 1) * 64, :end], p.astype(BF))
            outs.append(out * (1.0 / summed))
            total_ref[0, head : head + 1, row * block : end] = highest + jnp.log(summed)
        o_ref[row * block : end, :] = jnp.transpose(jnp.concatenate(outs, 0)).astype(BF)


def attend(packed):
    length = packed.shape[0]
    pairs = packed.shape[1] // 384
    part = lambda o: pl.BlockSpec((length, 128), lambda i: (0, o * pairs + i))
    return call(
        functools.partial(attend_body, block=min(512, length)),
        flops=1.2e10,
        moved=2 * length * pairs * 512,
        grid=(pairs,),
        in_specs=[part(0), part(1), part(2)],
        out_specs=[part(0), pl.BlockSpec((1, 2, length), lambda i: (i, 0, 0))],
        out_shape=[
            jax.ShapeDtypeStruct((length, pairs * 128), BF),
            jax.ShapeDtypeStruct((pairs, 2, length), F32),
        ],
    )(packed, packed, packed)


def attend_back_body(
    q_ref, k_ref, v_ref, o_ref, up_ref, total_ref, out_ref, acc_ref, *, block
):
    length = q_ref.shape[0]
    count = length // block
    lane = iota((1, 128), 1)
    inner = jnp.transpose(o_ref[...].astype(F32) * up_ref[...].astype(F32))
    inner = [jnp.sum(inner[:64], 0, keepdims=True), jnp.sum(inner[64:], 0, keepdims=True)]
    allowed = iota((block, block), 0) <= iota((block, block), 1)
    for part in range(count):
        begin, end = part * block, (part + 1) * block
        k = k_ref[begin:end, :]
        v = v_ref[begin:end, :]
        dk, dv = [], []
        for head in range(2):
            mine = lane // 64 == head
            q = jnp.where(mine, q_ref[begin:, :] * BF(SCALE), BF(0))
            up = jnp.where(mine, up_ref[begin:, :], BF(0))
            s = nt(k, q) - total_ref[0, head : head + 1, begin:]
            first = jnp.where(allowed, s[:, :block], NEGATIVE)
            s = jnp.concatenate([first, s[:, block:]], 1) if part < count - 1 else first
            p = jnp.exp(s)
            ds = (p * (nt(v, up) - inner[head][:, begin:])).astype(BF)
            dv.append(nn(p.astype(BF), up))
            dk.append(nn(ds, q))
            dq = tn(ds, jnp.where(mine, k * BF(SCALE), BF(0)))
            if part == 0 and head == 0:
                acc_ref[...] = dq
            else:
                acc_ref[begin:, :] += dq
        out_ref[1, begin:end, :] = (dk[0] + dk[1]).astype(BF)
        out_ref[2, begin:end, :] = (dv[0] + dv[1]).astype(BF)
    out_ref[0] = acc_ref[...].astype(BF)


def attend_back(packed, attended, totals, upstream):
    length = packed.shape[0]
    pairs = packed.shape[1] // 384
    part = lambda o: pl.BlockSpec((length, 128), lambda i: (0, o * pairs + i))
    return call(
        functools.partial(attend_back_body, block=min(256, length)),
        flops=3e10,
        moved=2 * length * pairs * 1024,
        grid=(pairs,),
        in_specs=[
            part(0), part(1), part(2), part(0), part(0),
            pl.BlockSpec((1, 2, length), lambda i: (i, 0, 0)),
        ],
        out_specs=pl.BlockSpec((3, length, 128), lambda i: (0, 0, i)),
        out_shape=jax.ShapeDtypeStruct((3, length, pairs * 128), BF),
        scratch_shapes=[pltpu.VMEM((length, 128), F32)],
    )(packed, packed, packed, attended, upstream, totals)


def dispatch_body(att_ref, w_ref, x_ref, gain_ref, row_ref, res_ref, *rest):
    send_refs, normed_ref = rest[:-1], rest[-1]
    for begin in range(0, att_ref.shape[0], 256):
        rows = slice(begin, begin + 256)
        residual = x_ref[rows, :].astype(F32) + nn(att_ref[rows, :], w_ref[...])
        res_ref[rows, :] = residual
        x_hat, _ = norm_parts(residual)
        normed_ref[rows, :] = (x_hat * gain_ref[...]).astype(BF)
    place(send_refs, row_ref[...], normed_ref, send_refs[0].shape[0])


def dispatch(attended, w, x, gain, row, experts, capacity):
    count, width = x.shape
    slots = experts * capacity
    return call(
        dispatch_body,
        flops=2 * count * width * (slots + width),
        moved=2 * width * (5 * count + slots),
        out_shape=[jax.ShapeDtypeStruct((count, width), F32)]
        + [jax.ShapeDtypeStruct((capacity, width), BF)] * experts,
        scratch_shapes=[pltpu.VMEM((count, width), BF)],
    )(attended, w, x, gain, row)


def expert_body(from_ref, *refs, parts, kept):
    x_refs, g_refs = refs[:parts], refs[parts : 2 * parts]
    w_ref, out_w_ref = refs[2 * parts : 2 * parts + 2]
    act_ref, gh_ref, x_ref, g_ref, *back_refs = refs[2 * parts + 2 + kept : -1]
    acc_ref = refs[-1]
    step = pl.program_id(0)
    size = x_refs[0].shape[0]
    c1 = 2.0 * math.sqrt(2.0 / math.pi)
    c2 = c1 * 0.044715

    @pl.when(step == 0)
    def _():
        for part in range(parts):
            rows = slice(part * size, (part + 1) * size)
            x_ref[rows, :] = x_refs[part][...]
            g_ref[rows, :] = g_refs[part][0]

    h = nn(x_ref[...], w_ref[...])
    ga = nn(g_ref[...], out_w_ref[...])
    square = h * h
    half = jnp.tanh(h * (0.5 * c1 + (0.5 * c2) * square)) * 0.5 + 0.5
    act = h * half
    slope = half + (act * (1.0 - half)) * (c1 + (3.0 * c2) * square)
    act_ref[...] = act.astype(BF)
    gh = (ga * slope).astype(BF)
    gh_ref[...] = gh
    back = nt(gh, w_ref[...])

    @pl.when(step == 0)
    def _():
        acc_ref[...] = back

    @pl.when(step > 0)
    def _():
        acc_ref[...] += back

    @pl.when(step == pl.num_programs(0) - 1)
    def _():
        for part in range(parts):
            back_refs[part][...] = acc_ref[part * size : (part + 1) * size, :].astype(BF)


def expert(chips, place_at, total, source, xs, g, w, out_w, earlier):
    parts = len(xs)
    size, width = xs[0].shape
    units = w.shape[1]
    block = min(1024, units)
    tall = parts * size
    tile = pl.BlockSpec((tall, block), lambda i, s: (place_at, i))
    rows = pl.BlockSpec((tall, width), lambda i, s: (place_at, 0))
    weight = pl.BlockSpec((width, block), lambda i, s: (0, i))
    pick = lambda k: pl.BlockSpec((1, size, width), lambda i, s: (s[k], 0, 0))
    every = total * size
    return pl.pallas_call(
        functools.partial(expert_body, parts=parts, kept=len(earlier)),
        grid_spec=pltpu.PrefetchScalarGridSpec(
            num_scalar_prefetch=1,
            grid=(units // block,),
            in_specs=[whole((size, width))] * parts
            + [pick(2 * chip + core) for chip in chips for core in range(2)]
            + [weight, weight]
            + [pl.BlockSpec(memory_space=pl.ANY)] * len(earlier),
            out_specs=[tile, tile, rows, rows] + [whole((size, width))] * parts,
            scratch_shapes=[pltpu.VMEM((tall, width), F32)],
        ),
        out_shape=[jax.ShapeDtypeStruct((every, units), BF)] * 2
        + [jax.ShapeDtypeStruct((every, width), BF)] * 2
        + [jax.ShapeDtypeStruct((size, width), BF)] * parts,
        input_output_aliases={1 + 2 * parts + 2 + i: i for i in range(len(earlier))},
        compiler_params=pltpu.CompilerParams(vmem_limit_bytes=60 << 20),
        cost_estimate=pl.CostEstimate(
            flops=6 * tall * width * units,
            bytes_accessed=2 * (5 * tall * width + 2 * width * units + 2 * tall * units),
            transcendentals=0,
        ),
    )(source, *xs, *[g] * parts, w, out_w, *earlier)


def weight_share_body(g_ref, act_ref, out_ref):
    out_ref[...] = tn(g_ref[...], act_ref[...]).astype(BF)


def weight_share(g, act, shares, begin, size):
    rows, width = g.shape
    share = act.shape[1] // shares
    block = math.gcd(768, size)
    per = size // block
    pick = pl.BlockSpec(
        (pl.Element(rows), pl.Element(block)),
        lambda i: (0, pl.multiple_of(i // per * share + begin + i % per * block, 128)),
    )
    return call(
        weight_share_body,
        flops=2 * rows * width * shares * size,
        moved=2 * (rows * width + rows * shares * size + width * shares * size),
        grid=(shares * per,),
        in_specs=[whole(g.shape), pick],
        out_specs=pl.BlockSpec((width, block), lambda i: (0, i)),
        out_shape=jax.ShapeDtypeStruct((width, shares * size), BF),
    )(g, act)


def result_body(chip_ref, act_ref, w_ref, out_ref):
    size = out_ref.shape[1]
    out = nt(act_ref[...], w_ref[...]).astype(BF)
    same = lax.axis_index("core") == 0

    @pl.when(same)
    def _():
        out_ref[0] = out[:size]
        out_ref[1] = out[size:]

    @pl.when(jnp.logical_not(same))
    def _():
        out_ref[0] = out[size:]
        out_ref[1] = out[:size]


def make_result(chips, active, w, experts):
    rows, units = active.shape
    width = w.shape[0]
    size = rows // experts
    return pl.pallas_call(
        result_body,
        grid_spec=pltpu.PrefetchScalarGridSpec(
            num_scalar_prefetch=1,
            grid=(experts // 2,),
            in_specs=[
                pl.BlockSpec((2 * size, units), lambda i, s: (i, 0)),
                pl.BlockSpec(w.shape, lambda i, s: (0, 0)),
            ],
            out_specs=pl.BlockSpec((2, size, width), lambda i, s: (s[i], 0, 0)),
        ),
        out_shape=jax.ShapeDtypeStruct((experts, size, width), BF),
        compiler_params=pltpu.CompilerParams(vmem_limit_bytes=60 << 20),
        cost_estimate=pl.CostEstimate(
            flops=2 * rows * units * width,
            bytes_accessed=2 * (rows * units + units * width + rows * width),
            transcendentals=0,
        ),
    )(chips, active, w)


def unplace(back_refs, col, rows_ref):
    size = back_refs[0].shape[0]

    @pl.when(pl.program_id(0) == 0)
    def _():
        for part, back_ref in enumerate(back_refs):
            rows_ref[part * size : (part + 1) * size, :] = back_ref[...]

    placer = (iota((col.shape[0], rows_ref.shape[0]), 1) == col).astype(BF)
    return nn(placer, rows_ref[...])


def collect_back_body(col_ref, res_ref, cot_ref, gain_ref, w_ref, *rest):
    back_refs, (gres_ref, gattn_ref, gatt_ref, ggain_ref, rows_ref) = rest[:-5], rest[-5:]
    step = pl.program_id(0)
    grad = unplace(back_refs, col_ref[...], rows_ref)
    x_hat, rate = norm_parts(res_ref[...])
    gres = cot_ref[...].astype(F32) + norm_grad(x_hat, rate, grad * gain_ref[...])
    gres_ref[...] = gres
    gain_part = jnp.sum(grad * x_hat, axis=0, keepdims=True)
    gattn = gres.astype(BF)
    gattn_ref[...] = gattn
    gatt_ref[...] = nt(gattn, w_ref[...]).astype(BF)

    @pl.when(step == 0)
    def _():
        ggain_ref[...] = gain_part

    @pl.when(step > 0)
    def _():
        ggain_ref[...] += gain_part


def collect_back(backs, col, residual, cot, gain, w):
    count, width = cot.shape
    size = backs[0].shape[0]
    block = 256
    row = pl.BlockSpec((block, width), lambda i: (i, 0))
    return call(
        collect_back_body,
        flops=2 * count * width * (len(backs) * size + 2 * width),
        moved=2 * width * (len(backs) * size + 8 * count),
        grid=(count // block,),
        in_specs=[
            pl.BlockSpec((block, 1), lambda i: (i, 0)), row, row,
            whole(gain.shape), whole(w.shape),
        ]
        + [whole((size, width))] * len(backs),
        out_specs=[row, row, row, whole((1, width))],
        out_shape=[
            jax.ShapeDtypeStruct((count, width), F32),
            jax.ShapeDtypeStruct((count, width), BF),
            jax.ShapeDtypeStruct((count, width), BF),
            jax.ShapeDtypeStruct((1, width), F32),
        ],
        scratch_shapes=[pltpu.VMEM((len(backs) * size, width), BF)],
    )(col, residual, cot, gain, w, *backs)


def collect_body(col_ref, res_ref, back_ref, out_ref):
    placer = (iota((col_ref.shape[0], back_ref.shape[0]), 1) == col_ref[...]).astype(BF)
    out_ref[...] = (res_ref[...] + nn(placer, back_ref[...])).astype(BF)


def collect(back, col, residual):
    count, width = residual.shape
    block = 256
    row = pl.BlockSpec((block, width), lambda i: (i, 0))
    return call(
        collect_body,
        flops=2 * count * width * back.shape[0],
        moved=2 * width * (back.shape[0] + 3 * count),
        grid=(count // block,),
        in_specs=[pl.BlockSpec((block, 1), lambda i: (i, 0)), row, whole(back.shape)],
        out_specs=row,
        out_shape=jax.ShapeDtypeStruct((count, width), BF),
    )(col, residual, back)


def weight_grad_body(normed_ref, g_ref, att_ref, gattn_ref, keep_ref, send_ref):
    step = pl.program_id(0)
    width = g_ref.shape[2]
    last = step == pl.num_programs(0) - 1
    rows = jnp.where(last, gattn_ref[...], g_ref[0])
    left = jnp.where(last, att_ref[...], normed_ref[...])
    out = tn(left, rows).astype(BF)
    mine = step // 2 == lax.axis_index("core")
    for half in range(2):
        columns = slice(half * width, (half + 1) * width)

        @pl.when((step % 2 == half) & mine)
        def _():
            keep_ref[:, columns] = out

        @pl.when((step % 2 == half) & jnp.logical_not(mine))
        def _():
            send_ref[:, columns] = out


def weight_grads(normed, g, attended, gattn):
    count, width = normed.shape
    out = jax.ShapeDtypeStruct((width, 2 * width), BF)
    return call(
        weight_grad_body,
        flops=8 * width * count * width,
        moved=2 * (6 * width * count + 4 * width * width),
        grid=(4,),
        in_specs=[
            whole(normed.shape),
            pl.BlockSpec((1, count, width), lambda i: (jnp.minimum(i, 2), 0, 0)),
            whole(attended.shape),
            whole(gattn.shape),
        ],
        out_specs=[whole(out.shape)] * 2,
        out_shape=[out] * 2,
    )(normed, g, attended, gattn)


def grad_in_body(x_ref, gain_ref, w_ref, g_ref, gres_ref, out_ref, ggain_ref):
    step = pl.program_id(0)
    width = x_ref.shape[1]
    x_hat, rate = norm_parts(x_ref[...].astype(F32))
    grad = nt(g_ref[0], w_ref[:, :width])
    grad += nt(g_ref[1], w_ref[:, width : 2 * width])
    grad += nt(g_ref[2], w_ref[:, 2 * width :])
    out_ref[...] = gres_ref[...] + norm_grad(x_hat, rate, grad * gain_ref[...])
    part = jnp.sum(grad * x_hat, axis=0, keepdims=True)

    @pl.when(step == 0)
    def _():
        ggain_ref[...] = part

    @pl.when(step > 0)
    def _():
        ggain_ref[...] += part


def grad_in(x, gain, w, g, gres):
    count, width = x.shape
    block = 256
    row = pl.BlockSpec((block, width), lambda i: (i, 0))
    return call(
        grad_in_body,
        flops=6 * count * width * width,
        moved=2 * width * 9 * count,
        grid=(count // block,),
        in_specs=[
            row, whole(gain.shape), whole(w.shape),
            pl.BlockSpec((3, block, width), lambda i: (0, i, 0)), row,
        ],
        out_specs=[row, whole((1, width))],
        out_shape=[
            jax.ShapeDtypeStruct((count, width), F32),
            jax.ShapeDtypeStruct((1, width), F32),
        ],
    )(x, gain, w, g, gres)


def shift(a, axis, k):
    n = lax.axis_size(axis)
    return lax.ppermute(a, axis, [(i, (i + k) % n) for i in range(n)])


def groups(chips):
    sizes = [1]
    while sum(sizes) < chips:
        sizes.append((chips - sum(sizes) + 1) // 2)
    out, begin, at = [], 0, chips
    tall = sorted(sizes, reverse=True)
    for i, size in enumerate(sizes):
        rank = tall.index(size) + sizes[:i].count(size)
        out.append((tuple(range(begin, begin + size)), sum(tall[:rank]) // size))
        begin += size
    return out


def source_parts(sides):
    high, low = sides
    y, x, core = (lax.axis_index(axis) for axis in PLANE)
    out = []
    for dy in range(high):
        for dx in range(low):
            for dc in range(2):
                chip = lax.rem(y + high - dy, high) * low + lax.rem(x + low - dx, low)
                out.append(chip * 2 + lax.rem(core + dc, 2))
    return jnp.stack(out).astype(jnp.int32)


def plane_shift(a, part, sign, sides):
    if part == 0:
        return a
    high, low = sides
    dy, dx, dc = sign * (part // (2 * low)), sign * (part // 2 % low), part % 2
    pairs = []
    for y in range(high):
        for x in range(low):
            for core in range(2):
                to = ((y + dy) % high * low + (x + dx) % low) * 2 + (core + dc) % 2
                pairs.append(((y * low + x) * 2 + core, to))
    return lax.ppermute(a, PLANE, pairs)


def cut(a, index, pieces, dim):
    size = a.shape[dim] // pieces
    return lax.dynamic_slice_in_dim(a, index * size, size, dim)


def scatter_sum(a, axis, dim):
    n = lax.axis_size(axis)
    me = lax.axis_index(axis)
    total = cut(a, me, n, dim).astype(F32)
    for k in range(1, n):
        total += shift(cut(a, lax.rem(me + k, n), n, dim), axis, k).astype(F32)
    return total.astype(a.dtype)


def gather_all(a, axis, dim):
    n = lax.axis_size(axis)
    me = lax.axis_index(axis)
    size = a.shape[dim]
    shape = a.shape[:dim] + (n * size,) + a.shape[dim + 1 :]
    out = lax.dynamic_update_slice_in_dim(jnp.zeros(shape, a.dtype), a, me * size, dim)
    for k in range(1, n):
        got = shift(a, axis, k)
        out = lax.dynamic_update_slice_in_dim(out, got, lax.rem(me - k + n, n) * size, dim)
    return out


def after(value, *first):
    return lax.optimization_barrier((value, first))[0]


def split_body(keep_ref, got_ref, one_ref, two_ref, *out_refs, ways):
    wide = keep_ref.shape[1]
    half = keep_ref.shape[0] // 2
    turned = jnp.transpose(
        jnp.concatenate([one_ref[...], two_ref[...]] + [jnp.zeros_like(one_ref[...])] * 6, 0)
    )
    turned = jnp.concatenate([turned, jnp.zeros((turned.shape[0], 120), F32)], 1)
    at = 0
    for begin, axis, count in ((0, "x", ways[1]), (half, "y", ways[0])):
        size = half // count
        me = lax.axis_index(axis)
        for k in range(count):
            piece = lax.rem(me + k, count)
            rows = pl.ds(pl.multiple_of(begin + piece * size, 8), size)
            out = out_refs[at]
            out[:, :wide] = (keep_ref[rows, :].astype(F32) + got_ref[rows, :].astype(F32)).astype(BF)
            for other in range(count):

                @pl.when(piece == other)
                def _():
                    begin_here = begin + other * size
                    out[:, wide:] = turned[begin_here : begin_here + size].astype(BF)

            at += 1


def split(keep, got, one, two, ways):
    rows, wide = keep.shape
    sizes = [rows // 2 // ways[1]] * ways[1] + [rows // 2 // ways[0]] * ways[0]
    outs = call(
        functools.partial(split_body, ways=ways),
        moved=6 * rows * wide,
        out_shape=[jax.ShapeDtypeStruct((size, wide + 128), BF) for size in sizes],
    )(keep, got, one, two)
    return outs[: ways[1]], outs[ways[1] :]


def add_up(parts, axis):
    return [parts[0]] + [shift(a, axis, k) for k, a in enumerate(parts) if k]


def total(parts):
    out = parts[0].astype(F32)
    for a in parts[1:]:
        out += a.astype(F32)
    return out.astype(parts[0].dtype)


def sum_planes(top, low, first):
    top = scatter_sum(total(top), "y", 0)
    low = scatter_sum(total(low), "x", 0)
    both = scatter_sum(jnp.stack([top, low]), "dp", 1)
    both = after(both, first)
    return gather_all(both, "dp", 1), both


def gather_planes(both, during_last):
    top = gather_all(both[0], "y", 0)
    low = gather_all(both[1], "x", 0)
    top, low = after((top, low), *during_last)
    top = gather_all(top, "x", 0)
    low = gather_all(low, "y", 0)
    mine = jnp.concatenate([top, low], 0)
    return mine, shift(mine, "core", 1)


def unpack_body(mine_ref, other_ref, qkv_ref, proj_ref, one_ref, two_ref):
    width = proj_ref.shape[1]
    first = lax.axis_index("core") == 0
    gains = mine_ref[:, 2 * width :].astype(F32) + other_ref[:, 2 * width :].astype(F32)
    gains = jnp.transpose(gains)
    one_ref[...] = gains[:1]
    two_ref[...] = gains[1:2]

    @pl.when(first)
    def _():
        qkv_ref[:, : 2 * width] = mine_ref[:, : 2 * width].astype(F32)
        qkv_ref[:, 2 * width :] = other_ref[:, :width].astype(F32)
        proj_ref[...] = other_ref[:, width : 2 * width].astype(F32)

    @pl.when(jnp.logical_not(first))
    def _():
        qkv_ref[:, : 2 * width] = other_ref[:, : 2 * width].astype(F32)
        qkv_ref[:, 2 * width :] = mine_ref[:, :width].astype(F32)
        proj_ref[...] = mine_ref[:, width : 2 * width].astype(F32)


def unpack(mine, other):
    width = mine.shape[0]
    block = min(256, width)
    row = lambda wide: pl.BlockSpec((block, wide), lambda i: (i, 0))
    return call(
        unpack_body,
        moved=24 * width * width,
        grid=(width // block,),
        in_specs=[row(mine.shape[1])] * 2,
        out_specs=[row(3 * width), row(width)] + [pl.BlockSpec((1, block), lambda i: (0, i))] * 2,
        out_shape=[
            jax.ShapeDtypeStruct((width, 3 * width), F32),
            jax.ShapeDtypeStruct((width, width), F32),
            jax.ShapeDtypeStruct((1, width), F32),
            jax.ShapeDtypeStruct((1, width), F32),
        ],
    )(mine, other)


def widen_body(*refs):
    at = 0
    for ref in refs[:-1]:
        refs[-1][:, :, at : at + ref.shape[2]] = ref[...].astype(F32)
        at += ref.shape[2]


def widen(*parts):
    rows = parts[0].shape[1]
    wide = sum(a.shape[2] for a in parts)
    block = lambda columns: pl.BlockSpec((1, rows // 2, columns), lambda i: (0, i, 0))
    return call(
        widen_body,
        moved=6 * rows * wide,
        grid=(2,),
        in_specs=[block(a.shape[2]) for a in parts],
        out_specs=block(wide),
        out_shape=jax.ShapeDtypeStruct((1, rows, wide), F32),
    )(*parts)


def local(tokens, token_ids, hash_table, gain_one, w_qkv, w_proj, gain_two, w_in, w_out, cotangent):
    width = tokens.shape[-1]
    x = tokens.reshape(-1, width)
    cot = cotangent.reshape(-1, width)
    count = x.shape[0]
    sides = (lax.axis_size("y"), lax.axis_size("x"))
    experts = lax.axis_size(PLANE)
    capacity = 2 * count // experts
    first_gain = gain_one.reshape(1, width)
    second_gain = gain_two.reshape(1, width)
    inner, outer = w_in[0], w_out[0]

    def exchange_all(a):
        return lax.all_to_all(a, PLANE, split_axis=0, concat_axis=0, tiled=True)

    def exchange(parts, sign):
        return {i: plane_shift(a, i, sign, sides) for i, a in parts.items()}

    row, col, first_col, grad_send = route(
        token_ids.reshape(1, count), hash_table.reshape(-1, 128), cot, sides, capacity
    )
    flat_grad = exchange_all(grad_send)
    packed, normed = make_packed(x, first_gain, w_qkv)
    attended, totals = attend(packed)
    residual, *outgoing = dispatch(attended, w_proj, x, second_gain, row, experts, capacity)
    outgoing = dict(enumerate(outgoing))
    far = {i: outgoing.pop(i) for i in range(experts - 2, experts)}
    arrived = exchange(outgoing, 1)
    source = source_parts(sides)
    kept, backs = (), {}
    plan = groups(experts // 2)
    for chips, place_at in plan:
        parts = [2 * chip + core for chip in chips for core in range(2)]
        flat = after(flat_grad, *[backs[i] for i in sorted(backs) if i < 2 and len(parts) < 4])
        out = expert(
            chips, place_at, experts, source, [arrived[i] for i in parts], flat,
            inner, outer, kept,
        )
        kept = out[:4]
        backs.update(exchange(dict(zip(parts, out[4:])), -1))
        if chips == (0,):
            near = [arrived[i] for i in range(2, experts - 2)]
            arrived.update(exchange(after(far, near, kept[0]), 1))
    active, grad_hidden, rows_in, rows_grad = kept
    shares = lax.axis_size("dp")
    share = inner.shape[1] // shares
    near_backs = [backs[i] for i in range(experts - 2)]
    grad_back = near_backs + [backs[i] for i in range(experts - 2, experts)]
    def scatter(a):
        return lax.psum_scatter(a[None], "dp", scatter_dimension=2, tiled=True)

    grad_outer = weight_share(after(rows_grad, *near_backs), active, shares, 0, share)
    grad_w_out = widen(scatter(grad_outer))
    part = share * 2 // 3 // 256 * 256
    grad_inner = weight_share(after(rows_in, grad_outer), grad_hidden, shares, 0, part)
    grad_w_in = [scatter(grad_inner)]
    tall_first = sorted((chips for chips, _ in plan), key=lambda chips: (-len(chips), chips))
    order = [chip for chips in tall_first for chip in chips]
    chips = jnp.stack([source[2 * chip] // 2 for chip in order])
    results = make_result(chips, after(active, grad_inner), outer, experts)
    returned = exchange_all(results)

    grad_residual, grad_attn, grad_attended, grad_gain_two = collect_back(
        after(grad_back, results), col, residual, cot, second_gain, w_proj
    )
    grad_packed = attend_back(packed, attended, totals, grad_attended)
    returned, grad_packed = after((returned, grad_packed), grad_packed)
    keep, send = weight_grads(normed, grad_packed, attended, grad_attn)
    got = shift(send, "core", 1)
    grad_tokens, grad_gain_one = grad_in(
        x, first_gain, w_qkv, after(grad_packed, keep, grad_w_out), grad_residual
    )
    top, low = split(keep, after(got, grad_tokens), grad_gain_one, grad_gain_two, sides)
    grad_later = weight_share(
        after(rows_in, top, low), grad_hidden, shares, part, share - part
    )
    outputs = collect(after(returned.reshape(-1, width), grad_later), first_col, residual)
    top, low = after((add_up(top, "x"), add_up(low, "y")), outputs)
    both, summed = sum_planes(top, low, grad_w_in[0])
    grad_w_in.append(scatter(after(grad_later, summed)))
    grad_qkv, grad_proj, one, two = unpack(*gather_planes(both, ()))
    grad_w_in = widen(grad_w_in[0], after(grad_w_in[1], grad_qkv))
    return (
        outputs.reshape(tokens.shape),
        grad_tokens.reshape(tokens.shape),
        one.reshape(width),
        grad_qkv,
        grad_proj,
        two.reshape(width),
        grad_w_in,
        grad_w_out,
    )


def solution(mesh):
    dp, experts = mesh.devices.shape
    side = math.isqrt(experts // 2)
    parts = Mesh(mesh.devices.reshape(dp, side, experts // 2 // side, 2), ("dp", "y", "x", "core"))
    rows = ("dp",) + PLANE
    in_specs = (
        P(rows, None, None),
        P(rows, None),
        P(),
        P(),
        P(),
        P(),
        P(),
        P(PLANE, None, None),
        P(PLANE, None, None),
        P(rows, None, None),
    )
    out_specs = (
        P(rows, None, None),
        P(rows, None, None),
        P(),
        P(),
        P(),
        P(),
        P(PLANE, None, "dp"),
        P(PLANE, None, "dp"),
    )
    return jax.shard_map(local, mesh=parts, in_specs=in_specs, out_specs=out_specs, check_vma=False)
```

```python
import functools
import math

import jax
import jax.numpy as jnp
from jax import lax
from jax.experimental import pallas as pl
from jax.experimental.pallas import tpu as pltpu
from jax.sharding import Mesh, PartitionSpec as P

HEADS = 12
HEAD_DIM = 64
EPSILON = 1e-05
NEGATIVE = -1e30
SCALE = HEAD_DIM ** (-0.5)
BF = jnp.bfloat16
F32 = jnp.float32
PLANE = ("y", "x", "core")


def nn(a, b):
    return lax.dot_general(a, b, (((1,), (0,)), ((), ())), preferred_element_type=F32)


def nt(a, b):
    return lax.dot_general(a, b, (((1,), (1,)), ((), ())), preferred_element_type=F32)


def tn(a, b):
    return lax.dot_general(a, b, (((0,), (0,)), ((), ())), preferred_element_type=F32)


def iota(shape, dim):
    return lax.broadcasted_iota(jnp.int32, shape, dim)


def call(body, flops=0, moved=0, limit=60, **kw):
    return pl.pallas_call(
        body,
        compiler_params=pltpu.CompilerParams(vmem_limit_bytes=limit << 20),
        cost_estimate=pl.CostEstimate(
            flops=int(flops), bytes_accessed=int(moved), transcendentals=0
        ),
        **kw,
    )


def whole(shape):
    return pl.BlockSpec(shape, lambda *i: (0,) * len(shape))


def norm_parts(v):
    centred = v - jnp.mean(v, axis=-1, keepdims=True)
    rate = lax.rsqrt(jnp.mean(centred * centred, axis=-1, keepdims=True) + EPSILON)
    return centred * rate, rate


def norm_grad(x_hat, rate, u):
    return rate * (
        u
        - jnp.mean(u, axis=-1, keepdims=True)
        - x_hat * jnp.mean(u * x_hat, axis=-1, keepdims=True)
    )


def route_body(
    ids_ref, table_ref, cot_ref, row_ref, col_ref, send_ref, *, sides, capacity
):
    high_side, low_side = sides
    count = ids_ref.shape[1]
    ids = ids_ref[...]
    table = table_ref[...].astype(BF)
    high = (iota((table.shape[0], count), 0) == (ids >> 7)).astype(BF)
    picked = tn(table, high)
    low = iota((128, count), 0) == (ids & 127)
    chosen = jnp.sum(jnp.where(low, picked, 0.0), axis=0, keepdims=True).astype(jnp.int32)
    bits = low_side.bit_length()
    here = [lax.axis_index(axis) for axis in PLANE]
    part_y = ((chosen >> bits) - here[0]) & (high_side - 1)
    part_x = ((chosen >> 1) - here[1]) & (low_side - 1)
    part_core = (chosen - here[2]) & 1
    relative = (part_y * low_side + part_x) * 2 + part_core
    slots = max(16, send_ref.shape[0])
    member = iota((slots, count), 0) == relative
    before = (iota((count, count), 0) < iota((count, count), 1)).astype(BF)
    earlier = nn(member.astype(BF), before)
    rank = jnp.sum(jnp.where(member, earlier, 0.0), axis=0, keepdims=True)
    target = relative.astype(F32) * capacity + rank
    row = target.astype(jnp.int32)
    row_ref[...] = row
    first = chosen.astype(F32) * capacity + rank
    turned = jnp.transpose(jnp.broadcast_to(first, (8, count)))
    col_ref[...] = turned[:, :1].astype(jnp.int32)
    first = first.astype(jnp.int32)
    place([send_ref.at[part] for part in range(send_ref.shape[0])], first, cot_ref, capacity)


def place(send_refs, row, rows_ref, capacity):
    for part, send_ref in enumerate(send_refs):
        placer = (iota((capacity, row.shape[1]), 0) + part * capacity == row).astype(BF)
        send_ref[...] = nn(placer, rows_ref[...]).astype(BF)


def route(ids, table, cot, sides, capacity):
    count, width = cot.shape
    experts = 2 * sides[0] * sides[1]
    slots = experts * capacity
    return call(
        functools.partial(route_body, sides=sides, capacity=capacity),
        flops=2 * slots * count * width,
        moved=2 * (count + slots) * width,
        out_shape=[
            jax.ShapeDtypeStruct((1, count), jnp.int32),
            jax.ShapeDtypeStruct((count, 1), jnp.int32),
            jax.ShapeDtypeStruct((experts, capacity, width), BF),
        ],
    )(ids, table, cot)


def packed_body(x_ref, gain_ref, w_ref, packed_ref, normed_ref):
    x_hat, _ = norm_parts(x_ref[...].astype(F32))
    normed = (x_hat * gain_ref[...]).astype(BF)
    packed_ref[...] = nn(normed, w_ref[...]).astype(BF)
    normed_ref[...] = normed


def make_packed(x, gain, w):
    count, width = x.shape
    wide = w.shape[1]
    block = 256
    return call(
        packed_body,
        flops=2 * count * width * wide,
        moved=2 * (count * (2 * width + wide) + width * wide),
        grid=(count // block,),
        in_specs=[
            pl.BlockSpec((block, width), lambda i: (i, 0)),
            whole(gain.shape),
            whole(w.shape),
        ],
        out_specs=[
            pl.BlockSpec((block, wide), lambda i: (i, 0)),
            pl.BlockSpec((block, width), lambda i: (i, 0)),
        ],
        out_shape=[
            jax.ShapeDtypeStruct((count, wide), BF),
            jax.ShapeDtypeStruct((count, width), BF),
        ],
    )(x, gain, w)


def attend_body(q_ref, k_ref, v_ref, o_ref, total_ref, *, block):
    length = q_ref.shape[0]
    lane = iota((1, 128), 1)
    v_turned = jnp.transpose(v_ref[...])
    allowed = iota((block, block), 0) <= iota((block, block), 1)
    for row in range(length // block):
        end = (row + 1) * block
        outs = []
        for head in range(2):
            q = jnp.where(lane // 64 == head, q_ref[row * block : end, :] * BF(SCALE), BF(0))
            s = nt(k_ref[:end, :], q)
            last = jnp.where(allowed, s[end - block :], NEGATIVE)
            s = jnp.concatenate([s[: end - block], last], 0) if row else last
            highest = jnp.max(s, 0, keepdims=True)
            p = jnp.exp(s - highest)
            summed = jnp.sum(p, 0, keepdims=True)
            out = nn(v_turned[head * 64 : (head + 1) * 64, :end], p.astype(BF))
            outs.append(out * (1.0 / summed))
            total_ref[0, head : head + 1, row * block : end] = highest + jnp.log(summed)
        o_ref[row * block : end, :] = jnp.transpose(jnp.concatenate(outs, 0)).astype(BF)


def attend(packed):
    length = packed.shape[0]
    pairs = packed.shape[1] // 384
    part = lambda o: pl.BlockSpec((length, 128), lambda i: (0, o * pairs + i))
    return call(
        functools.partial(attend_body, block=min(512, length)),
        flops=1.2e10,
        moved=2 * length * pairs * 512,
        grid=(pairs,),
        in_specs=[part(0), part(1), part(2)],
        out_specs=[part(0), pl.BlockSpec((1, 2, length), lambda i: (i, 0, 0))],
        out_shape=[
            jax.ShapeDtypeStruct((length, pairs * 128), BF),
            jax.ShapeDtypeStruct((pairs, 2, length), F32),
        ],
    )(packed, packed, packed)


def attend_back_body(
    q_ref, k_ref, v_ref, o_ref, up_ref, total_ref, out_ref, acc_ref, *, block
):
    length = q_ref.shape[0]
    count = length // block
    lane = iota((1, 128), 1)
    inner = jnp.transpose(o_ref[...].astype(F32) * up_ref[...].astype(F32))
    inner = [jnp.sum(inner[:64], 0, keepdims=True), jnp.sum(inner[64:], 0, keepdims=True)]
    allowed = iota((block, block), 0) <= iota((block, block), 1)
    for part in range(count):
        begin, end = part * block, (part + 1) * block
        k = k_ref[begin:end, :]
        v = v_ref[begin:end, :]
        dk, dv = [], []
        for head in range(2):
            mine = lane // 64 == head
            q = jnp.where(mine, q_ref[begin:, :] * BF(SCALE), BF(0))
            up = jnp.where(mine, up_ref[begin:, :], BF(0))
            s = nt(k, q) - total_ref[0, head : head + 1, begin:]
            first = jnp.where(allowed, s[:, :block], NEGATIVE)
            s = jnp.concatenate([first, s[:, block:]], 1) if part < count - 1 else first
            p = jnp.exp(s)
            ds = (p * (nt(v, up) - inner[head][:, begin:])).astype(BF)
            dv.append(nn(p.astype(BF), up))
            dk.append(nn(ds, q))
            dq = tn(ds, jnp.where(mine, k * BF(SCALE), BF(0)))
            if part == 0 and head == 0:
                acc_ref[...] = dq
            else:
                acc_ref[begin:, :] += dq
        out_ref[1, begin:end, :] = (dk[0] + dk[1]).astype(BF)
        out_ref[2, begin:end, :] = (dv[0] + dv[1]).astype(BF)
    out_ref[0] = acc_ref[...].astype(BF)


def attend_back(packed, attended, totals, upstream):
    length = packed.shape[0]
    pairs = packed.shape[1] // 384
    part = lambda o: pl.BlockSpec((length, 128), lambda i: (0, o * pairs + i))
    return call(
        functools.partial(attend_back_body, block=min(256, length)),
        flops=3e10,
        moved=2 * length * pairs * 1024,
        grid=(pairs,),
        in_specs=[
            part(0), part(1), part(2), part(0), part(0),
            pl.BlockSpec((1, 2, length), lambda i: (i, 0, 0)),
        ],
        out_specs=pl.BlockSpec((3, length, 128), lambda i: (0, 0, i)),
        out_shape=jax.ShapeDtypeStruct((3, length, pairs * 128), BF),
        scratch_shapes=[pltpu.VMEM((length, 128), F32)],
    )(packed, packed, packed, attended, upstream, totals)


def dispatch_body(att_ref, w_ref, x_ref, gain_ref, row_ref, res_ref, *rest):
    send_refs, normed_ref = rest[:-1], rest[-1]
    for begin in range(0, att_ref.shape[0], 256):
        rows = slice(begin, begin + 256)
        residual = x_ref[rows, :].astype(F32) + nn(att_ref[rows, :], w_ref[...])
        res_ref[rows, :] = residual
        x_hat, _ = norm_parts(residual)
        normed_ref[rows, :] = (x_hat * gain_ref[...]).astype(BF)
    place(send_refs, row_ref[...], normed_ref, send_refs[0].shape[0])


def dispatch(attended, w, x, gain, row, experts, capacity):
    count, width = x.shape
    slots = experts * capacity
    return call(
        dispatch_body,
        flops=2 * count * width * (slots + width),
        moved=2 * width * (5 * count + slots),
        out_shape=[jax.ShapeDtypeStruct((count, width), F32)]
        + [jax.ShapeDtypeStruct((capacity, width), BF)] * experts,
        scratch_shapes=[pltpu.VMEM((count, width), BF)],
    )(attended, w, x, gain, row)


def expert_body(from_ref, *refs, parts, kept):
    x_refs, g_refs = refs[:parts], refs[parts : 2 * parts]
    w_ref, out_w_ref = refs[2 * parts : 2 * parts + 2]
    act_ref, gh_ref, x_ref, g_ref = refs[2 * parts + 2 + kept :]
    step = pl.program_id(0)
    size = x_refs[0].shape[0]
    c1 = 2.0 * math.sqrt(2.0 / math.pi)
    c2 = c1 * 0.044715

    @pl.when(step == 0)
    def _():
        for part in range(parts):
            rows = slice(part * size, (part + 1) * size)
            x_ref[rows, :] = x_refs[part][...]
            g_ref[rows, :] = g_refs[part][0]

    h = nn(x_ref[...], w_ref[...])
    ga = nn(g_ref[...], out_w_ref[...])
    square = h * h
    half = jnp.tanh(h * (0.5 * c1 + (0.5 * c2) * square)) * 0.5 + 0.5
    act = h * half
    slope = half + (act * (1.0 - half)) * (c1 + (3.0 * c2) * square)
    act_ref[...] = act.astype(BF)
    gh_ref[...] = (ga * slope).astype(BF)


def expert(chips, place_at, total, source, xs, g, w, out_w, earlier):
    parts = len(xs)
    size, width = xs[0].shape
    units = w.shape[1]
    block = min(1024, units)
    tall = parts * size
    tile = pl.BlockSpec((tall, block), lambda i, s: (place_at, i))
    rows = pl.BlockSpec((tall, width), lambda i, s: (place_at, 0))
    weight = pl.BlockSpec((width, block), lambda i, s: (0, i))
    pick = lambda k: pl.BlockSpec((1, size, width), lambda i, s: (s[k], 0, 0))
    every = total * size
    return pl.pallas_call(
        functools.partial(expert_body, parts=parts, kept=len(earlier)),
        grid_spec=pltpu.PrefetchScalarGridSpec(
            num_scalar_prefetch=1,
            grid=(units // block,),
            in_specs=[whole((size, width))] * parts
            + [pick(2 * chip + core) for chip in chips for core in range(2)]
            + [weight, weight]
            + [pl.BlockSpec(memory_space=pl.ANY)] * len(earlier),
            out_specs=[tile, tile, rows, rows],
        ),
        out_shape=[jax.ShapeDtypeStruct((every, units), BF)] * 2
        + [jax.ShapeDtypeStruct((every, width), BF)] * 2,
        input_output_aliases={1 + 2 * parts + 2 + i: i for i in range(len(earlier))},
        compiler_params=pltpu.CompilerParams(vmem_limit_bytes=60 << 20),
        cost_estimate=pl.CostEstimate(
            flops=4 * tall * width * units,
            bytes_accessed=2 * (4 * tall * width + 2 * width * units + 2 * tall * units),
            transcendentals=0,
        ),
    )(source, *xs, *[g] * parts, w, out_w, *earlier)


def weight_share_body(g_ref, act_ref, out_ref):
    out_ref[...] = tn(g_ref[...], act_ref[...]).astype(BF)


def weight_share(g, act, shares, begin, size):
    rows, width = g.shape
    share = act.shape[1] // shares
    block = math.gcd(768, size)
    per = size // block
    pick = pl.BlockSpec(
        (pl.Element(rows), pl.Element(block)),
        lambda i: (0, pl.multiple_of(i // per * share + begin + i % per * block, 128)),
    )
    return call(
        weight_share_body,
        flops=2 * rows * width * shares * size,
        moved=2 * (rows * width + rows * shares * size + width * shares * size),
        grid=(shares * per,),
        in_specs=[whole(g.shape), pick],
        out_specs=pl.BlockSpec((width, block), lambda i: (0, i)),
        out_shape=jax.ShapeDtypeStruct((width, shares * size), BF),
    )(g, act)


def result_body(chip_ref, act_ref, w_ref, out_ref):
    size = out_ref.shape[1]
    out = nt(act_ref[...], w_ref[...]).astype(BF)
    same = lax.axis_index("core") == 0

    @pl.when(same)
    def _():
        out_ref[0] = out[:size]
        out_ref[1] = out[size:]

    @pl.when(jnp.logical_not(same))
    def _():
        out_ref[0] = out[size:]
        out_ref[1] = out[:size]


def make_result(chips, active, w, experts):
    rows, units = active.shape
    width = w.shape[0]
    size = rows // experts
    return pl.pallas_call(
        result_body,
        grid_spec=pltpu.PrefetchScalarGridSpec(
            num_scalar_prefetch=1,
            grid=(experts // 2,),
            in_specs=[
                pl.BlockSpec((2 * size, units), lambda i, s: (i, 0)),
                pl.BlockSpec(w.shape, lambda i, s: (0, 0)),
            ],
            out_specs=pl.BlockSpec((2, size, width), lambda i, s: (s[i], 0, 0)),
        ),
        out_shape=jax.ShapeDtypeStruct((experts, size, width), BF),
        compiler_params=pltpu.CompilerParams(vmem_limit_bytes=60 << 20),
        cost_estimate=pl.CostEstimate(
            flops=2 * rows * units * width,
            bytes_accessed=2 * (rows * units + units * width + rows * width),
            transcendentals=0,
        ),
    )(chips, active, w)


def collect_back_body(
    col_ref, res_ref, cot_ref, gain_ref, w_ref, back_ref, gres_ref, gattn_ref, gatt_ref, ggain_ref
):
    step = pl.program_id(0)
    placer = (iota((col_ref.shape[0], back_ref.shape[0]), 1) == col_ref[...]).astype(BF)
    grad = nn(placer, back_ref[...])
    x_hat, rate = norm_parts(res_ref[...])
    gres = cot_ref[...].astype(F32) + norm_grad(x_hat, rate, grad * gain_ref[...])
    gres_ref[...] = gres
    gain_part = jnp.sum(grad * x_hat, axis=0, keepdims=True)
    gattn = gres.astype(BF)
    gattn_ref[...] = gattn
    gatt_ref[...] = nt(gattn, w_ref[...]).astype(BF)

    @pl.when(step == 0)
    def _():
        ggain_ref[...] = gain_part

    @pl.when(step > 0)
    def _():
        ggain_ref[...] += gain_part


def collect_back(back, col, residual, cot, gain, w):
    count, width = cot.shape
    block = 256
    row = pl.BlockSpec((block, width), lambda i: (i, 0))
    return call(
        collect_back_body,
        flops=2 * count * width * (back.shape[0] + 2 * width),
        moved=2 * width * (back.shape[0] + 8 * count),
        grid=(count // block,),
        in_specs=[
            pl.BlockSpec((block, 1), lambda i: (i, 0)), row, row,
            whole(gain.shape), whole(w.shape), whole(back.shape),
        ],
        out_specs=[row, row, row, whole((1, width))],
        out_shape=[
            jax.ShapeDtypeStruct((count, width), F32),
            jax.ShapeDtypeStruct((count, width), BF),
            jax.ShapeDtypeStruct((count, width), BF),
            jax.ShapeDtypeStruct((1, width), F32),
        ],
    )(col, residual, cot, gain, w, back)


def collect_body(col_ref, res_ref, back_ref, out_ref):
    placer = (iota((col_ref.shape[0], back_ref.shape[0]), 1) == col_ref[...]).astype(BF)
    out_ref[...] = (res_ref[...] + nn(placer, back_ref[...])).astype(BF)


def collect(back, col, residual):
    count, width = residual.shape
    block = 256
    row = pl.BlockSpec((block, width), lambda i: (i, 0))
    return call(
        collect_body,
        flops=2 * count * width * back.shape[0],
        moved=2 * width * (back.shape[0] + 3 * count),
        grid=(count // block,),
        in_specs=[pl.BlockSpec((block, 1), lambda i: (i, 0)), row, whole(back.shape)],
        out_specs=row,
        out_shape=jax.ShapeDtypeStruct((count, width), BF),
    )(col, residual, back)


def weight_grad_body(normed_ref, g_ref, att_ref, gattn_ref, keep_ref, send_ref):
    step = pl.program_id(0)
    width = g_ref.shape[2]
    last = step == pl.num_programs(0) - 1
    rows = jnp.where(last, gattn_ref[...], g_ref[0])
    left = jnp.where(last, att_ref[...], normed_ref[...])
    out = tn(left, rows).astype(BF)
    mine = step // 2 == lax.axis_index("core")
    for half in range(2):
        columns = slice(half * width, (half + 1) * width)

        @pl.when((step % 2 == half) & mine)
        def _():
            keep_ref[:, columns] = out

        @pl.when((step % 2 == half) & jnp.logical_not(mine))
        def _():
            send_ref[:, columns] = out


def weight_grads(normed, g, attended, gattn):
    count, width = normed.shape
    out = jax.ShapeDtypeStruct((width, 2 * width), BF)
    return call(
        weight_grad_body,
        flops=8 * width * count * width,
        moved=2 * (6 * width * count + 4 * width * width),
        grid=(4,),
        in_specs=[
            whole(normed.shape),
            pl.BlockSpec((1, count, width), lambda i: (jnp.minimum(i, 2), 0, 0)),
            whole(attended.shape),
            whole(gattn.shape),
        ],
        out_specs=[whole(out.shape)] * 2,
        out_shape=[out] * 2,
    )(normed, g, attended, gattn)


def grad_in_body(x_ref, gain_ref, w_ref, g_ref, gres_ref, out_ref, ggain_ref):
    step = pl.program_id(0)
    width = x_ref.shape[1]
    x_hat, rate = norm_parts(x_ref[...].astype(F32))
    grad = nt(g_ref[0], w_ref[:, :width])
    grad += nt(g_ref[1], w_ref[:, width : 2 * width])
    grad += nt(g_ref[2], w_ref[:, 2 * width :])
    out_ref[...] = gres_ref[...] + norm_grad(x_hat, rate, grad * gain_ref[...])
    part = jnp.sum(grad * x_hat, axis=0, keepdims=True)

    @pl.when(step == 0)
    def _():
        ggain_ref[...] = part

    @pl.when(step > 0)
    def _():
        ggain_ref[...] += part


def grad_in(x, gain, w, g, gres):
    count, width = x.shape
    block = 256
    row = pl.BlockSpec((block, width), lambda i: (i, 0))
    return call(
        grad_in_body,
        flops=6 * count * width * width,
        moved=2 * width * 9 * count,
        grid=(count // block,),
        in_specs=[
            row, whole(gain.shape), whole(w.shape),
            pl.BlockSpec((3, block, width), lambda i: (0, i, 0)), row,
        ],
        out_specs=[row, whole((1, width))],
        out_shape=[
            jax.ShapeDtypeStruct((count, width), F32),
            jax.ShapeDtypeStruct((1, width), F32),
        ],
    )(x, gain, w, g, gres)


def shift(a, axis, k):
    n = lax.axis_size(axis)
    return lax.ppermute(a, axis, [(i, (i + k) % n) for i in range(n)])


def groups(chips):
    sizes = [1]
    while sum(sizes) < chips:
        sizes.append((chips - sum(sizes) + 1) // 2)
    out, begin, at = [], 0, chips
    tall = sorted(sizes, reverse=True)
    for i, size in enumerate(sizes):
        rank = tall.index(size) + sizes[:i].count(size)
        out.append((tuple(range(begin, begin + size)), sum(tall[:rank]) // size))
        begin += size
    return out


def source_parts(sides):
    high, low = sides
    y, x, core = (lax.axis_index(axis) for axis in PLANE)
    out = []
    for dy in range(high):
        for dx in range(low):
            for dc in range(2):
                chip = lax.rem(y + high - dy, high) * low + lax.rem(x + low - dx, low)
                out.append(chip * 2 + lax.rem(core + dc, 2))
    return jnp.stack(out).astype(jnp.int32)


def plane_shift(a, part, sides):
    if part == 0:
        return a
    high, low = sides
    dy, dx, dc = part // (2 * low), part // 2 % low, part % 2
    pairs = []
    for y in range(high):
        for x in range(low):
            for core in range(2):
                to = ((y + dy) % high * low + (x + dx) % low) * 2 + (core + dc) % 2
                pairs.append(((y * low + x) * 2 + core, to))
    return lax.ppermute(a, PLANE, pairs)


def cut(a, index, pieces, dim):
    size = a.shape[dim] // pieces
    return lax.dynamic_slice_in_dim(a, index * size, size, dim)


def gather_all(a, axis, dim):
    n = lax.axis_size(axis)
    me = lax.axis_index(axis)
    size = a.shape[dim]
    shape = a.shape[:dim] + (n * size,) + a.shape[dim + 1 :]
    out = lax.dynamic_update_slice_in_dim(jnp.zeros(shape, a.dtype), a, me * size, dim)
    for k in range(1, n):
        got = shift(a, axis, k)
        out = lax.dynamic_update_slice_in_dim(out, got, lax.rem(me - k + n, n) * size, dim)
    return out


def after(value, *first):
    return lax.optimization_barrier((value, first))[0]


def split_body(keep_ref, got_ref, one_ref, two_ref, *out_refs, ways):
    wide = keep_ref.shape[1]
    half = keep_ref.shape[0] // 2
    turned = jnp.transpose(
        jnp.concatenate([one_ref[...], two_ref[...]] + [jnp.zeros_like(one_ref[...])] * 6, 0)
    )
    turned = jnp.concatenate([turned, jnp.zeros((turned.shape[0], 120), F32)], 1)
    at = 0
    for begin, axis, count in ((0, "x", ways[1]), (half, "y", ways[0])):
        size = half // count
        me = lax.axis_index(axis)
        for k in range(count):
            piece = lax.rem(me + k, count)
            rows = pl.ds(pl.multiple_of(begin + piece * size, 8), size)
            out = out_refs[at]
            out[:, :wide] = (keep_ref[rows, :].astype(F32) + got_ref[rows, :].astype(F32)).astype(BF)
            for other in range(count):

                @pl.when(piece == other)
                def _():
                    begin_here = begin + other * size
                    out[:, wide:] = turned[begin_here : begin_here + size].astype(BF)

            at += 1


def split(keep, got, one, two, ways):
    rows, wide = keep.shape
    sizes = [rows // 2 // ways[1]] * ways[1] + [rows // 2 // ways[0]] * ways[0]
    outs = call(
        functools.partial(split_body, ways=ways),
        moved=6 * rows * wide,
        out_shape=[jax.ShapeDtypeStruct((size, wide + 128), BF) for size in sizes],
    )(keep, got, one, two)
    return outs[: ways[1]], outs[ways[1] :]


def add_up(parts, axis):
    return [parts[0]] + [shift(a, axis, k) for k, a in enumerate(parts) if k]


def total(parts):
    out = parts[0].astype(F32)
    for a in parts[1:]:
        out += a.astype(F32)
    return out.astype(parts[0].dtype)


def pieces_of(a, axis, dim):
    n = lax.axis_size(axis)
    me = lax.axis_index(axis)
    return [cut(a, lax.rem(me + k, n), n, dim) for k in range(n)]


def gather_planes(parts):
    return gather_all(total(parts), "dp", 1)


def gather_plane(both, during):
    top = gather_all(both[0], "y", 0)
    low = gather_all(both[1], "x", 0)
    top, low = after((top, low), *during)
    top = gather_all(top, "x", 0)
    low = gather_all(low, "y", 0)
    mine = jnp.concatenate([top, low], 0)
    return mine, shift(mine, "core", 1)


def unpack_body(mine_ref, other_ref, qkv_ref, proj_ref, one_ref, two_ref):
    width = proj_ref.shape[1]
    first = lax.axis_index("core") == 0
    gains = mine_ref[:, 2 * width :].astype(F32) + other_ref[:, 2 * width :].astype(F32)
    gains = jnp.transpose(gains)
    lines = gains.shape[1] // 128
    for part in range(lines):
        line = pl.ds(pl.program_id(0) * lines + part, 1)
        columns = slice(part * 128, (part + 1) * 128)
        one_ref[line, :] = gains[:1, columns]
        two_ref[line, :] = gains[1:2, columns]

    @pl.when(first)
    def _():
        qkv_ref[:, : 2 * width] = mine_ref[:, : 2 * width].astype(F32)
        qkv_ref[:, 2 * width :] = other_ref[:, :width].astype(F32)
        proj_ref[...] = other_ref[:, width : 2 * width].astype(F32)

    @pl.when(jnp.logical_not(first))
    def _():
        qkv_ref[:, : 2 * width] = other_ref[:, : 2 * width].astype(F32)
        qkv_ref[:, 2 * width :] = mine_ref[:, :width].astype(F32)
        proj_ref[...] = mine_ref[:, width : 2 * width].astype(F32)


def unpack(mine, other):
    width = mine.shape[0]
    block = min(256, width)
    row = lambda wide: pl.BlockSpec((block, wide), lambda i: (i, 0))
    return call(
        unpack_body,
        grid=(width // block,),
        in_specs=[row(mine.shape[1])] * 2,
        out_specs=[row(3 * width), row(width)] + [whole((width // 128, 128))] * 2,
        out_shape=[
            jax.ShapeDtypeStruct((width, 3 * width), F32),
            jax.ShapeDtypeStruct((width, width), F32),
            jax.ShapeDtypeStruct((width // 128, 128), F32),
            jax.ShapeDtypeStruct((width // 128, 128), F32),
        ],
    )(mine, other)


def widen_body(*refs):
    at = 0
    for ref in refs[:-1]:
        refs[-1][:, :, at : at + ref.shape[2]] = ref[...].astype(F32)
        at += ref.shape[2]


def widen(*parts):
    rows = parts[0].shape[1]
    wide = sum(a.shape[2] for a in parts)
    block = lambda columns: pl.BlockSpec((1, rows // 2, columns), lambda i: (0, i, 0))
    return call(
        widen_body,
        moved=6 * rows * wide,
        grid=(2,),
        in_specs=[block(a.shape[2]) for a in parts],
        out_specs=block(wide),
        out_shape=jax.ShapeDtypeStruct((1, rows, wide), F32),
    )(*parts)


def local(tokens, token_ids, hash_table, gain_one, w_qkv, w_proj, gain_two, w_in, w_out, cotangent):
    width = tokens.shape[-1]
    x = tokens.reshape(-1, width)
    cot = cotangent.reshape(-1, width)
    count = x.shape[0]
    sides = (lax.axis_size("y"), lax.axis_size("x"))
    experts = lax.axis_size(PLANE)
    capacity = 2 * count // experts
    first_gain = gain_one.reshape(1, width)
    second_gain = gain_two.reshape(1, width)
    inner, outer = w_in[0], w_out[0]

    def exchange_all(a):
        return lax.all_to_all(a, PLANE, split_axis=0, concat_axis=0, tiled=True)

    def exchange(parts):
        return {i: plane_shift(a, i, sides) for i, a in parts.items()}

    row, col, grad_send = route(
        token_ids.reshape(1, count), hash_table.reshape(-1, 128), cot, sides, capacity
    )
    flat_grad = exchange_all(grad_send)
    packed, normed = make_packed(x, first_gain, w_qkv)
    attended, totals = attend(packed)
    residual, *outgoing = dispatch(attended, w_proj, x, second_gain, row, experts, capacity)
    outgoing = dict(enumerate(outgoing))
    far = {i: outgoing.pop(i) for i in range(experts - 2, experts)}
    arrived = exchange(outgoing)
    source = source_parts(sides)
    kept = ()
    plan = groups(experts // 2)
    for chips, place_at in plan:
        parts = [2 * chip + core for chip in chips for core in range(2)]
        kept = expert(
            chips, place_at, experts, source, [arrived[i] for i in parts], flat_grad,
            inner, outer, kept,
        )
        if chips == (0,):
            near = [arrived[i] for i in range(2, experts - 2)]
            arrived.update(exchange(after(far, near, kept[0])))
    active, grad_hidden, rows_in, rows_grad = kept
    tall_first = sorted((chips for chips, _ in plan), key=lambda chips: (-len(chips), chips))
    chips = jnp.stack([source[2 * chip] // 2 for chips in tall_first for chip in chips])
    shares = lax.axis_size("dp")
    share = inner.shape[1] // shares
    def scatter(a):
        return lax.psum_scatter(a[None], "dp", scatter_dimension=2, tiled=True)

    grad_outer = weight_share(rows_grad, active, shares, 0, share)
    grad_w_out = scatter(grad_outer)
    grad_flat = make_result(chips, after(grad_hidden, grad_outer), inner, experts)
    grad_back = exchange_all(grad_flat).reshape(-1, width)
    grad_inner = weight_share(after(rows_in, grad_flat), grad_hidden, shares, 0, share)
    grad_w_in = scatter(grad_inner)
    results = make_result(chips, after(active, grad_inner), outer, experts)
    returned = exchange_all(after(results, grad_back))

    grad_residual, grad_attn, grad_attended, grad_gain_two = collect_back(
        after(grad_back, results), col, residual, cot, second_gain, w_proj
    )
    grad_packed = attend_back(packed, attended, totals, grad_attended)
    keep, send = weight_grads(normed, grad_packed, attended, grad_attn)
    got = shift(send, "core", 1)
    grad_tokens, grad_gain_one = grad_in(
        x, first_gain, w_qkv, after(grad_packed, keep, grad_w_out), grad_residual
    )
    top, low = split(keep, after(got, grad_tokens), grad_gain_one, grad_gain_two, sides)
    grad_w_out = widen(after(grad_w_out, top, low))
    outputs = collect(after(returned.reshape(-1, width), top, low), col, residual)
    top, low = after((add_up(top, "x"), add_up(low, "y")), outputs, grad_w_out)
    top = add_up(pieces_of(total(top), "y", 0), "y")
    low = add_up(pieces_of(total(low), "x", 0), "x")
    both = jnp.stack([total(top), total(low)])
    both = gather_planes(add_up(pieces_of(both, "dp", 1), "dp"))
    grad_w_in = widen(after(grad_w_in, both))
    mine, other = gather_plane(both, (grad_w_in,))
    grad_qkv, grad_proj, one, two = unpack(mine, other)
    return (
        outputs.reshape(tokens.shape),
        grad_tokens.reshape(tokens.shape),
        one.reshape(width),
        grad_qkv,
        grad_proj,
        two.reshape(width),
        grad_w_in,
        grad_w_out,
    )


def solution(mesh):
    dp, experts = mesh.devices.shape
    side = math.isqrt(experts // 2)
    parts = Mesh(mesh.devices.reshape(dp, side, experts // 2 // side, 2), ("dp", "y", "x", "core"))
    rows = ("dp",) + PLANE
    in_specs = (
        P(rows, None, None),
        P(rows, None),
        P(),
        P(),
        P(),
        P(),
        P(),
        P(PLANE, None, None),
        P(PLANE, None, None),
        P(rows, None, None),
    )
    out_specs = (
        P(rows, None, None),
        P(rows, None, None),
        P(),
        P(),
        P(),
        P(),
        P(PLANE, None, "dp"),
        P(PLANE, None, "dp"),
    )
    return jax.shard_map(local, mesh=parts, in_specs=in_specs, out_specs=out_specs, check_vma=False)
```

```python
import functools
import math

import jax
import jax.numpy as jnp
from jax import lax
from jax.experimental import pallas as pl
from jax.experimental.pallas import tpu as pltpu
from jax.sharding import Mesh, PartitionSpec as P

HEADS = 12
HEAD_DIM = 64
EPSILON = 1e-05
NEGATIVE = -1e30
SCALE = HEAD_DIM ** (-0.5)
BF = jnp.bfloat16
F32 = jnp.float32
PLANE = ("y", "x", "core")


def nn(a, b):
    return lax.dot_general(a, b, (((1,), (0,)), ((), ())), preferred_element_type=F32)


def nt(a, b):
    return lax.dot_general(a, b, (((1,), (1,)), ((), ())), preferred_element_type=F32)


def tn(a, b):
    return lax.dot_general(a, b, (((0,), (0,)), ((), ())), preferred_element_type=F32)


def iota(shape, dim):
    return lax.broadcasted_iota(jnp.int32, shape, dim)


def call(body, flops=0, moved=0, limit=62, **kw):
    return pl.pallas_call(
        body,
        compiler_params=pltpu.CompilerParams(vmem_limit_bytes=limit << 20),
        cost_estimate=pl.CostEstimate(
            flops=int(flops), bytes_accessed=int(moved), transcendentals=0
        ),
        **kw,
    )


def whole(shape):
    return pl.BlockSpec(shape, lambda *i: (0,) * len(shape))


def norm_parts(v):
    centred = v - jnp.mean(v, axis=-1, keepdims=True)
    rate = lax.rsqrt(jnp.mean(centred * centred, axis=-1, keepdims=True) + EPSILON)
    return centred * rate, rate


def norm_grad(x_hat, rate, u):
    return rate * (
        u
        - jnp.mean(u, axis=-1, keepdims=True)
        - x_hat * jnp.mean(u * x_hat, axis=-1, keepdims=True)
    )


def route_body(
    ids_ref, table_ref, cot_ref, row_ref, col_ref, send_ref, *, sides, capacity
):
    high_side, low_side = sides
    count = ids_ref.shape[1]
    ids = ids_ref[...]
    table = table_ref[...].astype(BF)
    high = (iota((table.shape[0], count), 0) == (ids >> 7)).astype(BF)
    picked = tn(table, high)
    low = iota((128, count), 0) == (ids & 127)
    chosen = jnp.sum(jnp.where(low, picked, 0.0), axis=0, keepdims=True).astype(jnp.int32)
    bits = low_side.bit_length()
    here = [lax.axis_index(axis) for axis in PLANE]
    part_y = ((chosen >> bits) - here[0]) & (high_side - 1)
    part_x = ((chosen >> 1) - here[1]) & (low_side - 1)
    part_core = (chosen - here[2]) & 1
    relative = (part_y * low_side + part_x) * 2 + part_core
    slots = max(16, send_ref.shape[0])
    member = iota((slots, count), 0) == relative
    before = (iota((count, count), 0) < iota((count, count), 1)).astype(BF)
    earlier = nn(member.astype(BF), before)
    rank = jnp.sum(jnp.where(member, earlier, 0.0), axis=0, keepdims=True)
    target = relative.astype(F32) * capacity + rank
    row = target.astype(jnp.int32)
    row_ref[...] = row
    first = chosen.astype(F32) * capacity + rank
    turned = jnp.transpose(jnp.broadcast_to(first, (8, count)))
    col_ref[...] = turned[:, :1].astype(jnp.int32)
    first = first.astype(jnp.int32)
    place([send_ref.at[part] for part in range(send_ref.shape[0])], first, cot_ref, capacity)


def place(send_refs, row, rows_ref, capacity):
    for part, send_ref in enumerate(send_refs):
        placer = (iota((capacity, row.shape[1]), 0) + part * capacity == row).astype(BF)
        send_ref[...] = nn(placer, rows_ref[...]).astype(BF)


def route(ids, table, cot, sides, capacity):
    count, width = cot.shape
    experts = 2 * sides[0] * sides[1]
    slots = experts * capacity
    return call(
        functools.partial(route_body, sides=sides, capacity=capacity),
        flops=2 * slots * count * width,
        moved=2 * (count + slots) * width,
        out_shape=[
            jax.ShapeDtypeStruct((1, count), jnp.int32),
            jax.ShapeDtypeStruct((count, 1), jnp.int32),
            jax.ShapeDtypeStruct((experts, capacity, width), BF),
        ],
    )(ids, table, cot)


def attend_body(
    x_ref, gain_ref, wq_ref, wk_ref, wv_ref, packed_ref, normed_ref, o_ref, total_ref, *, block
):
    length = x_ref.shape[0]

    @pl.when(pl.program_id(0) == 0)
    def _():
        for begin in range(0, length, 256):
            rows = slice(begin, begin + 256)
            x_hat, _ = norm_parts(x_ref[rows, :].astype(F32))
            normed_ref[rows, :] = (x_hat * gain_ref[...]).astype(BF)

    w = jnp.concatenate([wq_ref[...], wk_ref[...], wv_ref[...]], 1)
    packed = nn(normed_ref[...], w).astype(BF)
    for part in range(3):
        packed_ref[part] = packed[:, part * 128 : (part + 1) * 128]
    lane = iota((1, 128), 1)
    v_turned = jnp.transpose(packed_ref[2])
    allowed = iota((block, block), 0) <= iota((block, block), 1)
    for row in range(length // block):
        end = (row + 1) * block
        outs = []
        for head in range(2):
            q = packed_ref[0, row * block : end, :] * BF(SCALE)
            q = jnp.where(lane // 64 == head, q, BF(0))
            s = nt(packed_ref[1, :end, :], q)
            last = jnp.where(allowed, s[end - block :], NEGATIVE)
            s = jnp.concatenate([s[: end - block], last], 0) if row else last
            highest = jnp.max(s, 0, keepdims=True)
            p = jnp.exp(s - highest)
            summed = jnp.sum(p, 0, keepdims=True)
            out = nn(v_turned[head * 64 : (head + 1) * 64, :end], p.astype(BF))
            outs.append(out * (1.0 / summed))
            total_ref[0, head : head + 1, row * block : end] = highest + jnp.log(summed)
        o_ref[row * block : end, :] = jnp.transpose(jnp.concatenate(outs, 0)).astype(BF)


def attend(x, gain, w):
    length, width = x.shape
    pairs = width // 128
    part = lambda o: pl.BlockSpec((width, 128), lambda i: (0, o * pairs + i))
    return call(
        functools.partial(attend_body, block=min(512, length)),
        flops=1.2e10 + 6 * length * width * width,
        moved=2 * (length * width * 6 + 3 * width * width),
        grid=(pairs,),
        in_specs=[whole(x.shape), whole(gain.shape), part(0), part(1), part(2)],
        out_specs=[
            pl.BlockSpec((3, length, 128), lambda i: (0, 0, i)),
            whole(x.shape),
            pl.BlockSpec((length, 128), lambda i: (0, i)),
            pl.BlockSpec((1, 2, length), lambda i: (i, 0, 0)),
        ],
        out_shape=[
            jax.ShapeDtypeStruct((3, length, width), BF),
            jax.ShapeDtypeStruct(x.shape, BF),
            jax.ShapeDtypeStruct(x.shape, BF),
            jax.ShapeDtypeStruct((pairs, 2, length), F32),
        ],
    )(x, gain, w, w, w)


def attend_back_body(
    packed_ref, o_ref, up_ref, total_ref, out_ref, acc_ref, *, block
):
    q_ref, k_ref, v_ref = (packed_ref.at[part] for part in range(3))
    length = q_ref.shape[0]
    count = length // block
    lane = iota((1, 128), 1)
    inner = jnp.transpose(o_ref[...].astype(F32) * up_ref[...].astype(F32))
    inner = [jnp.sum(inner[:64], 0, keepdims=True), jnp.sum(inner[64:], 0, keepdims=True)]
    allowed = iota((block, block), 0) <= iota((block, block), 1)
    k_turned = jnp.transpose(k_ref[...] * BF(SCALE))
    q_turned = jnp.transpose(q_ref[...] * BF(SCALE))
    up_turned = jnp.transpose(up_ref[...])
    for part in range(count):
        begin, end = part * block, (part + 1) * block
        k = k_ref[begin:end, :]
        v = v_ref[begin:end, :]
        dk, dv = [], []
        for head in range(2):
            mine = lane // 64 == head
            q = jnp.where(mine, q_ref[begin:, :] * BF(SCALE), BF(0))
            up = jnp.where(mine, up_ref[begin:, :], BF(0))
            s = nt(k, q) - total_ref[0, head : head + 1, begin:]
            first = jnp.where(allowed, s[:, :block], NEGATIVE)
            s = jnp.concatenate([first, s[:, block:]], 1) if part < count - 1 else first
            p = jnp.exp(s)
            ds = (p * (nt(v, up) - inner[head][:, begin:])).astype(BF)
            dv.append(nt(up_turned[head * 64 : head * 64 + 64, begin:], p.astype(BF)))
            dk.append(nt(q_turned[head * 64 : head * 64 + 64, begin:], ds))
            dq = nn(k_turned[head * 64 : head * 64 + 64, begin:end], ds)
            if part == 0:
                acc_ref[head * 64 : head * 64 + 64, :] = dq
            else:
                acc_ref[head * 64 : head * 64 + 64, begin:] += dq
        out_ref[1, begin:end, :] = jnp.transpose(jnp.concatenate(dk, 0)).astype(BF)
        out_ref[2, begin:end, :] = jnp.transpose(jnp.concatenate(dv, 0)).astype(BF)
    out_ref[0] = jnp.transpose(acc_ref[...]).astype(BF)


def attend_back(packed, attended, totals, upstream):
    _, length, width = packed.shape
    pairs = width // 128
    part = pl.BlockSpec((length, 128), lambda i: (0, i))
    three = pl.BlockSpec((3, length, 128), lambda i: (0, 0, i))
    return call(
        functools.partial(attend_back_body, block=min(256, length)),
        flops=3e10,
        moved=2 * length * pairs * 1024,
        grid=(pairs,),
        in_specs=[
            three, part, part,
            pl.BlockSpec((1, 2, length), lambda i: (i, 0, 0)),
        ],
        out_specs=three,
        out_shape=jax.ShapeDtypeStruct(packed.shape, BF),
        scratch_shapes=[pltpu.VMEM((128, length), F32)],
    )(packed, attended, upstream, totals)


def dispatch_body(att_ref, w_ref, x_ref, gain_ref, row_ref, res_ref, *rest):
    send_refs, normed_ref = rest[:-1], rest[-1]
    for begin in range(0, att_ref.shape[0], 256):
        rows = slice(begin, begin + 256)
        residual = x_ref[rows, :].astype(F32) + nn(att_ref[rows, :], w_ref[...])
        res_ref[rows, :] = residual
        x_hat, _ = norm_parts(residual)
        normed_ref[rows, :] = (x_hat * gain_ref[...]).astype(BF)
    place(send_refs, row_ref[...], normed_ref, send_refs[0].shape[0])


def dispatch(attended, w, x, gain, row, experts, capacity):
    count, width = x.shape
    slots = experts * capacity
    return call(
        dispatch_body,
        flops=2 * count * width * (slots + width),
        moved=2 * width * (5 * count + slots),
        out_shape=[jax.ShapeDtypeStruct((count, width), F32)]
        + [jax.ShapeDtypeStruct((capacity, width), BF)] * experts,
        scratch_shapes=[pltpu.VMEM((count, width), BF)],
    )(attended, w, x, gain, row)


def expert_body(from_ref, *refs, parts, kept):
    x_refs, g_refs = refs[:parts], refs[parts : 2 * parts]
    w_ref, out_w_ref = refs[2 * parts : 2 * parts + 2]
    act_ref, gh_ref, x_ref, g_ref = refs[2 * parts + 2 + kept :]
    step = pl.program_id(0)
    size = x_refs[0].shape[0]
    c1 = 2.0 * math.sqrt(2.0 / math.pi)
    c2 = c1 * 0.044715

    @pl.when(step == 0)
    def _():
        for part in range(parts):
            rows = slice(part * size, (part + 1) * size)
            x_ref[rows, :] = x_refs[part][...]
            g_ref[rows, :] = g_refs[part][0]

    h = nn(x_ref[...], w_ref[...])
    ga = nn(g_ref[...], out_w_ref[...])
    square = h * h
    half = jnp.tanh(h * (0.5 * c1 + (0.5 * c2) * square)) * 0.5 + 0.5
    act = h * half
    slope = half + (act * (1.0 - half)) * (c1 + (3.0 * c2) * square)
    act_ref[...] = act.astype(BF)
    gh_ref[...] = (ga * slope).astype(BF)


def expert(chips, place_at, total, source, xs, g, w, out_w, earlier):
    parts = len(xs)
    size, width = xs[0].shape
    units = w.shape[1]
    block = min(1024, units)
    tall = parts * size
    tile = pl.BlockSpec((tall, block), lambda i, s: (place_at, i))
    rows = pl.BlockSpec((tall, width), lambda i, s: (place_at, 0))
    weight = pl.BlockSpec((width, block), lambda i, s: (0, i))
    pick = lambda k: pl.BlockSpec((1, size, width), lambda i, s: (s[k], 0, 0))
    every = total * size
    return pl.pallas_call(
        functools.partial(expert_body, parts=parts, kept=len(earlier)),
        grid_spec=pltpu.PrefetchScalarGridSpec(
            num_scalar_prefetch=1,
            grid=(units // block,),
            in_specs=[whole((size, width))] * parts
            + [pick(2 * chip + core) for chip in chips for core in range(2)]
            + [weight, weight]
            + [pl.BlockSpec(memory_space=pl.ANY)] * len(earlier),
            out_specs=[tile, tile, rows, rows],
        ),
        out_shape=[jax.ShapeDtypeStruct((every, units), BF)] * 2
        + [jax.ShapeDtypeStruct((every, width), BF)] * 2,
        input_output_aliases={1 + 2 * parts + 2 + i: i for i in range(len(earlier))},
        compiler_params=pltpu.CompilerParams(vmem_limit_bytes=62 << 20),
        cost_estimate=pl.CostEstimate(
            flops=4 * tall * width * units,
            bytes_accessed=2 * (4 * tall * width + 2 * width * units + 2 * tall * units),
            transcendentals=0,
        ),
    )(source, *xs, *[g] * parts, w, out_w, *earlier)


def weight_share_body(g_ref, act_ref, out_ref):
    out_ref[...] = tn(g_ref[...], act_ref[...]).astype(BF)


def weight_share(g, act, shares, begin, size):
    rows, width = g.shape
    share = act.shape[1] // shares
    block = math.gcd(768, size)
    per = size // block
    pick = pl.BlockSpec(
        (pl.Element(rows), pl.Element(block)),
        lambda i: (0, pl.multiple_of(i // per * share + begin + i % per * block, 128)),
    )
    return call(
        weight_share_body,
        flops=2 * rows * width * shares * size,
        moved=2 * (rows * width + rows * shares * size + width * shares * size),
        grid=(shares * per,),
        in_specs=[whole(g.shape), pick],
        out_specs=pl.BlockSpec((width, block), lambda i: (0, i)),
        out_shape=jax.ShapeDtypeStruct((width, shares * size), BF),
    )(g, act)


def result_body(chip_ref, act_ref, w_ref, out_ref):
    size = out_ref.shape[1]
    out = nt(act_ref[...], w_ref[...]).astype(BF)
    same = lax.axis_index("core") == 0

    @pl.when(same)
    def _():
        out_ref[0] = out[:size]
        out_ref[1] = out[size:]

    @pl.when(jnp.logical_not(same))
    def _():
        out_ref[0] = out[size:]
        out_ref[1] = out[:size]


def make_result(chips, active, w, experts):
    rows, units = active.shape
    width = w.shape[0]
    size = rows // experts
    return pl.pallas_call(
        result_body,
        grid_spec=pltpu.PrefetchScalarGridSpec(
            num_scalar_prefetch=1,
            grid=(experts // 2,),
            in_specs=[
                pl.BlockSpec((2 * size, units), lambda i, s: (i, 0)),
                pl.BlockSpec(w.shape, lambda i, s: (0, 0)),
            ],
            out_specs=pl.BlockSpec((2, size, width), lambda i, s: (s[i], 0, 0)),
        ),
        out_shape=jax.ShapeDtypeStruct((experts, size, width), BF),
        compiler_params=pltpu.CompilerParams(vmem_limit_bytes=62 << 20),
        cost_estimate=pl.CostEstimate(
            flops=2 * rows * units * width,
            bytes_accessed=2 * (rows * units + units * width + rows * width),
            transcendentals=0,
        ),
    )(chips, active, w)


def collect_back_body(
    col_ref, res_ref, cot_ref, gain_ref, w_ref, back_ref, gres_ref, gattn_ref, gatt_ref, ggain_ref
):
    step = pl.program_id(0)
    placer = (iota((col_ref.shape[0], back_ref.shape[0]), 1) == col_ref[...]).astype(BF)
    grad = nn(placer, back_ref[...])
    x_hat, rate = norm_parts(res_ref[...])
    gres = cot_ref[...].astype(F32) + norm_grad(x_hat, rate, grad * gain_ref[...])
    gres_ref[...] = gres
    gain_part = jnp.sum(grad * x_hat, axis=0, keepdims=True)
    gattn = gres.astype(BF)
    gattn_ref[...] = gattn
    gatt_ref[...] = nt(gattn, w_ref[...]).astype(BF)

    @pl.when(step == 0)
    def _():
        ggain_ref[...] = gain_part

    @pl.when(step > 0)
    def _():
        ggain_ref[...] += gain_part


def collect_back(back, col, residual, cot, gain, w):
    count, width = cot.shape
    block = 256
    row = pl.BlockSpec((block, width), lambda i: (i, 0))
    return call(
        collect_back_body,
        flops=2 * count * width * (back.shape[0] + 2 * width),
        moved=2 * width * (back.shape[0] + 8 * count),
        grid=(count // block,),
        in_specs=[
            pl.BlockSpec((block, 1), lambda i: (i, 0)), row, row,
            whole(gain.shape), whole(w.shape), whole(back.shape),
        ],
        out_specs=[row, row, row, whole((1, width))],
        out_shape=[
            jax.ShapeDtypeStruct((count, width), F32),
            jax.ShapeDtypeStruct((count, width), BF),
            jax.ShapeDtypeStruct((count, width), BF),
            jax.ShapeDtypeStruct((1, width), F32),
        ],
    )(col, residual, cot, gain, w, back)


def collect_body(col_ref, res_ref, back_ref, out_ref):
    placer = (iota((col_ref.shape[0], back_ref.shape[0]), 1) == col_ref[...]).astype(BF)
    out_ref[...] = (res_ref[...] + nn(placer, back_ref[...])).astype(BF)


def collect(back, col, residual):
    count, width = residual.shape
    block = 256
    row = pl.BlockSpec((block, width), lambda i: (i, 0))
    return call(
        collect_body,
        limit=60,
        flops=2 * count * width * back.shape[0],
        moved=2 * width * (back.shape[0] + 3 * count),
        grid=(count // block,),
        in_specs=[pl.BlockSpec((block, 1), lambda i: (i, 0)), row, whole(back.shape)],
        out_specs=row,
        out_shape=jax.ShapeDtypeStruct((count, width), BF),
    )(col, residual, back)


def weight_grad_body(normed_ref, g_ref, att_ref, gattn_ref, keep_ref, send_ref):
    step = pl.program_id(0)
    width = g_ref.shape[2]
    last = step == pl.num_programs(0) - 1
    rows = jnp.where(last, gattn_ref[...], g_ref[0])
    left = jnp.where(last, att_ref[...], normed_ref[...])
    out = tn(left, rows).astype(BF)
    mine = step // 2 == lax.axis_index("core")
    for half in range(2):
        columns = slice(half * width, (half + 1) * width)

        @pl.when((step % 2 == half) & mine)
        def _():
            keep_ref[:, columns] = out

        @pl.when((step % 2 == half) & jnp.logical_not(mine))
        def _():
            send_ref[:, columns] = out


def weight_grads(normed, g, attended, gattn):
    count, width = normed.shape
    out = jax.ShapeDtypeStruct((width, 2 * width), BF)
    return call(
        weight_grad_body,
        limit=60,
        flops=8 * width * count * width,
        moved=2 * (6 * width * count + 4 * width * width),
        grid=(4,),
        in_specs=[
            whole(normed.shape),
            pl.BlockSpec((1, count, width), lambda i: (jnp.minimum(i, 2), 0, 0)),
            whole(attended.shape),
            whole(gattn.shape),
        ],
        out_specs=[whole(out.shape)] * 2,
        out_shape=[out] * 2,
    )(normed, g, attended, gattn)


def grad_in_body(x_ref, gain_ref, w_ref, g_ref, gres_ref, out_ref, ggain_ref):
    step = pl.program_id(0)
    width = x_ref.shape[1]
    x_hat, rate = norm_parts(x_ref[...].astype(F32))
    grad = nt(g_ref[0], w_ref[:, :width])
    grad += nt(g_ref[1], w_ref[:, width : 2 * width])
    grad += nt(g_ref[2], w_ref[:, 2 * width :])
    out_ref[...] = gres_ref[...] + norm_grad(x_hat, rate, grad * gain_ref[...])
    part = jnp.sum(grad * x_hat, axis=0, keepdims=True)

    @pl.when(step == 0)
    def _():
        ggain_ref[...] = part

    @pl.when(step > 0)
    def _():
        ggain_ref[...] += part


def grad_in(x, gain, w, g, gres):
    count, width = x.shape
    block = 256
    row = pl.BlockSpec((block, width), lambda i: (i, 0))
    return call(
        grad_in_body,
        limit=60,
        flops=6 * count * width * width,
        moved=2 * width * 9 * count,
        grid=(count // block,),
        in_specs=[
            row, whole(gain.shape), whole(w.shape),
            pl.BlockSpec((3, block, width), lambda i: (0, i, 0)), row,
        ],
        out_specs=[row, whole((1, width))],
        out_shape=[
            jax.ShapeDtypeStruct((count, width), F32),
            jax.ShapeDtypeStruct((1, width), F32),
        ],
    )(x, gain, w, g, gres)


def shift(a, axis, k):
    n = lax.axis_size(axis)
    return lax.ppermute(a, axis, [(i, (i + k) % n) for i in range(n)])


def groups(chips):
    sizes = [1]
    while sum(sizes) < chips:
        sizes.append((chips - sum(sizes) + 1) // 2)
    out, begin, at = [], 0, chips
    tall = sorted(sizes, reverse=True)
    for i, size in enumerate(sizes):
        rank = tall.index(size) + sizes[:i].count(size)
        out.append((tuple(range(begin, begin + size)), sum(tall[:rank]) // size))
        begin += size
    return out


def source_parts(sides):
    high, low = sides
    y, x, core = (lax.axis_index(axis) for axis in PLANE)
    out = []
    for dy in range(high):
        for dx in range(low):
            for dc in range(2):
                chip = lax.rem(y + high - dy, high) * low + lax.rem(x + low - dx, low)
                out.append(chip * 2 + lax.rem(core + dc, 2))
    return jnp.stack(out).astype(jnp.int32)


def plane_shift(a, part, sides):
    if part == 0:
        return a
    high, low = sides
    dy, dx, dc = part // (2 * low), part // 2 % low, part % 2
    pairs = []
    for y in range(high):
        for x in range(low):
            for core in range(2):
                to = ((y + dy) % high * low + (x + dx) % low) * 2 + (core + dc) % 2
                pairs.append(((y * low + x) * 2 + core, to))
    return lax.ppermute(a, PLANE, pairs)


def cut(a, index, pieces, dim):
    size = a.shape[dim] // pieces
    return lax.dynamic_slice_in_dim(a, index * size, size, dim)


def gather_all(a, axis, dim):
    n = lax.axis_size(axis)
    me = lax.axis_index(axis)
    size = a.shape[dim]
    shape = a.shape[:dim] + (n * size,) + a.shape[dim + 1 :]
    out = lax.dynamic_update_slice_in_dim(jnp.zeros(shape, a.dtype), a, me * size, dim)
    for k in range(1, n):
        got = shift(a, axis, k)
        out = lax.dynamic_update_slice_in_dim(out, got, lax.rem(me - k + n, n) * size, dim)
    return out


def after(value, *first):
    return lax.optimization_barrier((value, first))[0]


def split_body(keep_ref, got_ref, *out_refs, ways):
    half = keep_ref.shape[0] // 2
    at = 0
    for begin, axis, count in ((0, "x", ways[1]), (half, "y", ways[0])):
        size = half // count
        me = lax.axis_index(axis)
        for k in range(count):
            rows = pl.ds(pl.multiple_of(begin + lax.rem(me + k, count) * size, 8), size)
            out_refs[at][...] = (
                keep_ref[rows, :].astype(F32) + got_ref[rows, :].astype(F32)
            ).astype(BF)
            at += 1


def split(keep, got, ways):
    rows, wide = keep.shape
    sizes = [rows // 2 // ways[1]] * ways[1] + [rows // 2 // ways[0]] * ways[0]
    outs = call(
        functools.partial(split_body, ways=ways),
        limit=20,
        moved=6 * rows * wide,
        out_shape=[jax.ShapeDtypeStruct((size, wide), BF) for size in sizes],
    )(keep, got)
    return outs[: ways[1]], outs[ways[1] :]


def add_up(parts, axis):
    return [parts[0]] + [shift(a, axis, k) for k, a in enumerate(parts) if k]


def sum_over(a, axis):
    out = a
    for k in range(1, lax.axis_size(axis)):
        out = out + shift(a, axis, k)
    return out


def total(parts):
    out = parts[0].astype(F32)
    for a in parts[1:]:
        out += a.astype(F32)
    return out.astype(parts[0].dtype)


def pieces_of(a, axis, dim):
    n = lax.axis_size(axis)
    me = lax.axis_index(axis)
    return [cut(a, lax.rem(me + k, n), n, dim) for k in range(n)]


def gather_planes(parts):
    return gather_all(total(parts), "dp", 1)


def gather_plane(both, during):
    top = gather_all(both[0], "y", 0)
    low = gather_all(both[1], "x", 0)
    top, low = after((top, low), *during)
    top = gather_all(top, "x", 0)
    low = gather_all(low, "y", 0)
    mine = jnp.concatenate([top, low], 0)
    return mine, shift(mine, "core", 1)


def unpack_body(mine_ref, other_ref, qkv_ref, proj_ref):
    width = proj_ref.shape[1]
    first = lax.axis_index("core") == 0

    @pl.when(first)
    def _():
        qkv_ref[:, : 2 * width] = mine_ref[...].astype(F32)
        qkv_ref[:, 2 * width :] = other_ref[:, :width].astype(F32)
        proj_ref[...] = other_ref[:, width:].astype(F32)

    @pl.when(jnp.logical_not(first))
    def _():
        qkv_ref[:, : 2 * width] = other_ref[...].astype(F32)
        qkv_ref[:, 2 * width :] = mine_ref[:, :width].astype(F32)
        proj_ref[...] = mine_ref[:, width:].astype(F32)


def unpack(mine, other):
    width = mine.shape[0]
    block = min(192, width)
    row = lambda wide: pl.BlockSpec((block, wide), lambda i: (i, 0))
    return call(
        unpack_body,
        limit=60,
        grid=(width // block,),
        in_specs=[row(2 * width)] * 2,
        out_specs=[row(3 * width), row(width)],
        out_shape=[
            jax.ShapeDtypeStruct((width, 3 * width), F32),
            jax.ShapeDtypeStruct((width, width), F32),
        ],
    )(mine, other)


def widen_body(*refs):
    at = 0
    for ref in refs[:-1]:
        refs[-1][:, :, at : at + ref.shape[2]] = ref[...].astype(F32)
        at += ref.shape[2]


def widen(*parts):
    rows = parts[0].shape[1]
    wide = sum(a.shape[2] for a in parts)
    block = lambda columns: pl.BlockSpec((1, rows // 2, columns), lambda i: (0, i, 0))
    return call(
        widen_body,
        limit=60,
        moved=6 * rows * wide,
        grid=(2,),
        in_specs=[block(a.shape[2]) for a in parts],
        out_specs=block(wide),
        out_shape=jax.ShapeDtypeStruct((1, rows, wide), F32),
    )(*parts)


def local(tokens, token_ids, hash_table, gain_one, w_qkv, w_proj, gain_two, w_in, w_out, cotangent):
    width = tokens.shape[-1]
    x = tokens.reshape(-1, width)
    cot = cotangent.reshape(-1, width)
    count = x.shape[0]
    sides = (lax.axis_size("y"), lax.axis_size("x"))
    experts = lax.axis_size(PLANE)
    capacity = 2 * count // experts
    first_gain = gain_one.reshape(1, width)
    second_gain = gain_two.reshape(1, width)
    inner, outer = w_in[0], w_out[0]

    def exchange_all(a):
        return lax.all_to_all(a, PLANE, split_axis=0, concat_axis=0, tiled=True)

    def exchange(parts):
        return {i: plane_shift(a, i, sides) for i, a in parts.items()}

    row, col, grad_send = route(
        token_ids.reshape(1, count), hash_table.reshape(-1, 128), cot, sides, capacity
    )
    flat_grad = exchange_all(grad_send)
    packed, normed, attended, totals = attend(x, first_gain, w_qkv)
    residual, *outgoing = dispatch(attended, w_proj, x, second_gain, row, experts, capacity)
    outgoing = dict(enumerate(outgoing))
    far = {i: outgoing.pop(i) for i in range(experts - 2, experts)}
    arrived = exchange(outgoing)
    source = source_parts(sides)
    kept = ()
    plan = groups(experts // 2)
    for chips, place_at in plan:
        parts = [2 * chip + core for chip in chips for core in range(2)]
        kept = expert(
            chips, place_at, experts, source, [arrived[i] for i in parts], flat_grad,
            inner, outer, kept,
        )
        if chips == (0,):
            near = [arrived[i] for i in range(2, experts - 2)]
            arrived.update(exchange(after(far, near, kept[0])))
    active, grad_hidden, rows_in, rows_grad = kept
    tall_first = sorted((chips for chips, _ in plan), key=lambda chips: (-len(chips), chips))
    chips = jnp.stack([source[2 * chip] // 2 for chips in tall_first for chip in chips])
    shares = lax.axis_size("dp")
    share = inner.shape[1] // shares
    def scatter(a):
        return lax.psum_scatter(a[None], "dp", scatter_dimension=2, tiled=True)

    grad_outer = weight_share(rows_grad, active, shares, 0, share)
    grad_w_out = scatter(grad_outer)
    grad_flat = make_result(chips, after(grad_hidden, grad_outer), inner, experts)
    grad_back = exchange_all(grad_flat).reshape(-1, width)
    grad_inner = weight_share(after(rows_in, grad_flat), grad_hidden, shares, 0, share)
    grad_w_in = scatter(grad_inner)
    results = make_result(chips, after(active, grad_inner), outer, experts)
    returned = exchange_all(after(results, grad_back))

    grad_residual, grad_attn, grad_attended, grad_gain_two = collect_back(
        after(grad_back, results), col, residual, cot, second_gain, w_proj
    )
    grad_packed = attend_back(packed, attended, totals, grad_attended)
    keep, send = weight_grads(normed, grad_packed, attended, grad_attn)
    got = shift(send, "core", 1)
    grad_w_out = widen(after(grad_w_out, keep))
    top, low = split(keep, after(got, grad_w_out, returned), sides)
    grad_tokens, grad_gain_one = grad_in(
        x, first_gain, w_qkv, after(grad_packed, top, low), grad_residual
    )
    small = jnp.concatenate([grad_gain_one, grad_gain_two], 0).reshape(-1, 128)
    small = sum_over(small, "core")
    top, low = after((add_up(top, "x"), add_up(low, "y")), grad_tokens)
    top, low = pieces_of(total(top), "y", 0), pieces_of(total(low), "x", 0)
    small = sum_over(sum_over(small, "x"), "y")
    top, low = add_up(top, "y"), add_up(low, "x")
    both = jnp.stack([total(top), total(low)])
    pad = both.shape[0] * both.shape[1] - small.shape[0]
    small = jnp.concatenate([small, jnp.zeros((pad, 128), F32)], 0).astype(BF)
    both = jnp.concatenate([both, small.reshape(both.shape[:2] + (128,))], 2)
    pieces = pieces_of(both, "dp", 1)
    outputs = collect(after(returned.reshape(-1, width), pieces), col, residual)
    both = gather_planes(after(add_up(pieces, "dp"), outputs))
    small = both[:, :, 2 * width :].reshape(-1, 128)[: 2 * width // 128]
    gains = small.astype(F32).reshape(2, width)
    grad_w_in = widen(after(grad_w_in, both))
    mine, other = gather_plane(both[:, :, : 2 * width], (grad_w_in,))
    grad_qkv, grad_proj = unpack(mine, other)
    return (
        outputs.reshape(tokens.shape),
        grad_tokens.reshape(tokens.shape),
        gains[0],
        grad_qkv,
        grad_proj,
        gains[1],
        grad_w_in,
        grad_w_out,
    )


def solution(mesh):
    dp, experts = mesh.devices.shape
    side = math.isqrt(experts // 2)
    parts = Mesh(mesh.devices.reshape(dp, side, experts // 2 // side, 2), ("dp", "y", "x", "core"))
    rows = ("dp",) + PLANE
    in_specs = (
        P(rows, None, None),
        P(rows, None),
        P(),
        P(),
        P(),
        P(),
        P(),
        P(PLANE, None, None),
        P(PLANE, None, None),
        P(rows, None, None),
    )
    out_specs = (
        P(rows, None, None),
        P(rows, None, None),
        P(),
        P(),
        P(),
        P(),
        P(PLANE, None, "dp"),
        P(PLANE, None, "dp"),
    )
    return jax.shard_map(local, mesh=parts, in_specs=in_specs, out_specs=out_specs, check_vma=False)
```

```python
import functools
import math

import jax
import jax.numpy as jnp
from jax import lax
from jax.experimental import pallas as pl
from jax.experimental.pallas import tpu as pltpu
from jax.sharding import Mesh, PartitionSpec as P

HEADS = 12
HEAD_DIM = 64
EPSILON = 1e-05
NEGATIVE = -1e30
SCALE = HEAD_DIM ** (-0.5)
BF = jnp.bfloat16
F32 = jnp.float32
PLANE = ("y", "x", "core")


def nn(a, b):
    return lax.dot_general(a, b, (((1,), (0,)), ((), ())), preferred_element_type=F32)


def nt(a, b):
    return lax.dot_general(a, b, (((1,), (1,)), ((), ())), preferred_element_type=F32)


def tn(a, b):
    return lax.dot_general(a, b, (((0,), (0,)), ((), ())), preferred_element_type=F32)


def iota(shape, dim):
    return lax.broadcasted_iota(jnp.int32, shape, dim)


def call(body, flops=0, moved=0, limit=62, **kw):
    return pl.pallas_call(
        body,
        compiler_params=pltpu.CompilerParams(vmem_limit_bytes=limit << 20),
        cost_estimate=pl.CostEstimate(
            flops=int(flops), bytes_accessed=int(moved), transcendentals=0
        ),
        **kw,
    )


ANY = pl.BlockSpec(memory_space=pl.ANY)


def whole(shape):
    return pl.BlockSpec(shape, lambda *i: (0,) * len(shape))


def norm_parts(v):
    centred = v - jnp.mean(v, axis=-1, keepdims=True)
    rate = lax.rsqrt(jnp.mean(centred * centred, axis=-1, keepdims=True) + EPSILON)
    return centred * rate, rate


def norm_grad(x_hat, rate, u):
    return rate * (
        u
        - jnp.mean(u, axis=-1, keepdims=True)
        - x_hat * jnp.mean(u * x_hat, axis=-1, keepdims=True)
    )


def route_body(
    ids_ref, table_ref, cot_ref, row_ref, col_ref, send_ref, *, sides, capacity
):
    high_side, low_side = sides
    count = ids_ref.shape[1]
    ids = ids_ref[...]
    table = table_ref[...].astype(BF)
    high = (iota((table.shape[0], count), 0) == (ids >> 7)).astype(BF)
    picked = tn(table, high)
    low = iota((128, count), 0) == (ids & 127)
    chosen = jnp.sum(jnp.where(low, picked, 0.0), axis=0, keepdims=True).astype(jnp.int32)
    bits = low_side.bit_length()
    here = [lax.axis_index(axis) for axis in PLANE]
    part_y = ((chosen >> bits) - here[0]) & (high_side - 1)
    part_x = ((chosen >> 1) - here[1]) & (low_side - 1)
    part_core = (chosen - here[2]) & 1
    relative = (part_y * low_side + part_x) * 2 + part_core
    slots = max(16, send_ref.shape[0])
    member = iota((slots, count), 0) == relative
    before = (iota((count, count), 0) < iota((count, count), 1)).astype(BF)
    earlier = nn(member.astype(BF), before)
    rank = jnp.sum(jnp.where(member, earlier, 0.0), axis=0, keepdims=True)
    target = relative.astype(F32) * capacity + rank
    row = target.astype(jnp.int32)
    row_ref[...] = row
    first = chosen.astype(F32) * capacity + rank
    turned = jnp.transpose(jnp.broadcast_to(first, (8, count)))
    col_ref[...] = turned[:, :1].astype(jnp.int32)
    first = first.astype(jnp.int32)
    place([send_ref.at[part] for part in range(send_ref.shape[0])], first, cot_ref, capacity)


def place(send_refs, row, rows_ref, capacity):
    for part, send_ref in enumerate(send_refs):
        placer = (iota((capacity, row.shape[1]), 0) + part * capacity == row).astype(BF)
        send_ref[...] = nn(placer, rows_ref[...]).astype(BF)


def route(ids, table, cot, sides, capacity):
    count, width = cot.shape
    experts = 2 * sides[0] * sides[1]
    slots = experts * capacity
    return call(
        functools.partial(route_body, sides=sides, capacity=capacity),
        flops=2 * slots * count * width,
        moved=2 * (count + slots) * width,
        out_shape=[
            jax.ShapeDtypeStruct((1, count), jnp.int32),
            jax.ShapeDtypeStruct((count, 1), jnp.int32),
            jax.ShapeDtypeStruct((experts, capacity, width), BF),
        ],
    )(ids, table, cot)


def attend_body(
    x_ref, gain_ref, wq_ref, wk_ref, wv_ref, packed_ref, normed_ref, o_ref, total_ref, *, block
):
    length = x_ref.shape[0]

    @pl.when(pl.program_id(0) == 0)
    def _():
        for begin in range(0, length, 256):
            rows = slice(begin, begin + 256)
            x_hat, _ = norm_parts(x_ref[rows, :].astype(F32))
            normed_ref[rows, :] = (x_hat * gain_ref[...]).astype(BF)

    w = jnp.concatenate([wq_ref[...], wk_ref[...], wv_ref[...]], 1)
    packed = nn(normed_ref[...], w).astype(BF)
    for part in range(3):
        packed_ref[part] = packed[:, part * 128 : (part + 1) * 128]
    lane = iota((1, 128), 1)
    v_turned = jnp.transpose(packed_ref[2])
    allowed = iota((block, block), 0) <= iota((block, block), 1)
    for row in range(length // block):
        end = (row + 1) * block
        outs = []
        for head in range(2):
            q = packed_ref[0, row * block : end, :] * BF(SCALE)
            q = jnp.where(lane // 64 == head, q, BF(0))
            s = nt(packed_ref[1, :end, :], q)
            last = jnp.where(allowed, s[end - block :], NEGATIVE)
            s = jnp.concatenate([s[: end - block], last], 0) if row else last
            highest = jnp.max(s, 0, keepdims=True)
            p = jnp.exp(s - highest)
            summed = jnp.sum(p, 0, keepdims=True)
            out = nn(v_turned[head * 64 : (head + 1) * 64, :end], p.astype(BF))
            outs.append(out * (1.0 / summed))
            total_ref[0, head : head + 1, row * block : end] = highest + jnp.log(summed)
        o_ref[row * block : end, :] = jnp.transpose(jnp.concatenate(outs, 0)).astype(BF)


def attend(x, gain, w):
    length, width = x.shape
    pairs = width // 128
    part = lambda o: pl.BlockSpec((width, 128), lambda i: (0, o * pairs + i))
    return call(
        functools.partial(attend_body, block=min(512, length)),
        flops=1.2e10 + 6 * length * width * width,
        moved=2 * (length * width * 6 + 3 * width * width),
        grid=(pairs,),
        in_specs=[whole(x.shape), whole(gain.shape), part(0), part(1), part(2)],
        out_specs=[
            pl.BlockSpec((3, length, 128), lambda i: (0, 0, i)),
            whole(x.shape),
            pl.BlockSpec((length, 128), lambda i: (0, i)),
            pl.BlockSpec((1, 2, length), lambda i: (i, 0, 0)),
        ],
        out_shape=[
            jax.ShapeDtypeStruct((3, length, width), BF),
            jax.ShapeDtypeStruct(x.shape, BF),
            jax.ShapeDtypeStruct(x.shape, BF),
            jax.ShapeDtypeStruct((pairs, 2, length), F32),
        ],
    )(x, gain, w, w, w)


def attend_back_body(
    packed_ref, o_ref, up_ref, total_ref, out_ref, acc_ref, *, block
):
    q_ref, k_ref, v_ref = (packed_ref.at[part] for part in range(3))
    length = q_ref.shape[0]
    count = length // block
    lane = iota((1, 128), 1)
    inner = jnp.transpose(o_ref[...].astype(F32) * up_ref[...].astype(F32))
    inner = [jnp.sum(inner[:64], 0, keepdims=True), jnp.sum(inner[64:], 0, keepdims=True)]
    allowed = iota((block, block), 0) <= iota((block, block), 1)
    k_turned = jnp.transpose(k_ref[...] * BF(SCALE))
    q_turned = jnp.transpose(q_ref[...] * BF(SCALE))
    up_turned = jnp.transpose(up_ref[...])
    for part in range(count):
        begin, end = part * block, (part + 1) * block
        k = k_ref[begin:end, :]
        v = v_ref[begin:end, :]
        dk, dv = [], []
        for head in range(2):
            mine = lane // 64 == head
            q = jnp.where(mine, q_ref[begin:, :] * BF(SCALE), BF(0))
            up = jnp.where(mine, up_ref[begin:, :], BF(0))
            s = nt(k, q) - total_ref[0, head : head + 1, begin:]
            first = jnp.where(allowed, s[:, :block], NEGATIVE)
            s = jnp.concatenate([first, s[:, block:]], 1) if part < count - 1 else first
            p = jnp.exp(s)
            ds = (p * (nt(v, up) - inner[head][:, begin:])).astype(BF)
            dv.append(nt(up_turned[head * 64 : head * 64 + 64, begin:], p.astype(BF)))
            dk.append(nt(q_turned[head * 64 : head * 64 + 64, begin:], ds))
            dq = nn(k_turned[head * 64 : head * 64 + 64, begin:end], ds)
            if part == 0:
                acc_ref[head * 64 : head * 64 + 64, :] = dq
            else:
                acc_ref[head * 64 : head * 64 + 64, begin:] += dq
        out_ref[1, begin:end, :] = jnp.transpose(jnp.concatenate(dk, 0)).astype(BF)
        out_ref[2, begin:end, :] = jnp.transpose(jnp.concatenate(dv, 0)).astype(BF)
    out_ref[0] = jnp.transpose(acc_ref[...]).astype(BF)


def attend_back(packed, attended, totals, upstream):
    _, length, width = packed.shape
    pairs = width // 128
    part = pl.BlockSpec((length, 128), lambda i: (0, i))
    three = pl.BlockSpec((3, length, 128), lambda i: (0, 0, i))
    return call(
        functools.partial(attend_back_body, block=min(256, length)),
        flops=3e10,
        moved=2 * length * pairs * 1024,
        grid=(pairs,),
        in_specs=[
            three, part, part,
            pl.BlockSpec((1, 2, length), lambda i: (i, 0, 0)),
        ],
        out_specs=three,
        out_shape=jax.ShapeDtypeStruct(packed.shape, BF),
        scratch_shapes=[pltpu.VMEM((128, length), F32)],
    )(packed, attended, upstream, totals)


def dispatch_body(att_ref, w_ref, x_ref, gain_ref, row_ref, res_ref, *rest):
    send_refs, normed_ref = rest[:-1], rest[-1]
    for begin in range(0, att_ref.shape[0], 256):
        rows = slice(begin, begin + 256)
        residual = x_ref[rows, :].astype(F32) + nn(att_ref[rows, :], w_ref[...])
        res_ref[rows, :] = residual
        x_hat, _ = norm_parts(residual)
        normed_ref[rows, :] = (x_hat * gain_ref[...]).astype(BF)
    place(send_refs, row_ref[...], normed_ref, send_refs[0].shape[0])


def dispatch(attended, w, x, gain, row, experts, capacity):
    count, width = x.shape
    slots = experts * capacity
    return call(
        dispatch_body,
        flops=2 * count * width * (slots + width),
        moved=2 * width * (5 * count + slots),
        out_shape=[jax.ShapeDtypeStruct((count, width), F32)]
        + [jax.ShapeDtypeStruct((capacity, width), BF)] * experts,
        scratch_shapes=[pltpu.VMEM((count, width), BF)],
    )(attended, w, x, gain, row)


def expert_body(from_ref, *refs, parts, kept):
    x_refs, g_refs = refs[:parts], refs[parts : 2 * parts]
    w_ref, out_w_ref = refs[2 * parts : 2 * parts + 2]
    act_ref, gh_ref, x_ref, g_ref = refs[2 * parts + 2 + kept :]
    step = pl.program_id(0)
    size = x_refs[0].shape[0]
    c1 = 2.0 * math.sqrt(2.0 / math.pi)
    c2 = c1 * 0.044715

    @pl.when(step == 0)
    def _():
        for part in range(parts):
            rows = slice(part * size, (part + 1) * size)
            x_ref[rows, :] = x_refs[part][...]
            g_ref[rows, :] = g_refs[part][0]

    h = nn(x_ref[...], w_ref[...])
    ga = nn(g_ref[...], out_w_ref[...])
    square = h * h
    half = jnp.tanh(h * (0.5 * c1 + (0.5 * c2) * square)) * 0.5 + 0.5
    act = h * half
    slope = half + (act * (1.0 - half)) * (c1 + (3.0 * c2) * square)
    act_ref[...] = act.astype(BF)
    gh_ref[...] = (ga * slope).astype(BF)


def expert(chips, place_at, total, source, xs, g, w, out_w, earlier):
    parts = len(xs)
    size, width = xs[0].shape
    units = w.shape[1]
    block = min(1024, units)
    tall = parts * size
    tile = pl.BlockSpec((tall, block), lambda i, s: (place_at, i))
    rows = pl.BlockSpec((tall, width), lambda i, s: (place_at, 0))
    weight = pl.BlockSpec((width, block), lambda i, s: (0, i))
    pick = lambda k: pl.BlockSpec((1, size, width), lambda i, s: (s[k], 0, 0))
    every = total * size
    return pl.pallas_call(
        functools.partial(expert_body, parts=parts, kept=len(earlier)),
        grid_spec=pltpu.PrefetchScalarGridSpec(
            num_scalar_prefetch=1,
            grid=(units // block,),
            in_specs=[whole((size, width))] * parts
            + [pick(2 * chip + core) for chip in chips for core in range(2)]
            + [weight, weight]
            + [pl.BlockSpec(memory_space=pl.ANY)] * len(earlier),
            out_specs=[tile, tile, rows, rows],
        ),
        out_shape=[jax.ShapeDtypeStruct((every, units), BF)] * 2
        + [jax.ShapeDtypeStruct((every, width), BF)] * 2,
        input_output_aliases={1 + 2 * parts + 2 + i: i for i in range(len(earlier))},
        compiler_params=pltpu.CompilerParams(vmem_limit_bytes=62 << 20),
        cost_estimate=pl.CostEstimate(
            flops=4 * tall * width * units,
            bytes_accessed=2 * (4 * tall * width + 2 * width * units + 2 * tall * units),
            transcendentals=0,
        ),
    )(source, *xs, *[g] * parts, w, out_w, *earlier)


def weight_share_body(g_ref, act_ref, *out_refs):
    out = tn(g_ref[...], act_ref[...]).astype(BF)
    at = 0
    for out_ref in out_refs:
        out_ref[...] = out[at : at + out_ref.shape[0]]
        at += out_ref.shape[0]


def weight_share(g, act, *heights):
    rows, width = g.shape
    units = act.shape[1]
    block = math.gcd(768, units)
    column = lambda height: pl.BlockSpec((height, block), lambda i: (0, i))
    return call(
        weight_share_body,
        flops=2 * rows * width * units,
        moved=2 * (rows * width + rows * units + width * units),
        grid=(units // block,),
        in_specs=[whole(g.shape), column(rows)],
        out_specs=[column(height) for height in heights],
        out_shape=[jax.ShapeDtypeStruct((height, units), BF) for height in heights],
    )(g, act)


def result_body(chip_ref, act_ref, w_ref, out_ref):
    size = out_ref.shape[1]
    out = nt(act_ref[...], w_ref[...]).astype(BF)
    same = lax.axis_index("core") == 0

    @pl.when(same)
    def _():
        out_ref[0] = out[:size]
        out_ref[1] = out[size:]

    @pl.when(jnp.logical_not(same))
    def _():
        out_ref[0] = out[size:]
        out_ref[1] = out[:size]


def make_result(chips, active, w, experts):
    rows, units = active.shape
    width = w.shape[0]
    size = rows // experts
    return pl.pallas_call(
        result_body,
        grid_spec=pltpu.PrefetchScalarGridSpec(
            num_scalar_prefetch=1,
            grid=(experts // 2,),
            in_specs=[
                pl.BlockSpec((2 * size, units), lambda i, s: (i, 0)),
                pl.BlockSpec(w.shape, lambda i, s: (0, 0)),
            ],
            out_specs=pl.BlockSpec((2, size, width), lambda i, s: (s[i], 0, 0)),
        ),
        out_shape=jax.ShapeDtypeStruct((experts, size, width), BF),
        compiler_params=pltpu.CompilerParams(vmem_limit_bytes=62 << 20),
        cost_estimate=pl.CostEstimate(
            flops=2 * rows * units * width,
            bytes_accessed=2 * (rows * units + units * width + rows * width),
            transcendentals=0,
        ),
    )(chips, active, w)


def collect_back_body(
    col_ref, res_ref, cot_ref, gain_ref, w_ref, back_ref, gres_ref, gattn_ref, gatt_ref, ggain_ref
):
    step = pl.program_id(0)
    placer = (iota((col_ref.shape[0], back_ref.shape[0]), 1) == col_ref[...]).astype(BF)
    grad = nn(placer, back_ref[...])
    x_hat, rate = norm_parts(res_ref[...])
    gres = cot_ref[...].astype(F32) + norm_grad(x_hat, rate, grad * gain_ref[...])
    gres_ref[...] = gres
    gain_part = jnp.sum(grad * x_hat, axis=0, keepdims=True)
    gattn = gres.astype(BF)
    gattn_ref[...] = gattn
    gatt_ref[...] = nt(gattn, w_ref[...]).astype(BF)

    @pl.when(step == 0)
    def _():
        ggain_ref[...] = gain_part

    @pl.when(step > 0)
    def _():
        ggain_ref[...] += gain_part


def collect_back(back, col, residual, cot, gain, w):
    count, width = cot.shape
    block = 256
    row = pl.BlockSpec((block, width), lambda i: (i, 0))
    return call(
        collect_back_body,
        flops=2 * count * width * (back.shape[0] + 2 * width),
        moved=2 * width * (back.shape[0] + 8 * count),
        grid=(count // block,),
        in_specs=[
            pl.BlockSpec((block, 1), lambda i: (i, 0)), row, row,
            whole(gain.shape), whole(w.shape), whole(back.shape),
        ],
        out_specs=[row, row, row, whole((1, width))],
        out_shape=[
            jax.ShapeDtypeStruct((count, width), F32),
            jax.ShapeDtypeStruct((count, width), BF),
            jax.ShapeDtypeStruct((count, width), BF),
            jax.ShapeDtypeStruct((1, width), F32),
        ],
    )(col, residual, cot, gain, w, back)


def collect_body(col_ref, res_ref, back_ref, out_ref):
    placer = (iota((col_ref.shape[0], back_ref.shape[0]), 1) == col_ref[...]).astype(BF)
    out_ref[...] = (res_ref[...] + nn(placer, back_ref[...])).astype(BF)


def collect(back, col, residual):
    count, width = residual.shape
    block = 256
    row = pl.BlockSpec((block, width), lambda i: (i, 0))
    return call(
        collect_body,
        limit=60,
        flops=2 * count * width * back.shape[0],
        moved=2 * width * (back.shape[0] + 3 * count),
        grid=(count // block,),
        in_specs=[pl.BlockSpec((block, 1), lambda i: (i, 0)), row, whole(back.shape)],
        out_specs=row,
        out_shape=jax.ShapeDtypeStruct((count, width), BF),
    )(col, residual, back)


def weight_grad_body(normed_ref, g_ref, att_ref, gattn_ref, keep_ref, send_ref):
    step = pl.program_id(0)
    width = g_ref.shape[2]
    half = width // 2
    core = lax.axis_index("core")

    def put(owner, at, value):
        columns = slice(at, at + value.shape[1])

        @pl.when(core == owner)
        def _():
            keep_ref[:, columns] = value

        @pl.when(core != owner)
        def _():
            send_ref[:, columns] = value

    def packed_part():
        return tn(normed_ref[...], g_ref[0]).astype(BF)

    @pl.when(step == 0)
    def _():
        put(0, 0, packed_part())

    @pl.when(step == 1)
    def _():
        out = packed_part()
        put(0, width, out[:, :half])
        put(1, 0, out[:, half:])

    @pl.when(step == 2)
    def _():
        put(1, half, packed_part())

    @pl.when(step == 3)
    def _():
        out = tn(att_ref[...], gattn_ref[...]).astype(BF)
        put(0, width + half, out[:, :half])
        put(1, width + half, out[:, half:])


def weight_grads(normed, g, attended, gattn):
    count, width = normed.shape
    out = jax.ShapeDtypeStruct((width, 2 * width), BF)
    return call(
        weight_grad_body,
        limit=60,
        flops=8 * width * count * width,
        moved=2 * (6 * width * count + 4 * width * width),
        grid=(4,),
        in_specs=[
            whole(normed.shape),
            pl.BlockSpec((1, count, width), lambda i: (jnp.minimum(i, 2), 0, 0)),
            whole(attended.shape),
            whole(gattn.shape),
        ],
        out_specs=[whole(out.shape)] * 2,
        out_shape=[out] * 2,
    )(normed, g, attended, gattn)


def grad_in_body(x_ref, gain_ref, w_ref, g_ref, gres_ref, out_ref, ggain_ref):
    step = pl.program_id(0)
    width = x_ref.shape[1]
    x_hat, rate = norm_parts(x_ref[...].astype(F32))
    grad = nt(g_ref[0], w_ref[:, :width])
    grad += nt(g_ref[1], w_ref[:, width : 2 * width])
    grad += nt(g_ref[2], w_ref[:, 2 * width :])
    out_ref[...] = gres_ref[...] + norm_grad(x_hat, rate, grad * gain_ref[...])
    part = jnp.sum(grad * x_hat, axis=0, keepdims=True)

    @pl.when(step == 0)
    def _():
        ggain_ref[...] = part

    @pl.when(step > 0)
    def _():
        ggain_ref[...] += part


def grad_in(x, gain, w, g, gres):
    count, width = x.shape
    block = 256
    row = pl.BlockSpec((block, width), lambda i: (i, 0))
    return call(
        grad_in_body,
        limit=60,
        flops=6 * count * width * width,
        moved=2 * width * 9 * count,
        grid=(count // block,),
        in_specs=[
            row, whole(gain.shape), whole(w.shape),
            pl.BlockSpec((3, block, width), lambda i: (0, i, 0)), row,
        ],
        out_specs=[row, whole((1, width))],
        out_shape=[
            jax.ShapeDtypeStruct((count, width), F32),
            jax.ShapeDtypeStruct((1, width), F32),
        ],
    )(x, gain, w, g, gres)


def shift(a, axis, k):
    n = lax.axis_size(axis)
    return lax.ppermute(a, axis, [(i, (i + k) % n) for i in range(n)])


def groups(chips):
    sizes = [1]
    while sum(sizes) < chips:
        sizes.append((chips - sum(sizes) + 1) // 2)
    out, begin, at = [], 0, chips
    tall = sorted(sizes, reverse=True)
    for i, size in enumerate(sizes):
        rank = tall.index(size) + sizes[:i].count(size)
        out.append((tuple(range(begin, begin + size)), sum(tall[:rank]) // size))
        begin += size
    return out


def source_parts(sides):
    high, low = sides
    y, x, core = (lax.axis_index(axis) for axis in PLANE)
    out = []
    for dy in range(high):
        for dx in range(low):
            for dc in range(2):
                chip = lax.rem(y + high - dy, high) * low + lax.rem(x + low - dx, low)
                out.append(chip * 2 + lax.rem(core + dc, 2))
    return jnp.stack(out).astype(jnp.int32)


def plane_shift(a, part, sides):
    if part == 0:
        return a
    high, low = sides
    dy, dx, dc = part // (2 * low), part // 2 % low, part % 2
    pairs = []
    for y in range(high):
        for x in range(low):
            for core in range(2):
                to = ((y + dy) % high * low + (x + dx) % low) * 2 + (core + dc) % 2
                pairs.append(((y * low + x) * 2 + core, to))
    return lax.ppermute(a, PLANE, pairs)


def cut(a, index, pieces, dim):
    size = a.shape[dim] // pieces
    return lax.dynamic_slice_in_dim(a, index * size, size, dim)


def gather_all(a, axis, dim):
    n = lax.axis_size(axis)
    me = lax.axis_index(axis)
    size = a.shape[dim]
    shape = a.shape[:dim] + (n * size,) + a.shape[dim + 1 :]
    out = lax.dynamic_update_slice_in_dim(jnp.zeros(shape, a.dtype), a, me * size, dim)
    for k in range(1, n):
        got = shift(a, axis, k)
        out = lax.dynamic_update_slice_in_dim(out, got, lax.rem(me - k + n, n) * size, dim)
    return out


def after(value, *first):
    return lax.optimization_barrier((value, first))[0]


def split_body(keep_ref, got_ref, *out_refs, ways):
    half = keep_ref.shape[0] // 2
    at = 0
    for begin, axis, count in ((0, "x", ways[1]), (half, "y", ways[0])):
        size = half // count
        me = lax.axis_index(axis)
        for k in range(count):
            rows = pl.ds(pl.multiple_of(begin + lax.rem(me + k, count) * size, 8), size)
            out_refs[at][...] = (
                keep_ref[rows, :].astype(F32) + got_ref[rows, :].astype(F32)
            ).astype(BF)
            at += 1


def split(keep, got, ways):
    rows, wide = keep.shape
    sizes = [rows // 2 // ways[1]] * ways[1] + [rows // 2 // ways[0]] * ways[0]
    outs = call(
        functools.partial(split_body, ways=ways),
        limit=20,
        moved=6 * rows * wide,
        out_shape=[jax.ShapeDtypeStruct((size, wide), BF) for size in sizes],
    )(keep, got)
    return outs[: ways[1]], outs[ways[1] :]


def add_up(parts, axis):
    return [parts[0]] + [shift(a, axis, k) for k, a in enumerate(parts) if k]


def sum_over(a, axis):
    out = a
    for k in range(1, lax.axis_size(axis)):
        out = out + shift(a, axis, k)
    return out


def total(parts):
    out = parts[0].astype(F32)
    for a in parts[1:]:
        out += a.astype(F32)
    return out.astype(parts[0].dtype)


def pieces_of(a, axis, dim):
    n = lax.axis_size(axis)
    me = lax.axis_index(axis)
    return [cut(a, lax.rem(me + k, n), n, dim) for k in range(n)]


def gather_planes(parts):
    return gather_all(total(parts), "dp", 1)


def gather_plane(both, during):
    top = gather_all(both[0], "y", 0)
    low = gather_all(both[1], "x", 0)
    top, low = after((top, low), *during)
    top = gather_all(top, "x", 0)
    low = gather_all(low, "y", 0)
    mine = jnp.concatenate([top, low], 0)
    return mine, shift(mine, "core", 1)


def unpack_body(core_ref, in_ref, *refs):
    qkv_ref, proj_ref = refs[-2:]
    wide = qkv_ref.shape[1]
    qkv_ref[...] = in_ref[:, :wide].astype(F32)
    proj_ref[...] = in_ref[:, wide:].astype(F32)


def unpack(core, half, earlier):
    width = half.shape[0]
    block = min(192, width)
    shapes = [(width, 3 * width), (width, width)]
    return pl.pallas_call(
        unpack_body,
        grid_spec=pltpu.PrefetchScalarGridSpec(
            num_scalar_prefetch=1,
            grid=(width // block,),
            in_specs=[pl.BlockSpec((block, 2 * width), lambda i, s: (i, 0))]
            + [pl.BlockSpec(memory_space=pl.ANY)] * len(earlier),
            out_specs=[
                pl.BlockSpec((block, wide // 2), lambda i, s: (i, s[0])) for _, wide in shapes
            ],
        ),
        out_shape=[jax.ShapeDtypeStruct(shape, F32) for shape in shapes],
        input_output_aliases={2 + i: i for i in range(len(earlier))},
        compiler_params=pltpu.CompilerParams(vmem_limit_bytes=60 << 20),
        cost_estimate=pl.CostEstimate(
            flops=0, bytes_accessed=12 * width * width, transcendentals=0
        ),
    )(core, half, *earlier)


def widen_body(in_ref, *refs):
    refs[-1][...] = in_ref[...].astype(F32)


def widen(a, at, rows, *earlier):
    _, height, wide = a.shape
    block = math.gcd(height, 384)
    return call(
        widen_body,
        limit=60,
        moved=6 * height * wide,
        grid=(height // block,),
        in_specs=[pl.BlockSpec((1, block, wide), lambda i: (0, i, 0))] + [ANY] * len(earlier),
        out_specs=pl.BlockSpec((1, block, wide), lambda i: (0, at // block + i, 0)),
        out_shape=jax.ShapeDtypeStruct((1, rows, wide), F32),
        input_output_aliases={1: 0} if earlier else {},
    )(a, *earlier)


def local(tokens, token_ids, hash_table, gain_one, w_qkv, w_proj, gain_two, w_in, w_out, cotangent):
    width = tokens.shape[-1]
    x = tokens.reshape(-1, width)
    cot = cotangent.reshape(-1, width)
    count = x.shape[0]
    sides = (lax.axis_size("y"), lax.axis_size("x"))
    experts = lax.axis_size(PLANE)
    capacity = 2 * count // experts
    first_gain = gain_one.reshape(1, width)
    second_gain = gain_two.reshape(1, width)
    inner, outer = w_in[0], w_out[0]

    def exchange_all(a):
        return lax.all_to_all(a, PLANE, split_axis=0, concat_axis=0, tiled=True)

    def exchange(parts):
        return {i: plane_shift(a, i, sides) for i, a in parts.items()}

    row, col, grad_send = route(
        token_ids.reshape(1, count), hash_table.reshape(-1, 128), cot, sides, capacity
    )
    flat_grad = exchange_all(grad_send)
    packed, normed, attended, totals = attend(x, first_gain, w_qkv)
    residual, *outgoing = dispatch(attended, w_proj, x, second_gain, row, experts, capacity)
    outgoing = dict(enumerate(outgoing))
    far = {i: outgoing.pop(i) for i in range(experts - 2, experts)}
    arrived = exchange(outgoing)
    source = source_parts(sides)
    kept = ()
    plan = groups(experts // 2)
    for chips, place_at in plan:
        parts = [2 * chip + core for chip in chips for core in range(2)]
        kept = expert(
            chips, place_at, experts, source, [arrived[i] for i in parts], flat_grad,
            inner, outer, kept,
        )
        if chips == (0,):
            near = [arrived[i] for i in range(2, experts - 2)]
            arrived.update(exchange(after(far, near, kept[0])))
    active, grad_hidden, rows_in, rows_grad = kept
    tall_first = sorted((chips for chips, _ in plan), key=lambda chips: (-len(chips), chips))
    chips = jnp.stack([source[2 * chip] // 2 for chips in tall_first for chip in chips])
    shares = lax.axis_size("dp")
    share = inner.shape[1] // shares
    def scatter(a):
        return lax.psum_scatter(a[None], "dp", scatter_dimension=2, tiled=True)

    (grad_outer,) = weight_share(rows_grad, active, width)
    grad_w_out = scatter(grad_outer)
    grad_flat = make_result(chips, after(grad_hidden, grad_outer), inner, experts)
    grad_back = exchange_all(grad_flat).reshape(-1, width)
    most = width * 3 // 4
    grad_inner, grad_later = weight_share(
        after(rows_in, grad_flat), grad_hidden, most, width - most
    )
    grad_w_in = scatter(grad_inner)
    results = make_result(chips, after(active, grad_inner), outer, experts)
    returned = exchange_all(after(results, grad_back))

    grad_residual, grad_attn, grad_attended, grad_gain_two = collect_back(
        after(grad_back, results), col, residual, cot, second_gain, w_proj
    )
    grad_packed = attend_back(packed, attended, totals, grad_attended)
    keep, send = weight_grads(normed, grad_packed, attended, grad_attn)
    got = shift(send, "core", 1)
    grad_w_out = widen(after(grad_w_out, keep), 0, width)
    top, low = split(keep, after(got, grad_w_out, returned), sides)
    grad_tokens, grad_gain_one = grad_in(
        x, first_gain, w_qkv, after(grad_packed, top, low), grad_residual
    )
    small = jnp.concatenate([grad_gain_one, grad_gain_two], 0).reshape(-1, 128)
    small = sum_over(small, "core")
    top, low = after((add_up(top, "x"), add_up(low, "y")), grad_tokens)
    top, low = pieces_of(total(top), "y", 0), pieces_of(total(low), "x", 0)
    small = sum_over(sum_over(small, "x"), "y")
    top, low = after((add_up(top, "y"), add_up(low, "x")), grad_w_in)
    both = jnp.stack([total(top), total(low)])
    pad = both.shape[0] * both.shape[1] - small.shape[0]
    small = jnp.concatenate([small, jnp.zeros((pad, 128), F32)], 0).astype(BF)
    both = jnp.concatenate([both, small.reshape(both.shape[:2] + (128,))], 2)
    pieces = pieces_of(both, "dp", 1)
    outputs = collect(after(returned.reshape(-1, width), pieces), col, residual)
    both = gather_planes(after(add_up(pieces, "dp"), outputs))
    small = both[:, :, 2 * width :].reshape(-1, 128)[: 2 * width // 128]
    gains = small.astype(F32).reshape(2, width)
    grad_w_in = widen(after(grad_w_in, both), 0, width)
    later = scatter(after(grad_later, both))
    core = lax.axis_index("core").reshape(1).astype(jnp.int32)

    def spread(both):
        mine, other = gather_plane(both, ())
        grads = unpack(core, mine, ())
        return tuple(unpack(1 - core, other, after(grads, other)))

    def skip(both):
        return tuple(jnp.zeros((width, wide), F32) for wide in (3 * width, width))

    grad_qkv, grad_proj = lax.cond(
        core[0] < 2, spread, skip, after(both[:, :, : 2 * width], grad_w_in)
    )
    grad_w_in = widen(after(later, grad_qkv), most, width, grad_w_in)
    return (
        outputs.reshape(tokens.shape),
        grad_tokens.reshape(tokens.shape),
        gains[0],
        grad_qkv,
        grad_proj,
        gains[1],
        grad_w_in,
        grad_w_out,
    )


def solution(mesh):
    dp, experts = mesh.devices.shape
    side = math.isqrt(experts // 2)
    parts = Mesh(mesh.devices.reshape(dp, side, experts // 2 // side, 2), ("dp", "y", "x", "core"))
    rows = ("dp",) + PLANE
    in_specs = (
        P(rows, None, None),
        P(rows, None),
        P(),
        P(),
        P(),
        P(),
        P(),
        P(PLANE, None, None),
        P(PLANE, None, None),
        P(rows, None, None),
    )
    out_specs = (
        P(rows, None, None),
        P(rows, None, None),
        P(),
        P(),
        P(),
        P(),
        P(PLANE, None, "dp"),
        P(PLANE, None, "dp"),
    )
    return jax.shard_map(local, mesh=parts, in_specs=in_specs, out_specs=out_specs, check_vma=False)
```

```python
import functools
import math

import jax
import jax.numpy as jnp
from jax import lax
from jax.experimental import pallas as pl
from jax.experimental.pallas import tpu as pltpu
from jax.sharding import Mesh, PartitionSpec as P

HEADS = 12
HEAD_DIM = 64
EPSILON = 1e-05
NEGATIVE = -1e30
SCALE = HEAD_DIM ** (-0.5)
BF = jnp.bfloat16
F32 = jnp.float32
PLANE = ("y", "x", "core")


def nn(a, b):
    return lax.dot_general(a, b, (((1,), (0,)), ((), ())), preferred_element_type=F32)


def nt(a, b):
    return lax.dot_general(a, b, (((1,), (1,)), ((), ())), preferred_element_type=F32)


def tn(a, b):
    return lax.dot_general(a, b, (((0,), (0,)), ((), ())), preferred_element_type=F32)


def iota(shape, dim):
    return lax.broadcasted_iota(jnp.int32, shape, dim)


def call(body, flops=0, moved=0, limit=62, **kw):
    return pl.pallas_call(
        body,
        compiler_params=pltpu.CompilerParams(vmem_limit_bytes=limit << 20),
        cost_estimate=pl.CostEstimate(
            flops=int(flops), bytes_accessed=int(moved), transcendentals=0
        ),
        **kw,
    )


ANY = pl.BlockSpec(memory_space=pl.ANY)


def whole(shape):
    return pl.BlockSpec(shape, lambda *i: (0,) * len(shape))


def norm_parts(v):
    centred = v - jnp.mean(v, axis=-1, keepdims=True)
    rate = lax.rsqrt(jnp.mean(centred * centred, axis=-1, keepdims=True) + EPSILON)
    return centred * rate, rate


def norm_grad(x_hat, rate, u):
    return rate * (
        u
        - jnp.mean(u, axis=-1, keepdims=True)
        - x_hat * jnp.mean(u * x_hat, axis=-1, keepdims=True)
    )


def route_body(
    ids_ref, table_ref, cot_ref, row_ref, col_ref, send_ref, *, sides, capacity
):
    high_side, low_side = sides
    count = ids_ref.shape[1]
    ids = ids_ref[...]
    table = table_ref[...].astype(BF)
    high = (iota((table.shape[0], count), 0) == (ids >> 7)).astype(BF)
    picked = tn(table, high)
    low = iota((128, count), 0) == (ids & 127)
    chosen = jnp.sum(jnp.where(low, picked, 0.0), axis=0, keepdims=True).astype(jnp.int32)
    bits = low_side.bit_length()
    here = [lax.axis_index(axis) for axis in PLANE]
    part_y = ((chosen >> bits) - here[0]) & (high_side - 1)
    part_x = ((chosen >> 1) - here[1]) & (low_side - 1)
    part_core = (chosen - here[2]) & 1
    relative = (part_y * low_side + part_x) * 2 + part_core
    slots = max(16, send_ref.shape[0])
    member = iota((slots, count), 0) == relative
    before = (iota((count, count), 0) < iota((count, count), 1)).astype(BF)
    earlier = nn(member.astype(BF), before)
    rank = jnp.sum(jnp.where(member, earlier, 0.0), axis=0, keepdims=True)
    target = relative.astype(F32) * capacity + rank
    row = target.astype(jnp.int32)
    row_ref[...] = row
    first = chosen.astype(F32) * capacity + rank
    turned = jnp.transpose(jnp.broadcast_to(first, (8, count)))
    col_ref[...] = turned[:, :1].astype(jnp.int32)
    first = first.astype(jnp.int32)
    place([send_ref.at[part] for part in range(send_ref.shape[0])], first, cot_ref, capacity)


def place(send_refs, row, rows_ref, capacity):
    for part, send_ref in enumerate(send_refs):
        placer = (iota((capacity, row.shape[1]), 0) + part * capacity == row).astype(BF)
        send_ref[...] = nn(placer, rows_ref[...]).astype(BF)


def route(ids, table, cot, sides, capacity):
    count, width = cot.shape
    experts = 2 * sides[0] * sides[1]
    slots = experts * capacity
    return call(
        functools.partial(route_body, sides=sides, capacity=capacity),
        flops=2 * slots * count * width,
        moved=2 * (count + slots) * width,
        out_shape=[
            jax.ShapeDtypeStruct((1, count), jnp.int32),
            jax.ShapeDtypeStruct((count, 1), jnp.int32),
            jax.ShapeDtypeStruct((experts, capacity, width), BF),
        ],
    )(ids, table, cot)


def attend_body(
    x_ref, gain_ref, wq_ref, wk_ref, wv_ref, packed_ref, normed_ref, o_ref, total_ref, *, block
):
    length = x_ref.shape[0]

    @pl.when(pl.program_id(0) == 0)
    def _():
        for begin in range(0, length, 256):
            rows = slice(begin, begin + 256)
            x_hat, _ = norm_parts(x_ref[rows, :].astype(F32))
            normed_ref[rows, :] = (x_hat * gain_ref[...]).astype(BF)

    w = jnp.concatenate([wq_ref[...], wk_ref[...], wv_ref[...]], 1)
    packed = nn(normed_ref[...], w).astype(BF)
    for part in range(3):
        packed_ref[part] = packed[:, part * 128 : (part + 1) * 128]
    lane = iota((1, 128), 1)
    v_turned = jnp.transpose(packed_ref[2])
    allowed = iota((block, block), 0) <= iota((block, block), 1)
    for row in range(length // block):
        end = (row + 1) * block
        outs = []
        for head in range(2):
            q = packed_ref[0, row * block : end, :] * BF(SCALE)
            q = jnp.where(lane // 64 == head, q, BF(0))
            s = nt(packed_ref[1, :end, :], q)
            last = jnp.where(allowed, s[end - block :], NEGATIVE)
            s = jnp.concatenate([s[: end - block], last], 0) if row else last
            highest = jnp.max(s, 0, keepdims=True)
            p = jnp.exp(s - highest)
            summed = jnp.sum(p, 0, keepdims=True)
            out = nn(v_turned[head * 64 : (head + 1) * 64, :end], p.astype(BF))
            outs.append(out * (1.0 / summed))
            total_ref[0, head : head + 1, row * block : end] = highest + jnp.log(summed)
        o_ref[row * block : end, :] = jnp.transpose(jnp.concatenate(outs, 0)).astype(BF)


def attend(x, gain, w):
    length, width = x.shape
    pairs = width // 128
    part = lambda o: pl.BlockSpec((width, 128), lambda i: (0, o * pairs + i))
    return call(
        functools.partial(attend_body, block=min(512, length)),
        flops=1.2e10 + 6 * length * width * width,
        moved=2 * (length * width * 6 + 3 * width * width),
        grid=(pairs,),
        in_specs=[whole(x.shape), whole(gain.shape), part(0), part(1), part(2)],
        out_specs=[
            pl.BlockSpec((3, length, 128), lambda i: (0, 0, i)),
            whole(x.shape),
            pl.BlockSpec((length, 128), lambda i: (0, i)),
            pl.BlockSpec((1, 2, length), lambda i: (i, 0, 0)),
        ],
        out_shape=[
            jax.ShapeDtypeStruct((3, length, width), BF),
            jax.ShapeDtypeStruct(x.shape, BF),
            jax.ShapeDtypeStruct(x.shape, BF),
            jax.ShapeDtypeStruct((pairs, 2, length), F32),
        ],
    )(x, gain, w, w, w)


def attend_back_body(
    packed_ref, o_ref, up_ref, total_ref, out_ref, acc_ref, *, block
):
    q_ref, k_ref, v_ref = (packed_ref.at[part] for part in range(3))
    length = q_ref.shape[0]
    count = length // block
    lane = iota((1, 128), 1)
    inner = jnp.transpose(o_ref[...].astype(F32) * up_ref[...].astype(F32))
    inner = [jnp.sum(inner[:64], 0, keepdims=True), jnp.sum(inner[64:], 0, keepdims=True)]
    allowed = iota((block, block), 0) <= iota((block, block), 1)
    k_turned = jnp.transpose(k_ref[...] * BF(SCALE))
    q_turned = jnp.transpose(q_ref[...] * BF(SCALE))
    up_turned = jnp.transpose(up_ref[...])
    for part in range(count):
        begin, end = part * block, (part + 1) * block
        k = k_ref[begin:end, :]
        v = v_ref[begin:end, :]
        dk, dv = [], []
        for head in range(2):
            mine = lane // 64 == head
            q = jnp.where(mine, q_ref[begin:, :] * BF(SCALE), BF(0))
            up = jnp.where(mine, up_ref[begin:, :], BF(0))
            s = nt(k, q) - total_ref[0, head : head + 1, begin:]
            first = jnp.where(allowed, s[:, :block], NEGATIVE)
            s = jnp.concatenate([first, s[:, block:]], 1) if part < count - 1 else first
            p = jnp.exp(s)
            ds = (p * (nt(v, up) - inner[head][:, begin:])).astype(BF)
            dv.append(nt(up_turned[head * 64 : head * 64 + 64, begin:], p.astype(BF)))
            dk.append(nt(q_turned[head * 64 : head * 64 + 64, begin:], ds))
            dq = nn(k_turned[head * 64 : head * 64 + 64, begin:end], ds)
            if part == 0:
                acc_ref[head * 64 : head * 64 + 64, :] = dq
            else:
                acc_ref[head * 64 : head * 64 + 64, begin:] += dq
        out_ref[1, begin:end, :] = jnp.transpose(jnp.concatenate(dk, 0)).astype(BF)
        out_ref[2, begin:end, :] = jnp.transpose(jnp.concatenate(dv, 0)).astype(BF)
    out_ref[0] = jnp.transpose(acc_ref[...]).astype(BF)


def attend_back(packed, attended, totals, upstream):
    _, length, width = packed.shape
    pairs = width // 128
    part = pl.BlockSpec((length, 128), lambda i: (0, i))
    three = pl.BlockSpec((3, length, 128), lambda i: (0, 0, i))
    return call(
        functools.partial(attend_back_body, block=min(256, length)),
        flops=3e10,
        moved=2 * length * pairs * 1024,
        grid=(pairs,),
        in_specs=[
            three, part, part,
            pl.BlockSpec((1, 2, length), lambda i: (i, 0, 0)),
        ],
        out_specs=three,
        out_shape=jax.ShapeDtypeStruct(packed.shape, BF),
        scratch_shapes=[pltpu.VMEM((128, length), F32)],
    )(packed, attended, upstream, totals)


def dispatch_body(att_ref, w_ref, x_ref, gain_ref, row_ref, res_ref, *rest):
    send_refs, normed_ref = rest[:-1], rest[-1]
    for begin in range(0, att_ref.shape[0], 256):
        rows = slice(begin, begin + 256)
        residual = x_ref[rows, :].astype(F32) + nn(att_ref[rows, :], w_ref[...])
        res_ref[rows, :] = residual
        x_hat, _ = norm_parts(residual)
        normed_ref[rows, :] = (x_hat * gain_ref[...]).astype(BF)
    place(send_refs, row_ref[...], normed_ref, send_refs[0].shape[0])


def dispatch(attended, w, x, gain, row, experts, capacity):
    count, width = x.shape
    slots = experts * capacity
    return call(
        dispatch_body,
        flops=2 * count * width * (slots + width),
        moved=2 * width * (5 * count + slots),
        out_shape=[jax.ShapeDtypeStruct((count, width), F32)]
        + [jax.ShapeDtypeStruct((capacity, width), BF)] * experts,
        scratch_shapes=[pltpu.VMEM((count, width), BF)],
    )(attended, w, x, gain, row)


def expert_body(from_ref, *refs, parts, kept):
    x_refs, g_refs = refs[:parts], refs[parts : 2 * parts]
    w_ref, out_w_ref = refs[2 * parts : 2 * parts + 2]
    act_ref, gh_ref, x_ref, g_ref = refs[2 * parts + 2 + kept :]
    step = pl.program_id(0)
    size = x_refs[0].shape[0]
    c1 = 2.0 * math.sqrt(2.0 / math.pi)
    c2 = c1 * 0.044715

    @pl.when(step == 0)
    def _():
        for part in range(parts):
            rows = slice(part * size, (part + 1) * size)
            x_ref[rows, :] = x_refs[part][...]
            g_ref[rows, :] = g_refs[part][0]

    h = nn(x_ref[...], w_ref[...])
    ga = nn(g_ref[...], out_w_ref[...])
    square = h * h
    half = jnp.tanh(h * (0.5 * c1 + (0.5 * c2) * square)) * 0.5 + 0.5
    act = h * half
    slope = half + (act * (1.0 - half)) * (c1 + (3.0 * c2) * square)
    act_ref[...] = act.astype(BF)
    gh_ref[...] = (ga * slope).astype(BF)


def expert(chips, place_at, total, source, xs, g, w, out_w, earlier):
    parts = len(xs)
    size, width = xs[0].shape
    units = w.shape[1]
    block = min(1024, units)
    tall = parts * size
    tile = pl.BlockSpec((tall, block), lambda i, s: (place_at, i))
    rows = pl.BlockSpec((tall, width), lambda i, s: (place_at, 0))
    weight = pl.BlockSpec((width, block), lambda i, s: (0, i))
    pick = lambda k: pl.BlockSpec((1, size, width), lambda i, s: (s[k], 0, 0))
    every = total * size
    return pl.pallas_call(
        functools.partial(expert_body, parts=parts, kept=len(earlier)),
        grid_spec=pltpu.PrefetchScalarGridSpec(
            num_scalar_prefetch=1,
            grid=(units // block,),
            in_specs=[whole((size, width))] * parts
            + [pick(2 * chip + core) for chip in chips for core in range(2)]
            + [weight, weight]
            + [pl.BlockSpec(memory_space=pl.ANY)] * len(earlier),
            out_specs=[tile, tile, rows, rows],
        ),
        out_shape=[jax.ShapeDtypeStruct((every, units), BF)] * 2
        + [jax.ShapeDtypeStruct((every, width), BF)] * 2,
        input_output_aliases={1 + 2 * parts + 2 + i: i for i in range(len(earlier))},
        compiler_params=pltpu.CompilerParams(vmem_limit_bytes=62 << 20),
        cost_estimate=pl.CostEstimate(
            flops=4 * tall * width * units,
            bytes_accessed=2 * (4 * tall * width + 2 * width * units + 2 * tall * units),
            transcendentals=0,
        ),
    )(source, *xs, *[g] * parts, w, out_w, *earlier)


def weight_share_body(g_ref, act_ref, *out_refs):
    out = tn(g_ref[...], act_ref[...]).astype(BF)
    at = 0
    for out_ref in out_refs:
        out_ref[...] = out[at : at + out_ref.shape[0]]
        at += out_ref.shape[0]


def weight_share(g, act, *heights):
    rows, width = g.shape
    units = act.shape[1]
    block = math.gcd(768, units)
    column = lambda height: pl.BlockSpec((height, block), lambda i: (0, i))
    return call(
        weight_share_body,
        flops=2 * rows * width * units,
        moved=2 * (rows * width + rows * units + width * units),
        grid=(units // block,),
        in_specs=[whole(g.shape), column(rows)],
        out_specs=[column(height) for height in heights],
        out_shape=[jax.ShapeDtypeStruct((height, units), BF) for height in heights],
    )(g, act)


def result_body(chip_ref, act_ref, w_ref, out_ref):
    size = out_ref.shape[1]
    out = nt(act_ref[...], w_ref[...]).astype(BF)
    same = lax.axis_index("core") == 0

    @pl.when(same)
    def _():
        out_ref[0] = out[:size]
        out_ref[1] = out[size:]

    @pl.when(jnp.logical_not(same))
    def _():
        out_ref[0] = out[size:]
        out_ref[1] = out[:size]


def make_result(chips, active, w, experts):
    rows, units = active.shape
    width = w.shape[0]
    size = rows // experts
    return pl.pallas_call(
        result_body,
        grid_spec=pltpu.PrefetchScalarGridSpec(
            num_scalar_prefetch=1,
            grid=(experts // 2,),
            in_specs=[
                pl.BlockSpec((2 * size, units), lambda i, s: (i, 0)),
                pl.BlockSpec(w.shape, lambda i, s: (0, 0)),
            ],
            out_specs=pl.BlockSpec((2, size, width), lambda i, s: (s[i], 0, 0)),
        ),
        out_shape=jax.ShapeDtypeStruct((experts, size, width), BF),
        compiler_params=pltpu.CompilerParams(vmem_limit_bytes=62 << 20),
        cost_estimate=pl.CostEstimate(
            flops=2 * rows * units * width,
            bytes_accessed=2 * (rows * units + units * width + rows * width),
            transcendentals=0,
        ),
    )(chips, active, w)


def collect_back_body(
    col_ref, res_ref, cot_ref, gain_ref, w_ref, back_ref, gres_ref, gattn_ref, gatt_ref, ggain_ref
):
    step = pl.program_id(0)
    placer = (iota((col_ref.shape[0], back_ref.shape[0]), 1) == col_ref[...]).astype(BF)
    grad = nn(placer, back_ref[...])
    x_hat, rate = norm_parts(res_ref[...])
    gres = cot_ref[...].astype(F32) + norm_grad(x_hat, rate, grad * gain_ref[...])
    gres_ref[...] = gres
    gain_part = jnp.sum(grad * x_hat, axis=0, keepdims=True)
    gattn = gres.astype(BF)
    gattn_ref[...] = gattn
    gatt_ref[...] = nt(gattn, w_ref[...]).astype(BF)

    @pl.when(step == 0)
    def _():
        ggain_ref[...] = gain_part

    @pl.when(step > 0)
    def _():
        ggain_ref[...] += gain_part


def collect_back(back, col, residual, cot, gain, w):
    count, width = cot.shape
    block = 256
    row = pl.BlockSpec((block, width), lambda i: (i, 0))
    return call(
        collect_back_body,
        flops=2 * count * width * (back.shape[0] + 2 * width),
        moved=2 * width * (back.shape[0] + 8 * count),
        grid=(count // block,),
        in_specs=[
            pl.BlockSpec((block, 1), lambda i: (i, 0)), row, row,
            whole(gain.shape), whole(w.shape), whole(back.shape),
        ],
        out_specs=[row, row, row, whole((1, width))],
        out_shape=[
            jax.ShapeDtypeStruct((count, width), F32),
            jax.ShapeDtypeStruct((count, width), BF),
            jax.ShapeDtypeStruct((count, width), BF),
            jax.ShapeDtypeStruct((1, width), F32),
        ],
    )(col, residual, cot, gain, w, back)


def collect_body(col_ref, res_ref, back_ref, out_ref):
    placer = (iota((col_ref.shape[0], back_ref.shape[0]), 1) == col_ref[...]).astype(BF)
    out_ref[...] = (res_ref[...] + nn(placer, back_ref[...])).astype(BF)


def collect(back, col, residual):
    count, width = residual.shape
    block = 256
    row = pl.BlockSpec((block, width), lambda i: (i, 0))
    return call(
        collect_body,
        limit=60,
        flops=2 * count * width * back.shape[0],
        moved=2 * width * (back.shape[0] + 3 * count),
        grid=(count // block,),
        in_specs=[pl.BlockSpec((block, 1), lambda i: (i, 0)), row, whole(back.shape)],
        out_specs=row,
        out_shape=jax.ShapeDtypeStruct((count, width), BF),
    )(col, residual, back)


def weight_grad_body(normed_ref, g_ref, att_ref, gattn_ref, keep_ref, send_ref):
    step = pl.program_id(0)
    width = g_ref.shape[2]
    half = width // 2
    core = lax.axis_index("core")

    def put(owner, at, value):
        columns = slice(at, at + value.shape[1])

        @pl.when(core == owner)
        def _():
            keep_ref[:, columns] = value

        @pl.when(core != owner)
        def _():
            send_ref[:, columns] = value

    def packed_part():
        return tn(normed_ref[...], g_ref[0]).astype(BF)

    @pl.when(step == 0)
    def _():
        put(0, 0, packed_part())

    @pl.when(step == 1)
    def _():
        out = packed_part()
        put(0, width, out[:, :half])
        put(1, 0, out[:, half:])

    @pl.when(step == 2)
    def _():
        put(1, half, packed_part())

    @pl.when(step == 3)
    def _():
        out = tn(att_ref[...], gattn_ref[...]).astype(BF)
        put(0, width + half, out[:, :half])
        put(1, width + half, out[:, half:])


def weight_grads(normed, g, attended, gattn):
    count, width = normed.shape
    out = jax.ShapeDtypeStruct((width, 2 * width), BF)
    return call(
        weight_grad_body,
        limit=60,
        flops=8 * width * count * width,
        moved=2 * (6 * width * count + 4 * width * width),
        grid=(4,),
        in_specs=[
            whole(normed.shape),
            pl.BlockSpec((1, count, width), lambda i: (jnp.minimum(i, 2), 0, 0)),
            whole(attended.shape),
            whole(gattn.shape),
        ],
        out_specs=[whole(out.shape)] * 2,
        out_shape=[out] * 2,
    )(normed, g, attended, gattn)


def grad_in_body(x_ref, gain_ref, w_ref, g_ref, gres_ref, out_ref, ggain_ref):
    step = pl.program_id(0)
    width = x_ref.shape[1]
    x_hat, rate = norm_parts(x_ref[...].astype(F32))
    grad = nt(g_ref[0], w_ref[:, :width])
    grad += nt(g_ref[1], w_ref[:, width : 2 * width])
    grad += nt(g_ref[2], w_ref[:, 2 * width :])
    out_ref[...] = gres_ref[...] + norm_grad(x_hat, rate, grad * gain_ref[...])
    part = jnp.sum(grad * x_hat, axis=0, keepdims=True)

    @pl.when(step == 0)
    def _():
        ggain_ref[...] = part

    @pl.when(step > 0)
    def _():
        ggain_ref[...] += part


def grad_in(x, gain, w, g, gres):
    count, width = x.shape
    block = 256
    row = pl.BlockSpec((block, width), lambda i: (i, 0))
    return call(
        grad_in_body,
        limit=60,
        flops=6 * count * width * width,
        moved=2 * width * 9 * count,
        grid=(count // block,),
        in_specs=[
            row, whole(gain.shape), whole(w.shape),
            pl.BlockSpec((3, block, width), lambda i: (0, i, 0)), row,
        ],
        out_specs=[row, whole((1, width))],
        out_shape=[
            jax.ShapeDtypeStruct((count, width), F32),
            jax.ShapeDtypeStruct((1, width), F32),
        ],
    )(x, gain, w, g, gres)


def shift(a, axis, k):
    n = lax.axis_size(axis)
    return lax.ppermute(a, axis, [(i, (i + k) % n) for i in range(n)])


def groups(chips):
    sizes = [1]
    while sum(sizes) < chips:
        sizes.append((chips - sum(sizes) + 1) // 2)
    out, begin, at = [], 0, chips
    tall = sorted(sizes, reverse=True)
    for i, size in enumerate(sizes):
        rank = tall.index(size) + sizes[:i].count(size)
        out.append((tuple(range(begin, begin + size)), sum(tall[:rank]) // size))
        begin += size
    return out


def source_parts(sides):
    high, low = sides
    y, x, core = (lax.axis_index(axis) for axis in PLANE)
    out = []
    for dy in range(high):
        for dx in range(low):
            for dc in range(2):
                chip = lax.rem(y + high - dy, high) * low + lax.rem(x + low - dx, low)
                out.append(chip * 2 + lax.rem(core + dc, 2))
    return jnp.stack(out).astype(jnp.int32)


def plane_shift(a, part, sides):
    if part == 0:
        return a
    high, low = sides
    dy, dx, dc = part // (2 * low), part // 2 % low, part % 2
    pairs = []
    for y in range(high):
        for x in range(low):
            for core in range(2):
                to = ((y + dy) % high * low + (x + dx) % low) * 2 + (core + dc) % 2
                pairs.append(((y * low + x) * 2 + core, to))
    return lax.ppermute(a, PLANE, pairs)


def cut(a, index, pieces, dim):
    size = a.shape[dim] // pieces
    return lax.dynamic_slice_in_dim(a, index * size, size, dim)


def gather_all(a, axis, dim):
    n = lax.axis_size(axis)
    me = lax.axis_index(axis)
    size = a.shape[dim]
    shape = a.shape[:dim] + (n * size,) + a.shape[dim + 1 :]
    out = lax.dynamic_update_slice_in_dim(jnp.zeros(shape, a.dtype), a, me * size, dim)
    for k in range(1, n):
        got = shift(a, axis, k)
        out = lax.dynamic_update_slice_in_dim(out, got, lax.rem(me - k + n, n) * size, dim)
    return out


def after(value, *first):
    return lax.optimization_barrier((value, first))[0]


def split_body(keep_ref, got_ref, *out_refs, ways):
    half = keep_ref.shape[0] // 2
    at = 0
    for begin, axis, count in ((0, "x", ways[1]), (half, "y", ways[0])):
        size = half // count
        me = lax.axis_index(axis)
        for k in range(count):
            rows = pl.ds(pl.multiple_of(begin + lax.rem(me + k, count) * size, 8), size)
            out_refs[at][...] = (
                keep_ref[rows, :].astype(F32) + got_ref[rows, :].astype(F32)
            ).astype(BF)
            at += 1


def split(keep, got, ways):
    rows, wide = keep.shape
    sizes = [rows // 2 // ways[1]] * ways[1] + [rows // 2 // ways[0]] * ways[0]
    outs = call(
        functools.partial(split_body, ways=ways),
        limit=20,
        moved=6 * rows * wide,
        out_shape=[jax.ShapeDtypeStruct((size, wide), BF) for size in sizes],
    )(keep, got)
    return outs[: ways[1]], outs[ways[1] :]


def add_up(parts, axis):
    return [parts[0]] + [shift(a, axis, k) for k, a in enumerate(parts) if k]


def sum_over(a, axis):
    out = a
    for k in range(1, lax.axis_size(axis)):
        out = out + shift(a, axis, k)
    return out


def total(parts):
    out = parts[0].astype(F32)
    for a in parts[1:]:
        out += a.astype(F32)
    return out.astype(parts[0].dtype)


def pieces_of(a, axis, dim):
    n = lax.axis_size(axis)
    me = lax.axis_index(axis)
    return [cut(a, lax.rem(me + k, n), n, dim) for k in range(n)]


def gather_planes(parts):
    return gather_all(total(parts), "dp", 1)


def gather_plane(both, during):
    top = gather_all(both[0], "y", 0)
    low = gather_all(both[1], "x", 0)
    top, low = after((top, low), *during)
    top = gather_all(top, "x", 0)
    low = gather_all(low, "y", 0)
    mine = jnp.concatenate([top, low], 0)
    return mine, shift(mine, "core", 1)


def unpack_body(core_ref, in_ref, *refs):
    qkv_ref, proj_ref = refs[-2:]
    wide = qkv_ref.shape[1]
    qkv_ref[...] = in_ref[:, :wide].astype(F32)
    proj_ref[...] = in_ref[:, wide:].astype(F32)


def unpack(core, half, earlier):
    width = half.shape[0]
    block = min(192, width)
    shapes = [(width, 3 * width), (width, width)]
    return pl.pallas_call(
        unpack_body,
        grid_spec=pltpu.PrefetchScalarGridSpec(
            num_scalar_prefetch=1,
            grid=(width // block,),
            in_specs=[pl.BlockSpec((block, 2 * width), lambda i, s: (i, 0))]
            + [pl.BlockSpec(memory_space=pl.ANY)] * len(earlier),
            out_specs=[
                pl.BlockSpec((block, wide // 2), lambda i, s: (i, s[0])) for _, wide in shapes
            ],
        ),
        out_shape=[jax.ShapeDtypeStruct(shape, F32) for shape in shapes],
        input_output_aliases={2 + i: i for i in range(len(earlier))},
        compiler_params=pltpu.CompilerParams(vmem_limit_bytes=60 << 20),
        cost_estimate=pl.CostEstimate(
            flops=0, bytes_accessed=12 * width * width, transcendentals=0
        ),
    )(core, half, *earlier)


def widen_body(in_ref, *refs):
    refs[-1][...] = in_ref[...].astype(F32)


def widen(a, at, rows, *earlier):
    _, height, wide = a.shape
    block = math.gcd(height, 256)
    return call(
        widen_body,
        limit=60,
        moved=6 * height * wide,
        grid=(height // block,),
        in_specs=[pl.BlockSpec((1, block, wide), lambda i: (0, i, 0))] + [ANY] * len(earlier),
        out_specs=pl.BlockSpec((1, block, wide), lambda i: (0, at // block + i, 0)),
        out_shape=jax.ShapeDtypeStruct((1, rows, wide), F32),
        input_output_aliases={1: 0} if earlier else {},
    )(a, *earlier)


def local(tokens, token_ids, hash_table, gain_one, w_qkv, w_proj, gain_two, w_in, w_out, cotangent):
    width = tokens.shape[-1]
    x = tokens.reshape(-1, width)
    cot = cotangent.reshape(-1, width)
    count = x.shape[0]
    sides = (lax.axis_size("y"), lax.axis_size("x"))
    experts = lax.axis_size(PLANE)
    capacity = 2 * count // experts
    first_gain = gain_one.reshape(1, width)
    second_gain = gain_two.reshape(1, width)
    inner, outer = w_in[0], w_out[0]

    def exchange_all(a):
        return lax.all_to_all(a, PLANE, split_axis=0, concat_axis=0, tiled=True)

    def exchange(parts):
        return {i: plane_shift(a, i, sides) for i, a in parts.items()}

    row, col, grad_send = route(
        token_ids.reshape(1, count), hash_table.reshape(-1, 128), cot, sides, capacity
    )
    flat_grad = exchange_all(grad_send)
    packed, normed, attended, totals = attend(x, first_gain, w_qkv)
    residual, *outgoing = dispatch(attended, w_proj, x, second_gain, row, experts, capacity)
    outgoing = dict(enumerate(outgoing))
    far = {i: outgoing.pop(i) for i in range(experts - 2, experts)}
    arrived = exchange(outgoing)
    source = source_parts(sides)
    kept = ()
    plan = groups(experts // 2)
    for chips, place_at in plan:
        parts = [2 * chip + core for chip in chips for core in range(2)]
        kept = expert(
            chips, place_at, experts, source, [arrived[i] for i in parts], flat_grad,
            inner, outer, kept,
        )
        if chips == (0,):
            near = [arrived[i] for i in range(2, experts - 2)]
            arrived.update(exchange(after(far, near, kept[0])))
    active, grad_hidden, rows_in, rows_grad = kept
    tall_first = sorted((chips for chips, _ in plan), key=lambda chips: (-len(chips), chips))
    chips = jnp.stack([source[2 * chip] // 2 for chips in tall_first for chip in chips])
    shares = lax.axis_size("dp")
    share = inner.shape[1] // shares
    def scatter(a):
        return lax.psum_scatter(a[None], "dp", scatter_dimension=2, tiled=True)

    (grad_outer,) = weight_share(rows_grad, active, width)
    grad_w_out = scatter(grad_outer)
    grad_flat = make_result(chips, after(grad_hidden, grad_outer), inner, experts)
    grad_back = exchange_all(grad_flat).reshape(-1, width)
    most = width * 2 // 3
    grad_inner, grad_later = weight_share(
        after(rows_in, grad_flat), grad_hidden, most, width - most
    )
    grad_w_in = scatter(grad_inner)
    results = make_result(chips, after(active, grad_inner), outer, experts)
    returned = exchange_all(after(results, grad_back))

    grad_residual, grad_attn, grad_attended, grad_gain_two = collect_back(
        after(grad_back, results), col, residual, cot, second_gain, w_proj
    )
    grad_packed = attend_back(packed, attended, totals, grad_attended)
    keep, send = weight_grads(normed, grad_packed, attended, grad_attn)
    got = shift(send, "core", 1)
    grad_w_out = widen(after(grad_w_out, keep), 0, width)
    top, low = split(keep, after(got, grad_w_out, returned), sides)
    grad_tokens, grad_gain_one = grad_in(
        x, first_gain, w_qkv, after(grad_packed, top, low), grad_residual
    )
    small = jnp.concatenate([grad_gain_one, grad_gain_two], 0).reshape(-1, 128)
    small = sum_over(small, "core")
    top, low = after((add_up(top, "x"), add_up(low, "y")), grad_tokens)
    top, low = pieces_of(total(top), "y", 0), pieces_of(total(low), "x", 0)
    small = sum_over(sum_over(small, "x"), "y")
    top, low = after((add_up(top, "y"), add_up(low, "x")), grad_w_in)
    both = jnp.stack([total(top), total(low)])
    pad = both.shape[0] * both.shape[1] - small.shape[0]
    small = jnp.concatenate([small, jnp.zeros((pad, 128), F32)], 0).astype(BF)
    both = jnp.concatenate([both, small.reshape(both.shape[:2] + (128,))], 2)
    pieces = pieces_of(both, "dp", 1)
    outputs = collect(after(returned.reshape(-1, width), pieces), col, residual)
    grad_w_in = widen(after(grad_w_in, pieces), 0, width)
    both = gather_planes(after(add_up(pieces, "dp"), outputs, grad_w_in))
    small = both[:, :, 2 * width :].reshape(-1, 128)[: 2 * width // 128]
    gains = small.astype(F32).reshape(2, width)
    later = scatter(after(grad_later, both))
    core = lax.axis_index("core").reshape(1).astype(jnp.int32)

    def spread(both):
        mine, other = gather_plane(both, ())
        grads = unpack(core, mine, ())
        return tuple(unpack(1 - core, other, after(grads, other)))

    def skip(both):
        return tuple(jnp.zeros((width, wide), F32) for wide in (3 * width, width))

    grad_qkv, grad_proj = lax.cond(
        core[0] < 2, spread, skip, both[:, :, : 2 * width]
    )
    grad_w_in = widen(after(later, grad_qkv), most, width, grad_w_in)
    return (
        outputs.reshape(tokens.shape),
        grad_tokens.reshape(tokens.shape),
        gains[0],
        grad_qkv,
        grad_proj,
        gains[1],
        grad_w_in,
        grad_w_out,
    )


def solution(mesh):
    dp, experts = mesh.devices.shape
    side = math.isqrt(experts // 2)
    parts = Mesh(mesh.devices.reshape(dp, side, experts // 2 // side, 2), ("dp", "y", "x", "core"))
    rows = ("dp",) + PLANE
    in_specs = (
        P(rows, None, None),
        P(rows, None),
        P(),
        P(),
        P(),
        P(),
        P(),
        P(PLANE, None, None),
        P(PLANE, None, None),
        P(rows, None, None),
    )
    out_specs = (
        P(rows, None, None),
        P(rows, None, None),
        P(),
        P(),
        P(),
        P(),
        P(PLANE, None, "dp"),
        P(PLANE, None, "dp"),
    )
    return jax.shard_map(local, mesh=parts, in_specs=in_specs, out_specs=out_specs, check_vma=False)
```
